32 devices in a mesh: dp: 8 (over z, y), ctx: 2 (over core), tp: 2 (over x).
Axes of the slice: x: 2, y: 2, z: 4, core: 2. Of those that a mesh axis runs over, the one named last changes fastest.
Arguments:
- tokens: bfloat16 [8, 2, 1024, 1536], P('dp', 'ctx'), may hold values from -6 to 6
- routes: int32 [8, 2, 1024, 8], P('dp', 'ctx'), may hold values from 0 to 15, all different within a row; in each aligned block of 1024 rows (0 to 1023, 1024 to 2047, ..., all dimensions but the last counted through in order) at most 576 rows name the same one
- cotangent: bfloat16 [8, 2, 1024, 1536], P('dp', 'ctx'), may hold values from -6 to 6
- norm_one: bfloat16 [1536], P('dp'), may hold values from 0.5 to 1.5
- w_query: bfloat16 [1536, 1536], P('dp', 'tp'), may hold values from -0.4375 to 0.4375
- key_weight: bfloat16 [1536, 512], P('dp', 'tp'), may hold values from -0.4375 to 0.4375
- value_weight: bfloat16 [1536, 512], P('dp', 'tp'), may hold values from -0.15625 to 0.15625
- w_output: bfloat16 [1536, 1536], P('dp', 'tp'), may hold values from -0.625 to 0.625
- norm_two: bfloat16 [1536], P('dp'), may hold values from 0.5 to 1.5
- w_router: bfloat16 [1536, 16], P('dp'), may hold values from -0.078125 to 0.078125
- w_gate: bfloat16 [16, 1536, 512], P(None, 'dp', 'tp'), may hold values from -0.15625 to 0.15625
- w_up: bfloat16 [16, 1536, 512], P(None, 'dp', 'tp'), may hold values from -0.15625 to 0.15625
- w_down: bfloat16 [16, 1536, 512], P(None, 'dp', 'tp'), may hold values from -1 to 1
Outputs:
- output: bfloat16 [8, 2, 1024, 1536], P('dp', 'ctx')
- token_grad: float32 [8, 2, 1024, 1536], P('dp', 'ctx')
- grad_norm_one: float32 [1536], P('dp')
- grad_query: float32 [1536, 1536], P('dp', 'tp')
- grad_key: float32 [1536, 512], P('dp', 'tp')
- grad_value: float32 [1536, 512], P('dp', 'tp')
- grad_output: float32 [1536, 1536], P('dp', 'tp')
- grad_norm_two: float32 [1536], P('dp')
- grad_router: float32 [1536, 16], P('dp')
- grad_gate: float32 [16, 1536, 512], P(None, 'dp', 'tp')
- grad_up: float32 [16, 1536, 512], P(None, 'dp', 'tp')
- grad_down: float32 [16, 1536, 512], P(None, 'dp', 'tp')
The draws below stay inside these ranges and needn't reach their ends.
Inputs may be any that keep to these rules, and one draw needn't show every extreme that they name: `routes`: each row names 8 different experts. In the rows of one slab no expert is named more than 576 times, a bound that some block reaches.
All inputs are finite; a program needn't handle non-finite values.
Results may differ from the reference program's by a relative error of at most 0.015.
Values may be sent and summed in bfloat16 or wider, within the bound.
No kernel may reach another device: no remote copies, remote signals or barrier semaphores. Data moves between devices by JAX's collectives and lax.ppermute only.
A program may use at most 448 MiB of HBM per device.

```python
import math
import jax
import jax.numpy as jnp
import numpy as np
from jax import lax

MODEL_DIM = 1536
QUERY_HEADS = 24
KEY_VALUE_HEADS = 8
HEAD_DIM = 64
FF = 512
EXPERTS = 16
TOPK = 8
PROMPT_TOKENS = 1024
TOK_DEV = 1024
CONTS = 2
GROUPS = 8
MOST = 576
N_CTX = 2


def levels(key, shape, shards, least, top_value):
    level, own = 1.0, jax.random.fold_in(key, 6)
    for axis_at, parts in shards:
        steps = jnp.exp(jax.random.uniform(jax.random.fold_in(own, axis_at), (parts,), jnp.float32, least / len(shards), top_value / len(shards)))
        level = level * jnp.repeat(steps, shape[axis_at] // parts).reshape([-1 if axis == axis_at else 1 for axis in range(len(shape))])
    return level


def routed_block(rng, own, number, rows, amount, top, limit, slope):
    sequence = jax.random.permutation(rng, amount)
    crowded, ordinary = portions_of(amount, rows * top, limit, slope, True), portions_of(amount, rows * top, limit, slope, False)
    places = jnp.arange(amount)

    def named(lengths, turn):
        used = int((lengths > 0).sum())
        fixed = max(1, used // 4)
        passed = fixed + (places - fixed + turn * (used - fixed)) % max(1, amount - fixed)
        return jnp.zeros((amount,), jnp.int32).at[sequence[jnp.where(places < fixed, places, passed)]].set(jnp.asarray(lengths, jnp.int32))

    lengths = jnp.where(number % 4 == 0, named(crowded, number // 4), named(ordinary, number - number // 4 - 1))
    mixed = jax.random.permutation(jax.random.fold_in(own, 3), amount)
    giver, receiver = mixed[0:amount // 2 * 2:2], mixed[1:amount // 2 * 2:2]
    margin = jnp.minimum(lengths[giver] - 1, limit - lengths[receiver]) // 2
    margin = jnp.where((giver == sequence[0]) | (receiver == sequence[0]) | (lengths[receiver] == 0), 0, jnp.maximum(margin, 0))
    passed = jax.random.randint(jax.random.fold_in(own, 4), (amount // 2,), 0, 1 << 20) % (margin + 1)
    lengths = lengths.at[giver].add(-passed).at[receiver].add(passed)
    labels = jnp.searchsorted(jnp.cumsum(lengths), jnp.arange(rows * top), side="right").astype(jnp.int32)
    table = labels.reshape(top, rows).T
    table = table[jax.random.permutation(jax.random.fold_in(own, 1), rows)]
    turn = jax.random.randint(jax.random.fold_in(own, 2), (rows, 1), 0, top)
    return jnp.take_along_axis(table, (jnp.arange(top)[None, :] + turn) % top, axis=1)


def portions_of(amount, total, most, skew, full):
    loads = [(1 << 20) // math.isqrt(rank ** skew) + 1 for rank in range(1, amount + 1)]
    largest = most if full else min(most, max(-(-total // amount), total * loads[0] // sum(loads)))
    least = 1 if total - largest >= amount - 1 else 0
    counts, spare = [largest] + [least] * (amount - 1), total - largest - least * (amount - 1)
    while spare > 0:
        candidates = [i for i in range(1, amount) if counts[i] < largest] or [i for i in range(1, amount) if counts[i] < most]
        mass, remaining = sum([loads[i] for i in candidates]), spare
        for i in candidates:
            extra = min(most - counts[i], max(1, remaining * loads[i] // mass), spare)
            counts[i] = counts[i] + extra
            spare = spare - extra
    return np.array(counts)


def gaussian(stream_key, shape, width, most, shards=(), held_as=jnp.bfloat16):
    array = jax.random.normal(stream_key, shape, jnp.float32) * width
    if len(shards) > 0:
        array = levels(stream_key, shape, shards, -0.22, 0.18) * array
    return jnp.clip(array, min=-most, max=most).astype(held_as)


def setup_inputs(seed: int = 0) -> dict:
    key_of = jax.random.split(jax.random.key(seed), 14)
    tokens = gaussian(key_of[0], (GROUPS, CONTS, TOK_DEV, MODEL_DIM), 1.0, 6.0, ((0, 8), (1, 2)))
    routes_keys = jax.random.split(jax.random.fold_in(key_of[1], 1), GROUPS * CONTS * TOK_DEV // TOK_DEV)
    routes_turns = jax.random.permutation(jax.random.fold_in(key_of[1], 3), GROUPS * CONTS * TOK_DEV // TOK_DEV)
    routes = jax.vmap(lambda own, number: routed_block(jax.random.fold_in(key_of[1], 2), own, number, TOK_DEV, EXPERTS, TOPK, MOST, 2))(routes_keys, routes_turns).reshape((GROUPS, CONTS, TOK_DEV, TOPK))
    cotangent = gaussian(key_of[2], (GROUPS, CONTS, TOK_DEV, MODEL_DIM), 1.0, 6.0, ((0, 8), (1, 2)))
    norm_one = jnp.clip(1.0 + 0.1 * jax.random.normal(key_of[3], (MODEL_DIM,), jnp.float32), 0.5, 1.5).astype(jnp.bfloat16)
    w_query = gaussian(key_of[4], (MODEL_DIM, QUERY_HEADS * HEAD_DIM), (MODEL_DIM // 8) ** -0.5, 0.4375, ((0, 8), (1, 2)))
    key_weight = gaussian(key_of[5], (MODEL_DIM, KEY_VALUE_HEADS * HEAD_DIM), (MODEL_DIM // 8) ** -0.5, 0.4375, ((0, 8), (1, 2)))
    value_weight = gaussian(key_of[6], (MODEL_DIM, KEY_VALUE_HEADS * HEAD_DIM), MODEL_DIM ** -0.5, 0.15625, ((0, 8), (1, 2)))
    w_output = gaussian(key_of[7], (MODEL_DIM, QUERY_HEADS * HEAD_DIM), (QUERY_HEADS * HEAD_DIM // 16) ** -0.5, 0.625, ((0, 8), (1, 2)))
    norm_two = jnp.clip(1.0 + 0.1 * jax.random.normal(key_of[8], (MODEL_DIM,), jnp.float32), 0.5, 1.5).astype(jnp.bfloat16)
    w_router = gaussian(key_of[9], (MODEL_DIM, EXPERTS), (4 * MODEL_DIM) ** -0.5, 0.078125, ((0, 8),))
    w_gate = gaussian(key_of[10], (EXPERTS, MODEL_DIM, FF), MODEL_DIM ** -0.5, 0.15625, ((1, 8), (2, 2)))
    w_up = gaussian(key_of[11], (EXPERTS, MODEL_DIM, FF), MODEL_DIM ** -0.5, 0.15625, ((1, 8), (2, 2)))
    w_down = gaussian(key_of[12], (EXPERTS, MODEL_DIM, FF), (FF // 16) ** -0.5, 1.0, ((1, 8), (2, 2)))
    return dict(tokens=tokens, routes=routes, cotangent=cotangent, norm_one=norm_one, w_query=w_query, key_weight=key_weight, value_weight=value_weight, w_output=w_output, norm_two=norm_two, w_router=w_router, w_gate=w_gate, w_up=w_up, w_down=w_down)


@jax.custom_vjp
def lower_precision(v):
    return lax.optimization_barrier(v.astype(jnp.bfloat16)).astype(jnp.float32)

@jax.custom_vjp
def low_back(v):
    return v

def low_keep(v):
    return (lower_precision(v), None)

def low_pass(kept, grad):
    return (grad,)

def back_keep(v):
    return (v, None)

def back_low(kept, grad):
    return (lower_precision(grad),)
lower_precision.defvjp(low_keep, low_pass)
low_back.defvjp(back_keep, back_low)
norm_eps = 1e-06
rope_base = 10000.0
highest = lax.Precision.HIGHEST
masked_score = -1e+30

def rms_scale(values, gain):
    return values * lax.rsqrt(lax.optimization_barrier(jnp.mean(values * values, axis=-1, keepdims=True)) + norm_eps) * gain

def apply_rotary(vectors, token_positions, turning):
    half_dim = vectors.shape[-1] // 2
    freq_ids = jnp.arange(half_dim).astype(jnp.float32)
    inverse = rope_base ** (-2.0 * freq_ids / vectors.shape[-1])
    angles = token_positions.astype(jnp.float32)[..., None, None] * inverse
    cosine = jnp.cos(angles)
    sine = jnp.sin(angles) * turning
    first = vectors[..., :half_dim]
    second = vectors[..., half_dim:]
    return jnp.concatenate([first * cosine - second * sine, second * cosine + first * sine], axis=-1)

def layer(tokens, routes, norm_one, w_query, key_weight, value_weight, w_output, norm_two, w_router, w_gate, w_up, w_down):
    token_groups, token_length, model_width = tokens.shape
    half_length = PROMPT_TOKENS // N_CTX
    heads_per_group = QUERY_HEADS // KEY_VALUE_HEADS
    offsets = jnp.arange(token_length).astype(jnp.int32)
    slab_ids = jnp.arange(token_groups).astype(jnp.int32)
    token_positions = jnp.where(offsets[None, :] < half_length, slab_ids[:, None] * half_length + offsets[None, :], PROMPT_TOKENS + offsets[None, :] - half_length)
    key_pos = jnp.concatenate([jnp.arange(PROMPT_TOKENS).astype(jnp.int32), PROMPT_TOKENS + jnp.arange(token_length - half_length).astype(jnp.int32)])
    normed = lower_precision(rms_scale(tokens, norm_one))
    query_rows = low_back(jnp.einsum('ctd,dq->ctq', normed, w_query, precision=highest))
    query_rows = lower_precision(apply_rotary(query_rows.reshape(token_groups, token_length, QUERY_HEADS, HEAD_DIM), token_positions, 1.0))
    key_matrix = low_back(jnp.einsum('ctd,dq->ctq', normed, key_weight, precision=highest))
    key_matrix = lower_precision(apply_rotary(key_matrix.reshape(token_groups, token_length, KEY_VALUE_HEADS, HEAD_DIM), token_positions, 1.0))
    value_matrix = lower_precision(low_back(jnp.einsum('ctd,dq->ctq', normed, value_weight, precision=highest)))
    value_matrix = value_matrix.reshape(token_groups, token_length, KEY_VALUE_HEADS, HEAD_DIM)
    prefix_keys = key_matrix[:, :half_length].reshape(PROMPT_TOKENS, KEY_VALUE_HEADS, HEAD_DIM)
    prefix_values = value_matrix[:, :half_length].reshape(PROMPT_TOKENS, KEY_VALUE_HEADS, HEAD_DIM)
    joined_keys = jnp.concatenate([jnp.broadcast_to(prefix_keys[None], (token_groups, PROMPT_TOKENS, KEY_VALUE_HEADS, HEAD_DIM)), key_matrix[:, half_length:]], axis=1)
    joined_values = jnp.concatenate([jnp.broadcast_to(prefix_values[None], (token_groups, PROMPT_TOKENS, KEY_VALUE_HEADS, HEAD_DIM)), value_matrix[:, half_length:]], axis=1)
    grouped_queries = query_rows.reshape(token_groups, token_length, KEY_VALUE_HEADS, heads_per_group, HEAD_DIM)
    scores = low_back(jnp.einsum('cthgd,ckhd->chgtk', grouped_queries, joined_keys, precision=highest) * (1.0 / HEAD_DIM))
    allowed = key_pos[None, None, :] <= token_positions[:, :, None]
    scores = jnp.where(allowed[:, None, None], scores, masked_score)
    attn_probs = jax.nn.softmax(scores, axis=-1)
    mixed = jnp.einsum('chgtk,ckhd->cthgd', lower_precision(attn_probs), joined_values, precision=highest)
    attended = lower_precision(low_back(mixed.reshape(token_groups, token_length, QUERY_HEADS * HEAD_DIM)))
    branch = low_back(jnp.einsum('ctq,dq->ctd', attended, w_output, precision=highest))
    residual = tokens + branch
    normed_two = lower_precision(rms_scale(residual, norm_two))
    logits = low_back(jnp.einsum('ctd,de->cte', normed_two, w_router, precision=highest))
    chosen = jnp.take_along_axis(logits, routes, axis=-1)
    gate_vals = jax.nn.softmax(chosen, axis=-1)
    picks = (routes[..., None] == jnp.arange(EXPERTS).astype(jnp.int32)).astype(jnp.float32)
    combine = lax.optimization_barrier(jnp.sum(picks * gate_vals[..., None], axis=2)).reshape(token_groups * token_length, EXPERTS)
    flat_in = normed_two.reshape(token_groups * token_length, model_width)

    def expert_step(running, expert_parts):
        gate_mat, up_mat, down_mat, weight_col = expert_parts
        gate_act = low_back(jnp.dot(flat_in, gate_mat, precision=highest))
        up_act = low_back(jnp.dot(flat_in, up_mat, precision=highest))
        hidden = lower_precision(jax.nn.silu(gate_act) * up_act)
        expert_out = low_back(jnp.dot(hidden, down_mat.T, precision=highest))
        return (running + weight_col[:, None] * expert_out, None)
    moe_total, _ = lax.scan(jax.checkpoint(expert_step), jnp.zeros(flat_in.shape, jnp.float32), (w_gate, w_up, w_down, combine.T))
    return residual + moe_total.reshape(token_groups, token_length, model_width)

def reference(tokens, routes, cotangent, norm_one, w_query, key_weight, value_weight, w_output, norm_two, w_router, w_gate, w_up, w_down):
    params = tuple((param.astype(jnp.float32) for param in (norm_one, w_query, key_weight, value_weight, w_output, norm_two, w_router, w_gate, w_up, w_down)))

    def group_step(running, group_parts):
        group_tokens, group_routes, group_cot = group_parts

        def forward(slab_tokens, *weights):
            return layer(slab_tokens, group_routes, *weights)
        result, pullback = jax.vjp(forward, group_tokens.astype(jnp.float32), *params)
        grads = pullback(group_cot.astype(jnp.float32))
        running = tuple((total + update for total, update in zip(running, grads[1:])))
        return (running, (result.astype(jnp.bfloat16), grads[0]))
    initial = tuple((jnp.zeros(param.shape, jnp.float32) for param in params))
    totals, (outputs, token_grads) = lax.scan(group_step, initial, (tokens, routes, cotangent))
    return (outputs, token_grads, totals[0], totals[1], totals[2], totals[3], totals[4], totals[5], totals[6], totals[7], totals[8], totals[9])
```

```python
import functools

import jax
import jax.numpy as jnp
from jax import lax
from jax.experimental import pallas as pl
from jax.experimental.pallas import tpu as pltpu
from jax.sharding import PartitionSpec as P

HEAD_DIM = 64
EXPERTS = 16
TOPK = 8
PROMPT_TOKENS = 1024
LANES = 128
ROUTER_LANE = 16

norm_eps = 1e-06
rope_base = 10000.0
masked_score = -1e30
bf = jnp.bfloat16
f32 = jnp.float32
contract_cols = (((1,), (1,)), ((), ()))
vmem_bytes = 58 * 1024 * 1024


def mm(a, b):
    return jnp.dot(a, b, preferred_element_type=f32)


def mm_nt(a, b):
    return lax.dot_general(a, b, contract_cols, preferred_element_type=f32)


def whole(shape):
    return pl.BlockSpec(shape, lambda *_: (0,) * len(shape), pipeline_mode=pl.Buffered(1))


def rows_of(block, width):
    return pl.BlockSpec((block, width), lambda i, *_: (i, 0))


def any_space():
    return pl.BlockSpec(memory_space=pl.ANY)


def call(kernel, name, grid, ins, in_specs, outs, out_specs, scratch, flops, scalars, limit=vmem_bytes):
    moved = sum(a.size * a.dtype.itemsize for a in (*ins, *outs))
    return pl.pallas_call(
        kernel,
        out_shape=tuple(outs),
        grid_spec=pltpu.PrefetchScalarGridSpec(
            num_scalar_prefetch=1,
            grid=grid,
            in_specs=in_specs,
            out_specs=tuple(out_specs),
            scratch_shapes=scratch,
        ),
        compiler_params=pltpu.CompilerParams(vmem_limit_bytes=limit),
        cost_estimate=pl.CostEstimate(flops=int(flops), bytes_accessed=int(moved), transcendentals=0),
        name=name,
    )(scalars, *ins)


def sds(shape, dtype):
    return jax.ShapeDtypeStruct(tuple(shape), dtype)


def ring_rank(place, count):
    place = lax.rem(place + 2 * count, count)
    return jnp.where(place < count // 2, 2 * place, 2 * count - 1 - 2 * place)


def ring_place(rank, count):
    return jnp.where(rank % 2 == 0, rank // 2, (2 * count - 1 - rank) // 2)


def ring_pairs(count):
    order = list(range(0, count, 2)) + list(range(count - 1, 0, -2))
    ahead = [(order[k], order[(k + 1) % count]) for k in range(count)]
    return ahead, [(d, s) for s, d in ahead]


def ring_gather(own, count):
    ahead, back = ring_pairs(count)
    cut = (own.shape[0] + 1) // 2
    kept, f, g = [own], own, own
    for hop in range(1, count // 2 + 1):
        if hop == count // 2:
            f, g = f[:cut], g[cut:]
        f, g = lax.ppermute(f, "dp", ahead), lax.ppermute(g, "dp", back)
        kept += [f, g]
    return kept


def ring_sources(place, count):
    away = [0]
    for hop in range(1, count // 2):
        away += [-hop, hop]
    away.append(count // 2)
    return [ring_rank(place + a, count) for a in away]


def ring_scatter(piece, place, count):
    ahead, back = ring_pairs(count)
    f = g = None
    for hop in range(1, count // 2 + 1):
        far = count // 2 - hop + 1
        if hop == 1:
            mine = piece(ring_rank(place + far, count))
            cut = (mine.shape[0] + 1) // 2
            f, g = mine[:cut].astype(bf), mine[cut:].astype(bf)
        else:
            mine_f = piece(ring_rank(place + far, count))
            mine_g = piece(ring_rank(place - far, count))
            if hop == 2:
                f = jnp.concatenate([mine_f[:cut] + f.astype(f32), mine_f[cut:]], axis=0).astype(bf)
                g = jnp.concatenate([mine_g[:cut], mine_g[cut:] + g.astype(f32)], axis=0).astype(bf)
            else:
                f = (mine_f + f.astype(f32)).astype(bf)
                g = (mine_g + g.astype(f32)).astype(bf)
        f, g = lax.ppermute(f, "dp", ahead), lax.ppermute(g, "dp", back)
    return piece(ring_rank(place, count)) + f.astype(f32) + g.astype(f32)


def swap(values, axis):
    return lax.ppermute(values, axis, [(0, 1), (1, 0)])


def take(values, start, size):
    return lax.dynamic_slice_in_dim(values, start, size, 0)


def load_shards(scalars, bufs, first_block, blocks, dst, shard, sem):
    total = len(bufs)
    cut = (blocks + 1) // 2
    for k, buf in enumerate(bufs):
        rows = pl.ds(pl.multiple_of(scalars[min(k, total - 2)] * shard, shard), shard)
        at = first_block + (cut if k == total - 1 else 0)
        size = blocks if k < total - 2 else (cut if k == total - 2 else blocks - cut)
        pltpu.make_async_copy(buf, dst.at[pl.ds(at, size), rows, :], sem).start()


def lanes_of(ref, first, count):
    return jnp.concatenate([ref[first + b] for b in range(count)], axis=1)


def rope(x, cosine, sine):
    lane = lax.broadcasted_iota(jnp.int32, x.shape, x.ndim - 1)
    ahead = pltpu.roll(x, x.shape[-1] - HEAD_DIM // 2, x.ndim - 1)
    behind = pltpu.roll(x, HEAD_DIM // 2, x.ndim - 1)
    return x * cosine + jnp.where(lax.rem(lane, HEAD_DIM) < HEAD_DIM // 2, ahead, behind) * sine


def qkv_kernel(shard, kinds, sc, tok, cosine, sine, *refs):
    heads, kvs, total = kinds
    bufs, (w_out, extra_out, q_out, k_out, v_out, nt_out, w, et, sem, out_sem) = refs[: 2 * total], refs[2 * total :]
    half = w.shape[0] // 2
    step = pl.program_id(0)

    @pl.when(step == 0)
    def _():
        for side in range(2):
            base = sc[total - 1 + side] * half
            load_shards(sc, bufs[side * total : (side + 1) * total], base, half, w, shard, sem)
        pltpu.make_async_copy(w, w, sem).wait()
        pltpu.make_async_copy(w, w_out, out_sem).start()
        et[...] = w[heads // 2 + kvs].T

    extra_out[...] = et[...]
    x = tok[...].astype(f32)
    scale = lax.rsqrt(jnp.mean(x * x, axis=-1, keepdims=True) + norm_eps)
    normed = (x * scale * et[0:1, :].astype(f32)).astype(bf)
    nt_out[...] = normed.T
    cs, sn = cosine[...], sine[...]
    for pair in range((heads + 2 * kvs) // 4):
        made = mm(normed, lanes_of(w, 2 * pair, 2))
        for side in range(2):
            first = 4 * pair + 2 * side
            part = made[:, side * LANES : (side + 1) * LANES]
            if first < heads + kvs:
                part = rope(part, cs, sn)
            if first < heads:
                part, out, at = part * (1.0 / HEAD_DIM), q_out, first
            elif first < heads + kvs:
                out, at = k_out, first - heads
            else:
                out, at = v_out, first - heads - kvs
            low = part.astype(bf)
            out[at] = low[:, :HEAD_DIM]
            out[at + 1] = low[:, HEAD_DIM:]

    @pl.when(step == pl.num_programs(0) - 1)
    def _():
        pltpu.make_async_copy(w, w_out, out_sem).wait()


def project(tokens, cosine, sine, scalars, own, mate, heads, kvs, block=256):
    rows, width = tokens.shape
    shard = own[0].shape[1]
    blocks = 2 * own[0].shape[0]
    head_spec = lambda count: pl.BlockSpec((count, block, HEAD_DIM), lambda i, s: (0, i, 0))
    outs = [
        sds((blocks, width, LANES), bf),
        sds((LANES, width), bf),
        sds((heads, rows, HEAD_DIM), bf),
        sds((kvs, rows, HEAD_DIM), bf),
        sds((kvs, rows, HEAD_DIM), bf),
        sds((width, rows), bf),
    ]
    return call(
        functools.partial(qkv_kernel, shard, (heads, kvs, len(own))),
        "project",
        (rows // block,),
        [tokens, cosine, sine, *own, *mate],
        [rows_of(block, width), rows_of(block, LANES), rows_of(block, LANES)] + [any_space()] * (2 * len(own)),
        outs,
        [
            any_space(),
            whole((LANES, width)),
            head_spec(heads),
            head_spec(kvs),
            head_spec(kvs),
            pl.BlockSpec((width, block), lambda i, s: (0, i)),
        ],
        [
            pltpu.VMEM((blocks, width, LANES), bf),
            pltpu.VMEM((LANES, width), bf),
            pltpu.SemaphoreType.DMA,
            pltpu.SemaphoreType.DMA,
        ],
        2 * rows * width * blocks * LANES,
        scalars,
    )


def assemble_kernel(shard, sc, *refs):
    total = (len(refs) - 2) // 2
    out, sem = refs[-2], refs[-1]
    half = out.shape[0] // 2
    for side in range(2):
        load_shards(sc, refs[side * total : (side + 1) * total], sc[total - 1 + side] * half, half, out, shard, sem)
    pltpu.make_async_copy(out, out, sem).wait()


def assemble(scalars, own, mate, width):
    shard = own[0].shape[1]
    return call(
        functools.partial(assemble_kernel, shard),
        "assemble",
        (1,),
        [*own, *mate],
        [any_space()] * (2 * len(own)),
        [sds((2 * own[0].shape[0], width, LANES), bf)],
        [any_space()],
        [pltpu.SemaphoreType.DMA],
        0,
        scalars,
    )[0]


def causal(scores):
    key = lax.broadcasted_iota(jnp.int32, scores.shape, 0)
    query = lax.broadcasted_iota(jnp.int32, scores.shape, 1)
    return jnp.where(key <= query, scores, masked_score)


def block_scores(query, keys, other_keys, at, block, prompt, bias):
    parts = []
    if at:
        parts.append(mm_nt(keys[0:at], query))
    parts.append(causal(mm_nt(keys[at : at + block], query)))
    other = mm_nt(other_keys, query)
    if at < prompt:
        other = other + bias
    parts.append(other)
    return parts


def attend_kernel(cfg, sc, q, k0, k1, o0, o1, v0, v1, w0, w1, mixed, lse):
    starts, block, prompt = cfg
    bias = jnp.where(sc[0] == 0, masked_score, 0.0).astype(f32)
    for side, (keys, other, values, other_values) in enumerate(((k0, o0, v0, w0), (k1, o1, v1, w1))):
        values_t = values[0].T
        other_t = other_values[0].T
        for a, at in enumerate(starts):
            rows = slice(a * block, a * block + block)
            scores = block_scores(q[side, rows, :], keys[0], other[0], at, block, prompt, bias)
            peak = functools.reduce(jnp.maximum, [jnp.max(s, axis=0, keepdims=True) for s in scores])
            raw = [jnp.exp(s - peak) for s in scores]
            total = sum(jnp.sum(r, axis=0, keepdims=True) for r in raw)
            low = [r.astype(bf) for r in raw]
            out = mm(other_t, low[-1]) + mm(values_t[:, at : at + block], low[-2])
            if at:
                out = out + mm(values_t[:, 0:at], low[0])
            out = out * (1.0 / total)
            mixed[rows, side * HEAD_DIM : side * HEAD_DIM + HEAD_DIM] = out.T.astype(bf)
            lse[0, side : side + 1, rows] = peak + jnp.log(total)


def kv_specs(kvs, rows, prompt, rep):
    index = lambda side: (lambda p, s: ((2 * p + side) // rep, 0, 0))
    own = [pl.BlockSpec((1, rows, HEAD_DIM), index(side)) for side in range(2)]
    other = [pl.BlockSpec((1, prompt, HEAD_DIM), index(side)) for side in range(2)]
    return own + other


def attend(q, k, v, other_k, other_v, core, part, block=256):
    heads, rows, _ = q.shape
    kvs, prompt = other_k.shape[:2]
    count = prompt if part == 0 else rows - prompt
    first = 0 if part == 0 else prompt
    starts = tuple(range(first, first + count, block))
    specs = kv_specs(kvs, rows, prompt, heads // kvs)
    return call(
        functools.partial(attend_kernel, (starts, block, prompt)),
        "attend",
        (heads // 2,),
        [q, k, k, other_k, other_k, v, v, other_v, other_v],
        [pl.BlockSpec((2, count, HEAD_DIM), lambda p, s: (p, part, 0)), *specs, *specs],
        [sds((count, heads * HEAD_DIM), bf), sds((heads // 2, 2, count), f32)],
        [
            pl.BlockSpec((count, LANES), lambda p, s: (0, p)),
            pl.BlockSpec((1, 2, count), lambda p, s: (p, 0, 0)),
        ],
        [],
        16 * heads * count * 1024 * HEAD_DIM,
        core,
    )


def attend_back_kernel(cfg, sc, q, k0, k1, o0, o1, v0, v1, w0, w1, dout, mixed_a, mixed_b, lse_a, lse_b, cosine, sine, dq, dk, dko, dv, dvo):
    rows_total, block, prompt, rep = cfg
    pair = pl.program_id(0)
    bias = jnp.where(sc[0] == 0, masked_score, 0.0).astype(f32)

    @pl.when(pair == 0)
    def _():
        for ref in (dk, dko, dv, dvo):
            ref[...] = jnp.zeros_like(ref)

    heads = ((k0, o0, v0, w0), (k1, o1, v1, w1))
    keys_t = [(keys[0].T, other[0].T) for keys, other, _, _ in heads]
    for at in range(0, rows_total, block):
        rows = slice(at, at + block)
        mixed, lse, local = (mixed_a, lse_a, at) if at < prompt else (mixed_b, lse_b, at - prompt)
        inner = slice(local, local + block)
        dot = (dout[rows, :].astype(f32) * mixed[inner, :].astype(f32)).T
        grads = []
        for side, (keys, other, values, other_values) in enumerate(heads):
            kv = (2 * pair + side) // rep
            query = q[side, rows, :]
            grad = dout[rows, side * HEAD_DIM : side * HEAD_DIM + HEAD_DIM]
            weighted = jnp.sum(dot[side * HEAD_DIM : side * HEAD_DIM + HEAD_DIM], axis=0, keepdims=True)
            norm = lse[0, side : side + 1, inner]
            scores = block_scores(query, keys[0], other[0], at, block, prompt, bias)
            spans = ([(False, 0, at)] if at else []) + [(False, at, block), (True, 0, prompt)]
            back = None
            for score, (is_other, first, size) in zip(scores, spans):
                probs = jnp.exp(score - norm)
                value = other_values[0] if is_other else values[0, first : first + size]
                score_low = (probs * (mm_nt(value, grad) - weighted)).astype(bf)
                key_sum, value_sum = (dko, dvo) if is_other else (dk, dv)
                span = pl.ds(first, size)
                value_sum[kv, span, :] += mm(probs.astype(bf), grad)
                key_sum[kv, span, :] += mm(score_low, query)
                key_t = keys_t[side][1] if is_other else keys_t[side][0][:, first : first + size]
                term = mm(key_t, score_low)
                back = term if back is None else back + term
            grads.append(back)
        both = jnp.concatenate(grads, axis=0).T * (1.0 / HEAD_DIM)
        dq[rows, :] = rope(both, cosine[rows, :], -sine[rows, :]).astype(bf)


def attend_back(q, k, v, other_k, other_v, dout, mixed, lse, cosine, sine, core, block=256):
    heads, rows, _ = q.shape
    kvs, prompt = other_k.shape[:2]
    specs = kv_specs(kvs, rows, prompt, heads // kvs)
    pair = pl.BlockSpec((rows, LANES), lambda p, s: (0, p))
    mixed_spec = lambda a: pl.BlockSpec((a.shape[0], LANES), lambda p, s: (0, p))
    lse_spec = lambda a: pl.BlockSpec((1, 2, a.shape[2]), lambda p, s: (p, 0, 0))
    return call(
        functools.partial(attend_back_kernel, (rows, block, prompt, heads // kvs)),
        "attend_back",
        (heads // 2,),
        [q, k, k, other_k, other_k, v, v, other_v, other_v, dout, *mixed, *lse, cosine, sine],
        [
            pl.BlockSpec((2, rows, HEAD_DIM), lambda p, s: (p, 0, 0)),
            *specs,
            *specs,
            pair,
            *[mixed_spec(a) for a in mixed],
            *[lse_spec(a) for a in lse],
            whole(cosine.shape),
            whole(sine.shape),
        ],
        [
            sds((rows, heads * HEAD_DIM), bf),
            sds((kvs, rows, HEAD_DIM), f32),
            sds((kvs, prompt, HEAD_DIM), f32),
            sds((kvs, rows, HEAD_DIM), f32),
            sds((kvs, prompt, HEAD_DIM), f32),
        ],
        [
            pair,
            whole((kvs, rows, HEAD_DIM)),
            whole((kvs, prompt, HEAD_DIM)),
            whole((kvs, rows, HEAD_DIM)),
            whole((kvs, prompt, HEAD_DIM)),
        ],
        [],
        40 * heads * rows * 1024 * HEAD_DIM,
        core,
    )


def load_halves(sc, mine, theirs, first_block, w, sem):
    half = mine.shape[0]
    pltpu.make_async_copy(mine, w.at[pl.ds(first_block + sc[0] * half, half)], sem).start()
    pltpu.make_async_copy(theirs, w.at[pl.ds(first_block + (1 - sc[0]) * half, half)], sem).start()


def settle_kernel(sc, tok, ids, own_a, own_b, far_a, far_b, extra, w_own, w_mine, w_theirs, res_out, n_out, nt_out, wt_out, w, sem):
    step = pl.program_id(0)
    blocks = w_own.shape[0]

    @pl.when(step == 0)
    def _():
        pltpu.make_async_copy(w_own, w.at[pl.ds(0, blocks)], sem).start()
        load_halves(sc, w_mine, w_theirs, blocks, w, sem)
        pltpu.make_async_copy(w, w, sem).wait()

    early = step < pl.num_programs(0) // 2
    own = jnp.where(early, own_a[...], own_b[...])
    far = jnp.where(early, far_a[...], far_b[...])
    branch = mm_nt(own, lanes_of(w, 0, blocks)) + mm_nt(far, lanes_of(w, blocks, blocks))
    residual = tok[...].astype(f32) + branch
    res_out[...] = residual
    scale = lax.rsqrt(jnp.mean(residual * residual, axis=-1, keepdims=True) + norm_eps)
    normed = (residual * scale * extra[1:2, :].astype(f32)).astype(bf)
    n_out[...] = normed
    nt_out[...] = normed.T
    logits = mm_nt(normed, extra[...])
    lane = lax.broadcasted_iota(jnp.int32, logits.shape, 1)
    routed = lane < 0
    for k in range(TOPK):
        routed = jnp.logical_or(routed, lane == ids[:, k : k + 1] + ROUTER_LANE)
    logits = jnp.where(routed, logits, masked_score)
    raw = jnp.where(routed, jnp.exp(logits - jnp.max(logits, axis=-1, keepdims=True)), 0.0)
    wt_out[...] = raw / jnp.sum(raw, axis=-1, keepdims=True)


def settle(tokens, ids, own, far, extra, w_own, w_mine, w_theirs, core, block=256):
    rows, width = tokens.shape
    halves = rows // block // 2
    cols = own[0].shape[1]
    low = pl.BlockSpec((block, cols), lambda i, s: (jnp.minimum(i, halves - 1), 0))
    high = pl.BlockSpec((block, cols), lambda i, s: (jnp.maximum(i - halves, 0), 0))
    return call(
        settle_kernel,
        "settle",
        (rows // block,),
        [tokens, ids, *own, *far, extra, w_own, w_mine, w_theirs],
        [rows_of(block, width), rows_of(block, TOPK), low, high, low, high, whole(extra.shape)] + [any_space()] * 3,
        [sds((rows, width), f32), sds((rows, width), bf), sds((width, rows), bf), sds((rows, LANES), f32)],
        [rows_of(block, width), rows_of(block, width), pl.BlockSpec((width, block), lambda i, s: (0, i)), rows_of(block, LANES)],
        [pltpu.VMEM((2 * w_own.shape[0], width, LANES), bf), pltpu.SemaphoreType.DMA],
        4 * rows * width * cols,
        core,
    )


def experts_kernel(cfg, sc, *refs):
    shard, width, rows_total, hidden, half, first, last, total = cfg
    block = 256
    step = pl.program_id(0)
    it = iter(refs)
    n2, n2t, cot, cott, wt = (next(it) for _ in range(5))
    mine = [next(it) for _ in range(total)]
    mate = [next(it) for _ in range(total)]
    if not first:
        moe_in, back_in = next(it), next(it)
    moe_out, back_out, keep, send, pick = (next(it) for _ in range(5))
    w, scaled, acts, sem, sum_sem = (next(it) for _ in range(5))
    moe, back = (next(it), next(it)) if last else (moe_out, back_out)
    cut = half // 2

    def fetch(at, slot):
        for side, bufs in enumerate((mine, mate)):
            lanes = pl.ds(side * hidden, hidden)

            def copy(k, start):
                rows = pl.ds(pl.multiple_of(sc[min(k, total - 2)] * shard, shard), shard)
                src = bufs[k].at[pl.ds(start * 3, 3)]
                pltpu.make_async_copy(src, w.at[slot, :, rows, lanes], sem.at[slot]).start()

            for k in range(total - 2):
                copy(k, at)

            @pl.when(at < cut)
            def _():
                copy(total - 2, at)

            @pl.when(at >= cut)
            def _():
                copy(total - 1, at - cut)

    slot = lax.rem(step, 2)

    @pl.when(step == 0)
    def _():
        fetch(0, 0)
        if not first:
            pltpu.make_async_copy(moe_in, moe, sum_sem.at[0]).start()
            pltpu.make_async_copy(back_in, back, sum_sem.at[1]).start()
        else:
            moe[...] = jnp.zeros_like(moe)
            back[...] = jnp.zeros_like(back)

    @pl.when(step + 1 < half)
    def _():
        fetch(step + 1, 1 - slot)

    pltpu.make_async_copy(w.at[slot], w.at[slot], sem.at[slot]).wait()
    experts = [sc[total - 1 + side] + step + ROUTER_LANE for side in range(2)]
    lane = lax.broadcasted_iota(jnp.int32, (block, LANES), 1)
    for at in range(0, rows_total, block):
        rows = pl.ds(at, block)
        x = n2[rows, :]
        gate = mm(x, w[slot, 0])
        up = mm(x, w[slot, 1])
        grad = mm(cot[rows, :], w[slot, 2])
        table = wt[rows, :]
        sig = 1.0 / (1.0 + jnp.exp(-gate))
        silu = gate * sig
        act = silu * up
        dots = act * grad
        picked = jnp.zeros(table.shape, f32)
        for side, expert in enumerate(experts):
            cols = slice(side * hidden, side * hidden + hidden)
            weight = jnp.sum(jnp.where(lane == expert, table, 0.0), axis=1, keepdims=True)
            picked = picked + jnp.where(lane == expert, jnp.sum(dots[:, cols], axis=1, keepdims=True), 0.0)
            scaled[rows, cols] = (act[:, cols] * weight).astype(bf)
            g = grad[:, cols] * weight
            s = sig[:, cols]
            acts[rows, cols] = (g * up[:, cols] * s * (1.0 + gate[:, cols] * (1.0 - s))).astype(bf)
            acts[rows, slice((2 + side) * hidden, (3 + side) * hidden)] = (g * silu[:, cols]).astype(bf)

        @pl.when(step == 0)
        def _():
            pick[rows, :] = picked

        @pl.when(step > 0)
        def _():
            pick[rows, :] += picked

    if not first:

        @pl.when(step == 0)
        def _():
            pltpu.make_async_copy(moe_in, moe, sum_sem.at[0]).wait()
            pltpu.make_async_copy(back_in, back, sum_sem.at[1]).wait()

    for at in range(0, rows_total, block):
        rows = pl.ds(at, block)
        moe[rows, :] += mm_nt(scaled[rows, :], w[slot, 2])
        back[rows, :] += mm_nt(acts[rows, 0 : 2 * hidden], w[slot, 0]) + mm_nt(acts[rows, 2 * hidden : 4 * hidden], w[slot, 1])
    for at in range(0, width, block):
        cols = pl.ds(at, block)
        down = mm(cott[cols, :], scaled[...])
        gate_up = mm(n2t[cols, :], acts[...])
        for k, made in enumerate((gate_up[:, : 2 * hidden], gate_up[:, 2 * hidden :], down)):
            keep[0, k, cols, :] = made[:, :hidden].astype(bf)
            send[0, k, cols, :] = made[:, hidden:].astype(bf)

    if last:

        @pl.when(step == half - 1)
        def _():
            moe_out[...] = moe[...].astype(moe_out.dtype)
            back_out[...] = back[...].astype(back_out.dtype)


def experts(n2, n2t, cot, cott, wt, scalars, mine, mate, sums, last):
    rows, width = n2.shape
    shard, hidden = mine[0].shape[1:]
    half = mine[0].shape[0] // 3
    first = sums is None
    cfg = (shard, width, rows, hidden, half, first, last, len(mine))
    dense = [n2, n2t, cot, cott, wt]
    ins = dense + list(mine) + list(mate) + ([] if first else list(sums))
    kind = bf if last else f32
    grads = pl.BlockSpec((1, 3, width, hidden), lambda i, s: (i, 0, 0, 0))
    return call(
        functools.partial(experts_kernel, cfg),
        "experts",
        (half,),
        ins,
        [whole(a.shape) for a in dense] + [any_space()] * (len(ins) - len(dense)),
        [
            sds((rows, width), kind),
            sds((rows, width), kind),
            sds((half, 3, width, hidden), bf),
            sds((half, 3, width, hidden), bf),
            sds((rows, LANES), f32),
        ],
        [whole((rows, width)), whole((rows, width)), grads, grads, whole((rows, LANES))],
        [
            pltpu.VMEM((2, 3, width, 2 * hidden), bf),
            pltpu.VMEM((rows, 2 * hidden), bf),
            pltpu.VMEM((rows, 4 * hidden), bf),
            pltpu.SemaphoreType.DMA((2,)),
            pltpu.SemaphoreType.DMA((2,)),
        ]
        + [pltpu.VMEM((rows, width), f32)] * (2 if last else 0),
        36 * rows * width * hidden * half,
        scalars,
    )


def norm_back(values, gain, grad):
    scale = lax.rsqrt(jnp.mean(values * values, axis=-1, keepdims=True) + norm_eps)
    inner = jnp.mean(values * gain * grad, axis=-1, keepdims=True)
    passed = scale * gain * grad - values * (scale * scale * scale * inner)
    return passed, jnp.sum(grad * values * scale, axis=0, keepdims=True)


def unsettle_kernel(sc, back_a, back_b, pick_a, pick_b, wt, res, cot, extra, w_own, rg_out, low_t_out, dout_out, ll_out, gain_out, w, sem):
    step = pl.program_id(0)

    @pl.when(step == 0)
    def _():
        pltpu.make_async_copy(w_own, w, sem).start()
        pltpu.make_async_copy(w_own, w, sem).wait()
        gain_out[...] = jnp.zeros_like(gain_out)

    weights = wt[...]
    picked = pick_a[...] + pick_b[...]
    logit_low = (weights * (picked - jnp.sum(weights * picked, axis=-1, keepdims=True))).astype(bf)
    ll_out[...] = logit_low
    grad = back_a[...].astype(f32) + back_b[...].astype(f32) + mm(logit_low, extra[...])
    passed, gain = norm_back(res[...], extra[1:2, :].astype(f32), grad)
    gain_out[...] += gain
    total = cot[...].astype(f32) + passed
    rg_out[...] = total
    low = total.astype(bf)
    low_t_out[...] = low.T
    dout_out[...] = mm(low, lanes_of(w, 0, w.shape[0])).astype(bf)


def unsettle(back, picks, wt, res, cot, extra, w_own, core, block=256):
    rows, width = res.shape
    cols = w_own.shape[0] * LANES
    wide, thin = rows_of(block, width), rows_of(block, LANES)
    return call(
        unsettle_kernel,
        "unsettle",
        (rows // block,),
        [*back, *picks, wt, res, cot, extra, w_own],
        [wide, wide, thin, thin, thin, wide, wide, whole(extra.shape), any_space()],
        [sds((rows, width), f32), sds((width, rows), bf), sds((rows, cols), bf), sds((rows, LANES), bf), sds((1, width), f32)],
        [wide, pl.BlockSpec((width, block), lambda i, s: (0, i)), rows_of(block, cols), thin, whole((1, width))],
        [pltpu.VMEM(w_own.shape, bf), pltpu.SemaphoreType.DMA],
        2 * rows * width * cols,
        core,
    )


def lane_column(row, shape, lane_at):
    lane = lax.broadcasted_iota(jnp.int32, shape, 1)
    return jnp.where(lane == lane_at, jnp.broadcast_to(row, (shape[1], shape[0])).T, 0.0)


def output_grads_kernel(sc, low_t, mixed_a, mixed_b, n2t, ll, gain, out):
    prompt = mixed_a.shape[0]
    made = mm(low_t[:, 0:prompt], mixed_a[...]) + mm(low_t[:, prompt:], mixed_b[...])
    count = made.shape[1] // LANES
    for b in range(count):
        out[b] = made[:, b * LANES : (b + 1) * LANES].astype(bf)
    router = mm(n2t[...], ll[...])
    out[count] = (router + lane_column(gain[...], router.shape, 1)).astype(bf)
    for b in range(count + 1, out.shape[0]):
        out[b] = jnp.zeros_like(out[b])


def output_grads(low_t, mixed, n2t, ll, gain, core, block=256):
    width, rows = low_t.shape
    blocks = mixed[0].shape[1] // LANES + 2
    tall = pl.BlockSpec((block, rows), lambda i, s: (i, 0))
    return call(
        output_grads_kernel,
        "output_grads",
        (width // block,),
        [low_t, *mixed, n2t, ll, gain],
        [tall, *[whole(a.shape) for a in mixed], tall, whole(ll.shape), pl.BlockSpec((1, block), lambda i, s: (0, i))],
        [sds((blocks, width, LANES), bf)],
        [pl.BlockSpec((blocks, block, LANES), lambda i, s: (0, i, 0))],
        [],
        2 * rows * width * blocks * LANES,
        core,
    )[0]


def unproject_kernel(sc, tok, dq, dk, dkx, dv, dvx, cosine, sine, w_own, low_out, part_out, gain_out, w, low_scr, sem):
    step = pl.program_id(0)
    cols = low_out.shape[1]
    blocks = cols // LANES
    kvs = dk.shape[0]

    @pl.when(step == 0)
    def _():
        pltpu.make_async_copy(w_own, w, sem).start()
        pltpu.make_async_copy(w_own, w, sem).wait()
        gain_out[...] = jnp.zeros_like(gain_out)

    shared = jnp.where(step < pl.num_programs(0) // 2, 1.0, 0.0).astype(f32)
    at = dq.shape[1]
    low_out[:, 0:at] = dq[...]
    for grads, more, turn in ((dk, dkx, True), (dv, dvx, False)):
        for kv in range(0, kvs, 2):
            pair = jnp.concatenate([grads[kv] + more[kv] * shared, grads[kv + 1] + more[kv + 1] * shared], axis=1)
            if turn:
                pair = rope(pair, cosine[...], -sine[...])
            low_out[:, at : at + LANES] = pair.astype(bf)
            at += LANES
    part = mm_nt(low_out[...], lanes_of(w, 0, blocks))
    part_out[...] = part
    x = tok[...].astype(f32)
    scale = lax.rsqrt(jnp.mean(x * x, axis=-1, keepdims=True) + norm_eps)
    gain_out[...] += jnp.sum(part * x * scale, axis=0, keepdims=True)


def unproject(tokens, dq, dk, dkx, dv, dvx, cosine, sine, w_own, core, block=256):
    rows, width = tokens.shape
    kvs, prompt = dkx.shape[:2]
    cols = dq.shape[1] + 2 * kvs * HEAD_DIM
    halves = prompt // block
    own = pl.BlockSpec((kvs, block, HEAD_DIM), lambda i, s: (0, i, 0))
    other = pl.BlockSpec((kvs, block, HEAD_DIM), lambda i, s: (0, jnp.minimum(i, halves - 1), 0))
    return call(
        unproject_kernel,
        "unproject",
        (rows // block,),
        [tokens, dq, dk, dkx, dv, dvx, cosine, sine, w_own],
        [rows_of(block, width), rows_of(block, dq.shape[1]), own, other, own, other, rows_of(block, LANES), rows_of(block, LANES), any_space()],
        [sds((rows, cols), bf), sds((rows, width), f32), sds((1, width), f32)],
        [rows_of(block, cols), rows_of(block, width), whole((1, width))],
        [pltpu.VMEM(w_own.shape, bf), pltpu.VMEM((8, LANES), f32), pltpu.SemaphoreType.DMA],
        2 * rows * width * cols,
        core,
    )


def project_grads_kernel(sc, nt, low, gain, out):
    made = mm(nt[...], low[...])
    count = made.shape[1] // LANES
    for b in range(count):
        out[b] = made[:, b * LANES : (b + 1) * LANES].astype(bf)
    out[count] = lane_column(gain[...], (made.shape[0], LANES), 0).astype(bf)
    for b in range(count + 1, out.shape[0]):
        out[b] = jnp.zeros_like(out[b])


def project_grads(nt, low, gain, core, block=256):
    width, rows = nt.shape
    blocks = low.shape[1] // LANES + 2
    return call(
        project_grads_kernel,
        "project_grads",
        (width // block,),
        [nt, low, gain],
        [pl.BlockSpec((block, rows), lambda i, s: (i, 0)), whole(low.shape), pl.BlockSpec((1, block), lambda i, s: (0, i))],
        [sds((blocks, width, LANES), bf)],
        [pl.BlockSpec((blocks, block, LANES), lambda i, s: (0, i, 0))],
        [],
        2 * rows * width * blocks * LANES,
        core,
    )[0]


def finish_kernel(sc, tok, part, far, extra, rg, w_mine, w_theirs, out, w, sem):
    @pl.when(pl.program_id(0) == 0)
    def _():
        load_halves(sc, w_mine, w_theirs, 0, w, sem)
        pltpu.make_async_copy(w, w, sem).wait()

    grad = part[...] + mm_nt(far[...], lanes_of(w, 0, w.shape[0]))
    passed, _ = norm_back(tok[...].astype(f32), extra[0:1, :].astype(f32), grad)
    out[...] = rg[...] + passed


def finish(tokens, part, far, extra, rg, w_mine, w_theirs, core, block=256):
    rows, width = tokens.shape
    wide = rows_of(block, width)
    return call(
        finish_kernel,
        "finish",
        (rows // block,),
        [tokens, part, far, extra, rg, w_mine, w_theirs],
        [wide, wide, rows_of(block, far.shape[1]), whole(extra.shape), wide, any_space(), any_space()],
        [sds((rows, width), f32)],
        [wide],
        [pltpu.VMEM((2 * w_mine.shape[0], width, LANES), bf), pltpu.SemaphoreType.DMA],
        2 * rows * width * far.shape[1],
        core,
    )[0]


def lane_blocks(values):
    rows, cols = values.shape
    return values.reshape(rows, cols // LANES, LANES).transpose(1, 0, 2)


def unblock(values):
    return values.transpose(1, 0, 2).reshape(values.shape[1], -1)


def body(
    tokens,
    routes,
    cotangent,
    norm_one,
    w_query,
    key_weight,
    value_weight,
    w_output,
    norm_two,
    w_router,
    w_gate,
    w_up,
    w_down,
):
    count = lax.axis_size("dp")
    core = lax.axis_index("ctx")
    place = ring_place(lax.axis_index("dp"), count)
    rows, width = tokens.shape[2:]
    prompt = PROMPT_TOKENS // lax.axis_size("ctx")
    heads = w_query.shape[1] // HEAD_DIM
    kvs = key_weight.shape[1] // HEAD_DIM
    shard, hidden = w_gate.shape[1:]
    chunk = 4
    half = chunk // 2
    core_only = jnp.stack([core, core]).astype(jnp.int32)
    sources = ring_sources(place, count)

    def scalars(*more):
        return jnp.stack([*sources, *more]).astype(jnp.int32)

    with_cores = scalars(core, 1 - core)
    tok = tokens.reshape(rows, width)
    cot = cotangent.reshape(rows, width)
    ids = routes.reshape(rows, TOPK)

    extra_shard = jnp.zeros((shard, LANES), bf)
    extra_shard = extra_shard.at[:, 0].set(norm_one).at[:, 1].set(norm_two)
    extra_shard = extra_shard.at[:, ROUTER_LANE : ROUTER_LANE + EXPERTS].set(w_router)
    packed = lane_blocks(jnp.concatenate([w_query, key_weight, value_weight, extra_shard, jnp.zeros_like(extra_shard)], axis=1))
    first_half = packed.shape[0] // 2
    first_own = ring_gather(take(packed, core * first_half, first_half), count)
    first_mate = [swap(b, "ctx") for b in first_own]
    packed_out = lane_blocks(w_output)
    out_half = packed_out.shape[0] // 2
    out_own = ring_gather(take(packed_out, core * out_half, out_half), count)
    out_mate = [swap(b, "ctx") for b in out_own]

    stacked = jnp.stack([w_gate, w_up, w_down], axis=1)
    expert_bufs = []
    for base in range(0, EXPERTS, chunk):
        mine = take(stacked, base + core * half, half).reshape(half * 3, shard, hidden)
        own = ring_gather(mine, count)
        expert_bufs.append((own, [swap(b, "ctx") for b in own]))

    offsets = jnp.arange(rows, dtype=jnp.int32)
    positions = jnp.where(offsets < prompt, core * prompt + offsets, PROMPT_TOKENS + offsets - prompt)
    half_dim = HEAD_DIM // 2
    inverse = rope_base ** (-2.0 * jnp.arange(half_dim).astype(f32) / HEAD_DIM)
    angles = positions.astype(f32)[:, None] * inverse
    cosine = jnp.tile(jnp.cos(angles), (1, LANES // half_dim))
    sine = jnp.sin(angles)
    sine = jnp.tile(jnp.concatenate([-sine, sine], axis=1), (1, LANES // HEAD_DIM))

    w_first, extra, q, k, v, n1t = project(tok, cosine, sine, with_cores, first_own, first_mate, heads, kvs)
    other_k, other_v = swap(k[:, :prompt], "ctx"), swap(v[:, :prompt], "ctx")
    w_out = assemble(with_cores, out_own, out_mate, width)
    out_far_mine = swap(take(w_out, core * out_half, out_half), "tp")
    out_far_theirs = swap(out_far_mine, "ctx")
    mixed_b, lse_b = attend(q, k, v, other_k, other_v, core_only, 1)
    far_b = swap(mixed_b, "tp")
    mixed_a, lse_a = attend(q, k, v, other_k, other_v, core_only, 0)
    far_a = swap(mixed_a, "tp")
    mixed, lse = (mixed_a, mixed_b), (lse_a, lse_b)
    first_count = (heads + 2 * kvs) // 2
    first_part = first_count // 2
    w_first = w_first[:first_count]
    first_far_mine = swap(take(w_first, core * first_part, first_part), "tp")
    first_far_theirs = swap(first_far_mine, "ctx")

    res, n2, n2t, wt = settle(tok, ids, mixed, (far_a, far_b), extra, w_out, out_far_mine, out_far_theirs, core_only)
    cott = cot.T
    sums, picks, shares = None, [], []

    def reduce_chunk(keep, send):
        got = swap(send, "ctx")

        def piece(rank):
            part = lambda a: lax.dynamic_slice_in_dim(a, rank * shard, shard, 2).reshape(half * 3, shard, hidden).astype(f32)
            return part(keep) + part(got)

        return ring_scatter(piece, place, count)

    for index, (own, mate) in enumerate(expert_bufs):
        base = index * chunk
        sc = scalars(base + core * half, base + (1 - core) * half)
        last = index == len(expert_bufs) - 1
        *sums, keep, send, pick = experts(n2, n2t, cot, cott, wt, sc, own, mate, sums, last)
        picks.append(pick)
        shares.append(reduce_chunk(keep, send))
    moe_low, back_low = sums
    pick = functools.reduce(jnp.add, picks)
    back_far = swap(back_low, "tp")
    pick_far = swap(pick, "tp")
    moe_far = swap(moe_low, "tp")
    result = (res + (moe_low.astype(f32) + moe_far.astype(f32))).astype(bf).reshape(tokens.shape)

    rg, low_t, dout, ll, gain_two = unsettle((back_low, back_far), (pick, pick_far), wt, res, cot, extra, w_out, core_only)
    second = output_grads(low_t, mixed, n2t, ll, gain_two, core_only)
    dq, dk, dko, dv, dvo = attend_back(q, k, v, other_k, other_v, dout, mixed, lse, cosine, sine, core_only)
    dkx, dvx = swap(dko, "ctx"), swap(dvo, "ctx")
    low, part, gain_one = unproject(tok, dq, dk, dkx, dv, dvx, cosine, sine, w_first, core_only)
    far = swap(low, "tp")
    first = project_grads(n1t, low, gain_one, core_only)
    token_grad = finish(tok, part, far, extra, rg, first_far_mine, first_far_theirs, core_only).reshape(tokens.shape)

    def reduce_blocks(grads):
        size = grads.shape[0] // 2
        keep = take(grads, core * size, size)
        got = swap(take(grads, (1 - core) * size, size), "ctx")

        def piece(rank):
            part = lambda a: lax.dynamic_slice_in_dim(a, rank * shard, shard, 1).astype(f32)
            return part(keep) + part(got)

        mine = ring_scatter(piece, place, count)
        theirs = swap(mine, "ctx")
        return jnp.concatenate([jnp.where(core == 0, mine, theirs), jnp.where(core == 0, theirs, mine)], axis=0)

    second = reduce_blocks(second)
    first = reduce_blocks(first)
    q_blocks, kv_blocks = heads // 2, kvs // 2
    grad_query = unblock(first[:q_blocks])
    grad_key = unblock(first[q_blocks : q_blocks + kv_blocks])
    grad_value = unblock(first[q_blocks + kv_blocks : q_blocks + 2 * kv_blocks])
    gain_part = first[q_blocks + 2 * kv_blocks][:, 0]
    grad_norm_one = gain_part + swap(gain_part, "tp")
    grad_output = unblock(second[:q_blocks])
    grad_norm_two = second[q_blocks][:, 1]
    grad_router = second[q_blocks][:, ROUTER_LANE : ROUTER_LANE + EXPERTS]

    parts = []
    for mine in shares:
        theirs = swap(mine, "ctx")
        parts += [jnp.where(core == 0, mine, theirs), jnp.where(core == 0, theirs, mine)]
    owned = jnp.concatenate(parts, axis=0).reshape(EXPERTS, 3, shard, hidden)
    return (
        result,
        token_grad,
        grad_norm_one,
        grad_query,
        grad_key,
        grad_value,
        grad_output,
        grad_norm_two,
        grad_router,
        owned[:, 0],
        owned[:, 1],
        owned[:, 2],
    )


def solution(mesh):
    slab = P("dp", "ctx", None, None)
    split, rows_only, expert = P("dp", "tp"), P("dp"), P(None, "dp", "tp")
    return jax.shard_map(
        body,
        mesh=mesh,
        in_specs=(slab, slab, slab, rows_only, split, split, split, split, rows_only, P("dp", None), expert, expert, expert),
        out_specs=(slab, slab, rows_only, split, split, split, split, rows_only, P("dp", None), expert, expert, expert),
        check_vma=False,
    )
```

```python
import functools

import jax
import jax.numpy as jnp
from jax import lax
from jax.experimental import pallas as pl
from jax.experimental.pallas import tpu as pltpu
from jax.sharding import PartitionSpec as P

HEAD_DIM = 64
EXPERTS = 16
TOPK = 8
PROMPT_TOKENS = 1024
LANES = 128
ROUTER_LANE = 16

norm_eps = 1e-06
rope_base = 10000.0
masked_score = -1e30
bf = jnp.bfloat16
f32 = jnp.float32
contract_cols = (((1,), (1,)), ((), ()))
vmem_bytes = 63 * 1024 * 1024


def mm(a, b):
    return jnp.dot(a, b, preferred_element_type=f32)


def mm_nt(a, b):
    return lax.dot_general(a, b, contract_cols, preferred_element_type=f32)


def whole(shape):
    return pl.BlockSpec(shape, lambda *_: (0,) * len(shape), pipeline_mode=pl.Buffered(1))


def rows_of(block, width):
    return pl.BlockSpec((block, width), lambda i, *_: (i, 0))


def any_space():
    return pl.BlockSpec(memory_space=pltpu.HBM)


def call(kernel, name, grid, ins, in_specs, outs, out_specs, scratch, flops, scalars, deps=(), limit=vmem_bytes, aliases=None):
    moved = sum(a.size * a.dtype.itemsize for a in (*ins, *outs))
    return pl.pallas_call(
        lambda sc, *refs: kernel(sc, *refs[len(deps) :]),
        out_shape=tuple(outs),
        grid_spec=pltpu.PrefetchScalarGridSpec(
            num_scalar_prefetch=1,
            grid=grid,
            in_specs=[pl.BlockSpec(memory_space=pltpu.HBM) for _ in deps] + list(in_specs),
            out_specs=tuple(out_specs),
            scratch_shapes=scratch,
        ),
        compiler_params=pltpu.CompilerParams(vmem_limit_bytes=limit),
        cost_estimate=pl.CostEstimate(flops=60_000_000_000 if flops else 1, bytes_accessed=int(moved), transcendentals=0),
        name=name,
        input_output_aliases=aliases or {},
    )(scalars, *deps, *ins)


def after(values, *deps):
    return lax.optimization_barrier((values, *deps))[0]


def sds(shape, dtype):
    return jax.ShapeDtypeStruct(tuple(shape), dtype)


def ring_rank(place, count):
    place = lax.rem(place + 2 * count, count)
    return jnp.where(place < count // 2, 2 * place, 2 * count - 1 - 2 * place)


def ring_place(rank, count):
    return jnp.where(rank % 2 == 0, rank // 2, (2 * count - 1 - rank) // 2)


def ring_hop(values, count):
    order = list(range(0, count, 2)) + list(range(count - 1, 0, -2))
    pairs = []
    for k in range(count):
        here, there = order[k], order[(k + 1) % count]
        pairs += [(2 * here, 2 * there), (2 * there + 1, 2 * here + 1)]
    return sent(lax.ppermute(values, ("dp", "ctx"), pairs))


def swap(values, axis):
    return sent(lax.ppermute(values, axis, [(0, 1), (1, 0)]))


class Window:
    def __init__(self):
        self.now, self.before = [], []

    def turn(self):
        due, self.before, self.now = self.before, self.now, []
        return due


window = Window()


def sent(values):
    window.now.append(values)
    return values


def take(values, start, size, axis=0):
    return lax.dynamic_slice_in_dim(values, start, size, axis)


def place_half(values, core, axis):
    zeros = jnp.zeros_like(values)
    return jnp.where(core == 0, jnp.concatenate([values, zeros], axis), jnp.concatenate([zeros, values], axis))


PLANNED = 4


class Gather:
    def __init__(self, own, core, count, axis):
        self.own, self.core, self.count, self.axis = own, core, count, axis
        self.mine, self.mate, self.hops = [], [], 0

    def share(self, *held):
        if len(self.mate) < len(self.mine):
            self.mate.append(swap(after(self.mine[-1], *held), "ctx"))

    def step(self, *held):
        for _ in range(1 if self.hops else self.count // 2 - PLANNED + 1):
            got = self.hop(*held)
        return got

    def hop(self, *held):
        self.share(*held)
        self.hops += 1
        last = after(self.mine[-1] if self.mine else self.own, *held)
        if self.hops == self.count // 2:
            size = last.shape[self.axis] // 2
            last = take(last, self.core * size, size, self.axis)
        self.mine.append(ring_hop(last, self.count))
        return self.mine[-1]

    def finish(self):
        while self.hops < self.count // 2:
            self.step()
        self.share()
        return self

    @property
    def bufs(self):
        return [self.own, *self.mine, *self.mate]


def gather_sources(place, core, count):
    sign = 1 - 2 * core
    away = list(range(1, count // 2 + 1))
    return [ring_rank(place, count)] + [ring_rank(place - sign * a, count) for a in away] + [ring_rank(place + sign * a, count) for a in away]


def scatter_sources(place, core, count):
    sign = 1 - 2 * core
    away = list(range(1, count // 2))
    keep = [ring_rank(place + sign * a, count) for a in away] + [ring_rank(place + count // 2, count)]
    send = [ring_rank(place - sign * a, count) for a in away] + [ring_rank(place, count)]
    return keep + send


class Scatter:
    def __init__(self, core, count, scalars, core_at):
        self.core, self.count, self.scalars, self.core_at = core, count, scalars, core_at
        self.keeps, self.gots, self.hops, self.got = [], [], 0, None

    def add(self, keep, send, *held):
        self.keeps.append(keep)
        self.gots.append(swap(after(send, *held), "ctx"))
        return self.gots[-1]

    def step(self, deps=()):
        for _ in range(1 if self.hops else self.count // 2 - PLANNED + 1):
            got = self.hop(deps)
        return got

    def hop(self, deps):
        self.hops += 1
        stage = {1: None, 2: "second"}.get(self.hops, "middle")
        slot = self.count // 2 - self.hops if self.hops > 1 else self.count // 2 - 1
        value = hop_sum(self.keeps, self.gots, self.got, slot, stage, self.scalars, self.core_at, deps)
        self.got = ring_hop(value, self.count)
        return self.got

    def finish(self, deps=()):
        while self.hops < self.count // 2:
            self.step()
        mine = hop_sum(self.keeps, self.gots, self.got, self.count // 2 - 1, "end", self.scalars, self.core_at, deps)
        return mine, swap(mine, "ctx")


def load_shards(sc, bufs, dst, shard, sem):
    total = len(bufs)
    hops = total // 2
    half = dst.shape[0] // 2
    for k, buf in enumerate(bufs):
        rows = pl.ds(pl.multiple_of(sc[k] * shard, shard), shard)
        if k in (hops, 2 * hops):
            side = sc[total] if k == hops else 1 - sc[total]
            target = dst.at[pl.ds(side * half, half), rows, :]
        else:
            target = dst.at[:, rows, :]
        pltpu.make_async_copy(buf, target, sem).start()


def lanes_of(ref, first, count):
    return jnp.concatenate([ref[first + b] for b in range(count)], axis=1)


def rope(x, cosine, sine):
    lane = lax.broadcasted_iota(jnp.int32, x.shape, x.ndim - 1)
    ahead = pltpu.roll(x, x.shape[-1] - HEAD_DIM // 2, x.ndim - 1)
    behind = pltpu.roll(x, HEAD_DIM // 2, x.ndim - 1)
    return x * cosine + jnp.where(lax.rem(lane, HEAD_DIM) < HEAD_DIM // 2, ahead, behind) * sine


def lane_column(row, shape, lane_at):
    lane = lax.broadcasted_iota(jnp.int32, shape, 1)
    return jnp.where(lane == lane_at, jnp.broadcast_to(row, (shape[1], shape[0])).T, 0.0)


def pack_kernel(sc, query, key, value, output, router, gain_one, gain_two, out):
    at = 0
    for ref in (query, key, value):
        for b in range(ref.shape[1] // LANES):
            out[at] = ref[:, b * LANES : (b + 1) * LANES]
            at += 1
    shape = out.shape[1:]
    extra = lane_column(gain_one[...].astype(f32), shape, 0) + lane_column(gain_two[...].astype(f32), shape, 1)
    out[at] = extra.astype(bf)
    out[at, :, ROUTER_LANE : ROUTER_LANE + EXPERTS] = router[...]
    for b in range(output.shape[1] // LANES):
        out[at + 1 + b] = output[:, b * LANES : (b + 1) * LANES]
    for b in range(at + 1 + output.shape[1] // LANES, out.shape[0]):
        out[b] = jnp.zeros(shape, bf)


def pack(query, key, value, output, router, gain_one, gain_two, core):
    shard = query.shape[0]
    ins = [query, key, value, output, router, gain_one.reshape(1, shard), gain_two.reshape(1, shard)]
    blocks = (query.shape[1] + key.shape[1] + value.shape[1] + output.shape[1]) // LANES + 1
    blocks += blocks % 2
    out = sds((blocks, shard, LANES), bf)
    return call(pack_kernel, "pack", (1,), ins, [whole(a.shape) for a in ins], [out], [whole(out.shape)], [], 0, core)[0]


def qkv_kernel(shard, kinds, sc, tok, cosine, sine, *refs):
    heads, kvs, total = kinds
    bufs, (w_first, w_out, w_half, extra_out, q_out, kv_out, packed_out, nt_out, w, et, sem, out_sem) = refs[:total], refs[total:]
    step = pl.program_id(0)
    count, half = w_first.shape[0], w_half.shape[0]
    copies = [
        (w.at[pl.ds(0, count)], w_first),
        (w.at[pl.ds(count + 1, 2 * half)], w_out),
        (w.at[pl.ds(count + 1 + sc[total] * half, half)], w_half),
    ]

    @pl.when(step == 0)
    def _():
        load_shards(sc, bufs, w, shard, sem)
        pltpu.make_async_copy(w, w, sem).wait()
        for k, (src, dst) in enumerate(copies):
            pltpu.make_async_copy(src, dst, out_sem.at[k]).start()
        et[...] = w[count].T

    extra_out[...] = et[...]
    x = tok[...].astype(f32)
    scale = lax.rsqrt(jnp.mean(x * x, axis=-1, keepdims=True) + norm_eps)
    normed = (x * scale * et[0:1, :].astype(f32)).astype(bf)
    nt_out[...] = normed.T
    cs, sn = cosine[...], sine[...]
    for pair in range((heads + 2 * kvs) // 4):
        made = mm(normed, lanes_of(w, 2 * pair, 2))
        for side in range(2):
            first = 4 * pair + 2 * side
            part = made[:, side * LANES : (side + 1) * LANES]
            if first < heads + kvs:
                part = rope(part, cs, sn)
            out, at = kv_out, first - heads
            if first < heads:
                part, out, at = part * (1.0 / HEAD_DIM), q_out, first
            low = part.astype(bf)
            for k in range(2):
                one = low[:, k * HEAD_DIM : (k + 1) * HEAD_DIM]
                out[at + k] = one
                if first >= heads:
                    for quarter in range(2):

                        @pl.when(step == quarter)
                        def _():
                            packed_out[at + k, :, quarter * HEAD_DIM : (quarter + 1) * HEAD_DIM] = one

    @pl.when(step == pl.num_programs(0) - 1)
    def _():
        for k, (src, dst) in enumerate(copies):
            pltpu.make_async_copy(src, dst, out_sem.at[k]).wait()


def project(tokens, cosine, sine, scalars, bufs, heads, kvs, prompt, deps, block=256):
    rows, width = tokens.shape
    blocks, shard = bufs[0].shape[:2]
    count = (heads + 2 * kvs) // 2
    head_spec = lambda n: pl.BlockSpec((n, block, HEAD_DIM), lambda i, s: (0, i, 0))
    outs = [
        sds((count, width, LANES), bf),
        sds((heads // 2, width, LANES), bf),
        sds((heads // 4, width, LANES), bf),
        sds((LANES, width), bf),
        sds((heads, rows, HEAD_DIM), bf),
        sds((2 * kvs, rows, HEAD_DIM), bf),
        sds((2 * kvs, prompt // 2, LANES), bf),
        sds((width, rows), bf),
    ]
    return call(
        functools.partial(qkv_kernel, shard, (heads, kvs, len(bufs))),
        "project",
        (rows // block,),
        [tokens, cosine, sine, *bufs],
        [rows_of(block, width), rows_of(block, LANES), rows_of(block, LANES)] + [any_space()] * len(bufs),
        outs,
        [
            any_space(),
            any_space(),
            any_space(),
            whole((LANES, width)),
            head_spec(heads),
            head_spec(2 * kvs),
            whole((2 * kvs, prompt // 2, LANES)),
            pl.BlockSpec((width, block), lambda i, s: (0, i)),
        ],
        [
            pltpu.VMEM((blocks, width, LANES), bf),
            pltpu.VMEM((LANES, width), bf),
            pltpu.SemaphoreType.DMA,
            pltpu.SemaphoreType.DMA((3,)),
        ],
        2 * rows * width * count * LANES,
        scalars,
        deps,
    )


def causal(scores):
    key = lax.broadcasted_iota(jnp.int32, scores.shape, 0)
    query = lax.broadcasted_iota(jnp.int32, scores.shape, 1)
    return jnp.where(key <= query, scores, masked_score)


def block_scores(query, keys, other_keys, at, block, prompt, bias):
    parts = []
    if at:
        parts.append(mm_nt(keys[0:at], query))
    parts.append(causal(mm_nt(keys[at : at + block], query)))
    other = mm_nt(other_keys, query)
    if at < prompt:
        other = other + bias
    parts.append(other)
    return parts


def unpack(ref):
    return jnp.concatenate([ref[0, :, :HEAD_DIM], ref[0, :, HEAD_DIM:]], axis=0)


def attend_kernel(cfg, sc, q, k0, k1, o0, o1, v0, v1, w0, w1, mixed, lse):
    starts, block, prompt = cfg
    bias = jnp.where(sc[0] == 0, masked_score, 0.0).astype(f32)
    for side, (keys, other, values, other_values) in enumerate(((k0, o0, v0, w0), (k1, o1, v1, w1))):
        values_t = values[0].T
        other_t = unpack(other_values).T
        other_keys = unpack(other)
        for a, at in enumerate(starts):
            rows = slice(a * block, a * block + block)
            scores = block_scores(q[side, rows, :], keys[0], other_keys, at, block, prompt, bias)
            peak = functools.reduce(jnp.maximum, [jnp.max(s, axis=0, keepdims=True) for s in scores])
            raw = [jnp.exp(s - peak) for s in scores]
            total = sum(jnp.sum(r, axis=0, keepdims=True) for r in raw)
            low = [r.astype(bf) for r in raw]
            out = mm(other_t, low[-1]) + mm(values_t[:, at : at + block], low[-2])
            if at:
                out = out + mm(values_t[:, 0:at], low[0])
            out = out * (1.0 / total)
            mixed[rows, side * HEAD_DIM : side * HEAD_DIM + HEAD_DIM] = out.T.astype(bf)
            lse[0, side : side + 1, rows] = peak + jnp.log(total)


def kv_specs(kvs, rows, prompt, rep, first_pair):
    index = lambda side, base: (lambda p, s: (base + (2 * (p + first_pair) + side) // rep, 0, 0))
    specs = []
    for base in (0, kvs):
        specs += [pl.BlockSpec((1, rows, HEAD_DIM), index(side, base)) for side in range(2)]
        specs += [pl.BlockSpec((1, prompt // 2, LANES), index(side, base)) for side in range(2)]
    return specs


def attend(q, kv, other, core, part, deps, block=256):
    heads, rows, _ = q.shape
    kvs, prompt = other.shape[0] // 2, 2 * other.shape[1]
    count = prompt if part == 0 else rows - prompt
    first = 0 if part == 0 else prompt
    starts = tuple(range(first, first + count, block))
    return call(
        functools.partial(attend_kernel, (starts, block, prompt)),
        "attend",
        (heads // 2,),
        [q, kv, kv, other, other, kv, kv, other, other],
        [pl.BlockSpec((2, count, HEAD_DIM), lambda p, s: (p, part, 0)), *kv_specs(kvs, rows, prompt, heads // kvs, 0)],
        [sds((count, heads * HEAD_DIM), bf), sds((heads // 2, 2, count), f32)],
        [
            pl.BlockSpec((count, LANES), lambda p, s: (0, p)),
            pl.BlockSpec((1, 2, count), lambda p, s: (p, 0, 0)),
        ],
        [],
        16 * heads * count * 1024 * HEAD_DIM,
        core,
        deps,
    )


def attend_back_kernel(cfg, sc, q, k0, k1, o0, o1, v0, v1, w0, w1, dout, mixed_a, mixed_b, lse_a, lse_b, cosine, sine, dq, dkv, dother_out, dother):
    rows_total, block, prompt, rep = cfg
    pair = pl.program_id(0)
    bias = jnp.where(sc[0] == 0, masked_score, 0.0).astype(f32)
    kvs = dkv.shape[0] // 2

    @pl.when(pair == 0)
    def _():
        dkv[...] = jnp.zeros_like(dkv)
        dother[...] = jnp.zeros_like(dother)

    heads = ((k0, unpack(o0), v0, unpack(w0)), (k1, unpack(o1), v1, unpack(w1)))
    keys_t = [(keys[0].T, other.T) for keys, other, _, _ in heads]
    for at in range(0, rows_total, block):
        rows = slice(at, at + block)
        mixed, lse, local = (mixed_a, lse_a, at) if at < prompt else (mixed_b, lse_b, at - prompt)
        inner = slice(local, local + block)
        dot = (dout[rows, :].astype(f32) * mixed[inner, :].astype(f32)).T
        grads = []
        for side, (keys, other, values, other_values) in enumerate(heads):
            head = (2 * pair + side) // rep
            query = q[side, rows, :]
            grad = dout[rows, side * HEAD_DIM : side * HEAD_DIM + HEAD_DIM]
            weighted = jnp.sum(dot[side * HEAD_DIM : side * HEAD_DIM + HEAD_DIM], axis=0, keepdims=True)
            norm = lse[0, side : side + 1, inner]
            scores = block_scores(query, keys[0], other, at, block, prompt, bias)
            spans = ([(False, 0, at)] if at else []) + [(False, at, block), (True, 0, prompt)]
            back = None
            for score, (is_other, first, size) in zip(scores, spans):
                probs = jnp.exp(score - norm)
                value = other_values if is_other else values[0, first : first + size]
                score_low = (probs * (mm_nt(value, grad) - weighted)).astype(bf)
                sums = dother if is_other else dkv
                span = pl.ds(first, size)
                sums[kvs + head, span, :] += mm(probs.astype(bf), grad)
                sums[head, span, :] += mm(score_low, query)
                key_t = keys_t[side][1] if is_other else keys_t[side][0][:, first : first + size]
                term = mm(key_t, score_low)
                back = term if back is None else back + term
            grads.append(back)
        both = jnp.concatenate(grads, axis=0).T * (1.0 / HEAD_DIM)
        dq[rows, :] = rope(both, cosine[rows, :], -sine[rows, :]).astype(bf)

    @pl.when(pair == pl.num_programs(0) - 1)
    def _():
        for h in range(dother.shape[0]):
            for quarter in range(2):
                part = dother[h, quarter * (prompt // 2) : (quarter + 1) * (prompt // 2), :]
                dother_out[h, :, quarter * HEAD_DIM : (quarter + 1) * HEAD_DIM] = part


def attend_back(q, kv, other, dout, mixed, lse, cosine, sine, core, part, parts, deps, block=256):
    heads, rows, _ = q.shape
    kvs, prompt = other.shape[0] // 2, 2 * other.shape[1]
    pairs = heads // 2 // parts
    first = part * pairs
    mine = 2 * kvs // parts
    pair = pl.BlockSpec((rows, LANES), lambda p, s: (0, p + first))
    mixed_spec = lambda a: pl.BlockSpec((a.shape[0], LANES), lambda p, s: (0, p + first))
    lse_spec = lambda a: pl.BlockSpec((1, 2, a.shape[2]), lambda p, s: (p + first, 0, 0))
    return call(
        functools.partial(attend_back_kernel, (rows, block, prompt, heads // kvs)),
        "attend_back",
        (pairs,),
        [q, kv, kv, other, other, kv, kv, other, other, dout, *mixed, *lse, cosine, sine],
        [
            pl.BlockSpec((2, rows, HEAD_DIM), lambda p, s: (p + first, 0, 0)),
            *kv_specs(kvs, rows, prompt, heads // kvs, first),
            pair,
            *[mixed_spec(a) for a in mixed],
            *[lse_spec(a) for a in lse],
            whole(cosine.shape),
            whole(sine.shape),
        ],
        [
            sds((rows, pairs * LANES), bf),
            sds((mine, rows, HEAD_DIM), f32),
            sds((mine, prompt // 2, LANES), f32),
        ],
        [
            pl.BlockSpec((rows, LANES), lambda p, s: (0, p)),
            whole((mine, rows, HEAD_DIM)),
            whole((mine, prompt // 2, LANES)),
        ],
        [pltpu.VMEM((mine, prompt, HEAD_DIM), f32)],
        40 * heads // parts * rows * 1024 * HEAD_DIM,
        core,
        deps,
    )


def load_halves(sc, mine, theirs, first_block, w, sem):
    half = mine.shape[0]
    pltpu.make_async_copy(mine, w.at[pl.ds(first_block + sc[0] * half, half)], sem).start()
    pltpu.make_async_copy(theirs, w.at[pl.ds(first_block + (1 - sc[0]) * half, half)], sem).start()


def settle_kernel(sc, tok, ids, own_a, own_b, far_a, far_b, extra, w_own, w_mine, w_theirs, res_out, n_out, nt_out, wt_out, w, sem):
    step = pl.program_id(0)
    blocks = w_own.shape[0]

    @pl.when(step == 0)
    def _():
        pltpu.make_async_copy(w_own, w.at[pl.ds(0, blocks)], sem).start()
        load_halves(sc, w_mine, w_theirs, blocks, w, sem)
        pltpu.make_async_copy(w, w, sem).wait()

    early = step < pl.num_programs(0) // 2
    own = jnp.where(early, own_a[...], own_b[...])
    far = jnp.where(early, far_a[...], far_b[...])
    branch = mm_nt(own, lanes_of(w, 0, blocks)) + mm_nt(far, lanes_of(w, blocks, blocks))
    residual = tok[...].astype(f32) + branch
    res_out[...] = residual
    scale = lax.rsqrt(jnp.mean(residual * residual, axis=-1, keepdims=True) + norm_eps)
    normed = (residual * scale * extra[1:2, :].astype(f32)).astype(bf)
    n_out[...] = normed
    nt_out[...] = normed.T
    logits = mm_nt(normed, extra[...])
    lane = lax.broadcasted_iota(jnp.int32, logits.shape, 1)
    routed = lane < 0
    for k in range(TOPK):
        routed = jnp.logical_or(routed, lane == ids[:, k : k + 1] + ROUTER_LANE)
    logits = jnp.where(routed, logits, masked_score)
    raw = jnp.where(routed, jnp.exp(logits - jnp.max(logits, axis=-1, keepdims=True)), 0.0)
    wt_out[...] = raw / jnp.sum(raw, axis=-1, keepdims=True)


def settle(tokens, ids, own, far, extra, w_own, w_mine, w_theirs, core, deps, block=256):
    rows, width = tokens.shape
    halves = rows // block // 2
    cols = own[0].shape[1]
    low = pl.BlockSpec((block, cols), lambda i, s: (jnp.minimum(i, halves - 1), 0))
    high = pl.BlockSpec((block, cols), lambda i, s: (jnp.maximum(i - halves, 0), 0))
    return call(
        settle_kernel,
        "settle",
        (rows // block,),
        [tokens, ids, *own, *far, extra, w_own, w_mine, w_theirs],
        [rows_of(block, width), rows_of(block, TOPK), low, high, low, high, whole(extra.shape)] + [any_space()] * 3,
        [sds((rows, width), f32), sds((rows, width), bf), sds((width, rows), bf), sds((rows, LANES), f32)],
        [rows_of(block, width), rows_of(block, width), pl.BlockSpec((width, block), lambda i, s: (0, i)), rows_of(block, LANES)],
        [pltpu.VMEM((2 * w_own.shape[0], width, LANES), bf), pltpu.SemaphoreType.DMA],
        4 * rows * width * cols,
        core,
        deps,
    )


def mix_halves(core, kept, sent):
    first = jnp.concatenate([kept[0], sent[0]], axis=-1)
    second = jnp.concatenate([kept[1], sent[1]], axis=-1)
    return jnp.where(core == 0, first, second), jnp.where(core == 0, second, first)


def experts_kernel(cfg, sc, *refs):
    shard, hidden, local, first, last, total = cfg
    block = 256
    it = iter(refs)
    n2, n2t, cot, cott, wt = (next(it) for _ in range(5))
    bufs = [next(it) for _ in range(total)]
    sums_in = () if first else (next(it), next(it))
    pick_in = None if first else next(it)
    moe_out, back_out, keep, send, pick = (next(it) for _ in range(5))
    pick_t = next(it) if last else None
    xs, cs, xt, ct, w, moe, back, scaled, acts, keep_s, send_s = (next(it) for _ in range(11))
    w_sem, x_sem, c_sem, t_sem, in_sem, out_sem, g_sem = (next(it) for _ in range(7))
    rows_total, width = xs.shape
    hops = total // 2
    core = sc[total]
    ranks = total + 1
    slots = hops
    lead = ranks + 2 * slots

    for side in range(2):
        for k, buf in enumerate(bufs):
            rows = pl.ds(pl.multiple_of(sc[k] * shard, shard), shard)
            lanes = pl.ds(side * hidden, hidden)
            if k in (hops, 2 * hops):
                at = core if k == hops else 1 - core
                lanes = pl.ds(pl.multiple_of(side * hidden + at * (hidden // 2), LANES), hidden // 2)
            pltpu.make_async_copy(buf.at[:, local + side], w.at[:, rows, lanes], w_sem).start()
    spans = [pl.ds(at, block) for at in range(0, rows_total, block)]
    for i, rows in enumerate(spans):
        pltpu.make_async_copy(n2.at[rows], xs.at[rows], x_sem.at[i]).start()
        pltpu.make_async_copy(cot.at[rows], cs.at[rows], c_sem.at[i]).start()
    pltpu.make_async_copy(w, w, w_sem).wait()
    lane = lax.broadcasted_iota(jnp.int32, (block, LANES), 1)
    ids = [sc[lead + side] + ROUTER_LANE for side in range(2)]
    for i, rows in enumerate(spans):
        pltpu.make_async_copy(n2.at[rows], xs.at[rows], x_sem.at[i]).wait()
        pltpu.make_async_copy(cot.at[rows], cs.at[rows], c_sem.at[i]).wait()
        if i == 1:
            for k, (src, dst) in enumerate(zip(sums_in, (moe, back))):
                pltpu.make_async_copy(src, dst, in_sem.at[k]).start()
            pltpu.make_async_copy(n2t, xt, t_sem.at[0]).start()
            pltpu.make_async_copy(cott, ct, t_sem.at[1]).start()
        x = xs[rows, :]
        gate = mm(x, w[0])
        up = mm(x, w[1])
        grad = mm(cs[rows, :], w[2])
        table = wt[rows, :]
        sig = 1.0 / (1.0 + jnp.exp(-gate))
        silu = gate * sig
        act = silu * up
        dots = act * grad
        picked = jnp.zeros(table.shape, f32) if first else pick_in[rows, :]
        for side, expert in enumerate(ids):
            cols = slice(side * hidden, side * hidden + hidden)
            weight = jnp.sum(jnp.where(lane == expert, table, 0.0), axis=1, keepdims=True)
            picked = picked + jnp.where(lane == expert, jnp.sum(dots[:, cols], axis=1, keepdims=True), 0.0)
            scaled[rows, cols] = (act[:, cols] * weight).astype(bf)
            g = grad[:, cols] * weight
            s = sig[:, cols]
            acts[rows, cols] = (g * up[:, cols] * s * (1.0 + gate[:, cols] * (1.0 - s))).astype(bf)
            acts[rows, slice((2 + side) * hidden, (3 + side) * hidden)] = (g * silu[:, cols]).astype(bf)
        pick[rows, :] = picked
        if last:
            pick_t[:, rows] = picked.T[ROUTER_LANE : ROUTER_LANE + EXPERTS]

    for k, (src, dst) in enumerate(zip(sums_in, (moe, back))):
        pltpu.make_async_copy(src, dst, in_sem.at[k]).wait()
    outs = [(xs, moe_out), (cs, back_out)] if last else [(moe, moe_out), (back, back_out)]
    for rows in spans:
        one = mm_nt(scaled[rows, :], w[2])
        two = mm_nt(acts[rows, 0 : 2 * hidden], w[0]) + mm_nt(acts[rows, 2 * hidden :], w[1])
        if not first:
            one, two = one + moe[rows, :], two + back[rows, :]
        for made, (scr, out), s in zip((one, two), outs, range(2)):
            scr[rows, :] = made.astype(scr.dtype)
            pltpu.make_async_copy(scr.at[rows], out.at[rows], out_sem.at[s]).start()

    pltpu.make_async_copy(n2t, xt, t_sem.at[0]).wait()
    pltpu.make_async_copy(cott, ct, t_sem.at[1]).wait()
    for slot in range(slots):
        at = [pl.ds(pl.multiple_of(sc[ranks + slots * k + slot] * shard, shard), shard) for k in range(2)]
        left = lambda ref: jnp.concatenate([ref[at[0], :], ref[at[1], :]], axis=0)
        gate_up = mm(left(xt), acts[...]).astype(bf)
        down = mm(left(ct), scaled[...]).astype(bf)
        kinds = (gate_up[:, : 2 * hidden], gate_up[:, 2 * hidden :], down)
        for kind, made in enumerate(kinds):
            for side in range(2):
                part = made[:, side * hidden : side * hidden + hidden]
                kept, sent = part[:shard], part[shard:]
                if slot == slots - 1:
                    cut = lambda a: (a[:, : hidden // 2], a[:, hidden // 2 :])
                    kept, sent = mix_halves(core, cut(kept), cut(sent))
                keep_s[slot, side * 3 + kind] = kept
                send_s[slot, side * 3 + kind] = sent
        pltpu.make_async_copy(keep_s.at[slot], keep.at[slot], g_sem.at[0]).start()
        pltpu.make_async_copy(send_s.at[slot], send.at[slot], g_sem.at[1]).start()

    for (scr, out), s in zip(outs, range(2)):
        pltpu.make_async_copy(scr, out, out_sem.at[s]).wait()
    pltpu.make_async_copy(keep_s, keep, g_sem.at[0]).wait()
    pltpu.make_async_copy(send_s, send, g_sem.at[1]).wait()


def experts(n2, n2t, cot, cott, wt, scalars, bufs, local, sums, last, deps):
    rows, width = n2.shape
    shard, hidden = bufs[0].shape[2:]
    slots = len(bufs) // 2
    first = sums is None
    ins = [n2, n2t, cot, cott, wt, *bufs, *([] if first else sums)]
    specs = [any_space()] * 4 + [whole(wt.shape)] + [any_space()] * (len(ins) - 5)
    if not first:
        specs[-1] = whole((rows, LANES))
    kind = bf if last else f32
    dma = pltpu.SemaphoreType.DMA
    return call(
        functools.partial(experts_kernel, (shard, hidden, local, first, last, len(bufs))),
        "experts",
        (1,),
        ins,
        specs,
        [
            sds((rows, width), kind),
            sds((rows, width), kind),
            sds((slots, 6, shard, hidden), bf),
            sds((slots, 6, shard, hidden), bf),
            sds((rows, LANES), f32),
        ]
        + ([sds((EXPERTS, rows), f32)] if last else []),
        [any_space()] * 4 + [whole((rows, LANES))] + ([whole((EXPERTS, rows))] if last else []),
        [
            pltpu.VMEM((rows, width), bf),
            pltpu.VMEM((rows, width), bf),
            pltpu.VMEM((width, rows), bf),
            pltpu.VMEM((width, rows), bf),
            pltpu.VMEM((3, width, 2 * hidden), bf),
            pltpu.VMEM((rows, width), f32),
            pltpu.VMEM((rows, width), f32),
            pltpu.VMEM((rows, 2 * hidden), bf),
            pltpu.VMEM((rows, 4 * hidden), bf),
            pltpu.VMEM((slots, 6, shard, hidden), bf),
            pltpu.VMEM((slots, 6, shard, hidden), bf),
            dma,
            dma((rows // 256,)),
            dma((rows // 256,)),
            dma((2,)),
            dma((2,)),
            dma((2,)),
            dma((2,)),
        ],
        36 * rows * width * hidden,
        scalars,
        deps,
    )


def hop_kernel(cfg, sc, *refs):
    pairs, stage, core_at = cfg
    core = sc[core_at]
    it = iter(refs)
    keeps = [next(it) for _ in range(pairs)]
    gots = [next(it) for _ in range(pairs)]
    came = next(it) if stage else None
    out = next(it)
    for p in range(pairs):
        total = keeps[p][0].astype(f32) + gots[p][0].astype(f32)
        if stage == "end":
            total = place_half(total, core, 2) + came[p].astype(f32)
        elif stage == "second":
            total = total + place_half(came[p].astype(f32), core, 2)
        elif stage:
            total = total + came[p].astype(f32)
        out[p] = total.astype(bf)


def hop_sum(keeps, gots, came, slot, stage, scalars, core_at, deps=()):
    pairs = len(keeps)
    slots, mats, shard, hidden = keeps[0].shape
    lanes = hidden // 2 if stage in (None, "end") else hidden
    side = 1 if stage == "end" else 0
    per = mats // 2
    piece = pl.BlockSpec((1, per, shard, lanes), lambda m, s: (slot, m, 0, side))
    wide = lambda a: pl.BlockSpec((pairs, per, shard, a.shape[3]), lambda m, s: (0, m, 0, 0))
    out = sds((pairs, mats, shard, hidden // 2 if stage is None else hidden), bf)
    ins = [*keeps, *gots] + ([] if came is None else [came])
    specs = [piece] * (2 * pairs) + ([] if came is None else [wide(came)])
    kernel = functools.partial(hop_kernel, (pairs, stage, core_at))
    return call(kernel, "hop_sum", (2,), ins, specs, [out], [wide(out)], [], 0, scalars, deps)[0]


def emit_kernel(sc, mine, theirs, *refs):
    for m in range(6):
        refs[m % 3 - 3][m // 3] = mine[0, m].astype(f32) + theirs[0, m].astype(f32)


def emit(group, first, total, into, core, deps):
    pairs, mats, shard, hidden = group[0].shape
    ins = [*group, *(into or [])]
    spec = pl.BlockSpec((1, mats, shard, hidden), lambda i, s: (i, 0, 0, 0))
    out_spec = pl.BlockSpec((2, shard, hidden), lambda i, s: (i + first // 2, 0, 0))
    outs = [sds((total, shard, hidden), f32)] * 3
    aliases = {1 + len(deps) + 2 + k: k for k in range(3)} if into else {}
    specs = [spec, spec] + [any_space()] * (len(ins) - 2)
    return call(emit_kernel, "emit", (pairs,), ins, specs, outs, [out_spec] * 3, [], 0, core, deps, aliases=aliases)


def norm_back(values, gain, grad):
    scale = lax.rsqrt(jnp.mean(values * values, axis=-1, keepdims=True) + norm_eps)
    inner = jnp.mean(values * gain * grad, axis=-1, keepdims=True)
    passed = scale * gain * grad - values * (scale * scale * scale * inner)
    return passed, jnp.sum(grad * values * scale, axis=0, keepdims=True)


def unsettle_kernel(sc, back_a, back_b, pick_a, pick_b, wt, res, cot, extra, w_own, rg_out, low_t_out, dout_out, ll_out, gain_out, w, sem):
    step = pl.program_id(0)

    @pl.when(step == 0)
    def _():
        pltpu.make_async_copy(w_own, w, sem).start()
        pltpu.make_async_copy(w_own, w, sem).wait()
        gain_out[...] = jnp.zeros_like(gain_out)

    weights = wt[...]
    picked = pick_a[...] + pick_b[...]
    room = lambda n: jnp.zeros((n, picked.shape[1]), f32)
    picked = jnp.concatenate([room(ROUTER_LANE), picked, room(LANES - ROUTER_LANE - EXPERTS)], axis=0).T
    logit_low = (weights * (picked - jnp.sum(weights * picked, axis=-1, keepdims=True))).astype(bf)
    ll_out[...] = logit_low
    grad = back_a[...].astype(f32) + back_b[...].astype(f32) + mm(logit_low, extra[...])
    passed, gain = norm_back(res[...], extra[1:2, :].astype(f32), grad)
    gain_out[...] += gain
    total = cot[...].astype(f32) + passed
    rg_out[...] = total
    low = total.astype(bf)
    low_t_out[...] = low.T
    dout_out[...] = mm(low, lanes_of(w, 0, w.shape[0])).astype(bf)


def unsettle(back, picks, wt, res, cot, extra, w_own, core, deps, block=256):
    rows, width = res.shape
    cols = w_own.shape[0] * LANES
    wide, thin = rows_of(block, width), rows_of(block, LANES)
    across = pl.BlockSpec((EXPERTS, block), lambda i, s: (0, i))
    return call(
        unsettle_kernel,
        "unsettle",
        (rows // block,),
        [*back, *picks, wt, res, cot, extra, w_own],
        [wide, wide, across, across, thin, wide, wide, whole(extra.shape), any_space()],
        [sds((rows, width), f32), sds((width, rows), bf), sds((rows, cols), bf), sds((rows, LANES), bf), sds((1, width), f32)],
        [wide, pl.BlockSpec((width, block), lambda i, s: (0, i)), rows_of(block, cols), thin, whole((1, width))],
        [pltpu.VMEM(w_own.shape, bf), pltpu.SemaphoreType.DMA],
        2 * rows * width * cols,
        core,
        deps,
    )


def weight_grads_kernel(cfg, sc, *refs):
    sides, extra_sides, core_at, count = cfg
    keep, send = refs[-2:]
    core = sc[core_at]
    last = pl.program_id(0) == pl.num_programs(0) - 1
    it = iter(refs[:-2])

    def left():
        return jnp.concatenate([next(it)[...], next(it)[...]], axis=0)

    tall = left()
    made, at = None, 0
    for kind in range(sides):
        right = next(it)
        size = right.shape[0]
        made_here = mm(tall[:, at : at + size] if size < tall.shape[1] else tall, right[...])
        if size < tall.shape[1]:
            made = made_here if made is None else made + made_here
            at += size
        else:
            made = [made_here] if made is None else made + [made_here]
    if isinstance(made, list):
        made = jnp.concatenate(made, axis=1) if len(made) > 1 else made[0]
    extra = None
    if extra_sides:
        tall = left()
        extra = mm(tall, next(it)[...])
    column = left()
    extra = column if extra is None else extra + column
    wide = 2 * LANES
    made = jnp.concatenate([made, extra, jnp.zeros_like(extra)], axis=1).astype(bf)
    shard = extra.shape[0] // 2
    cut = lambda a: (a[:, :LANES], a[:, LANES:])
    blocks = [made[:, b * wide : (b + 1) * wide] for b in range(count)]

    @pl.when(jnp.logical_not(last))
    def _():
        for b in range(count):
            keep[0, b] = blocks[b][:shard]
            send[0, b] = blocks[b][shard:]

    @pl.when(last)
    def _():
        for b in range(count):
            keep[0, b], send[0, b] = mix_halves(core, cut(blocks[b][:shard]), cut(blocks[b][shard:]))


def weight_grads(name, left, rights, extra, column, scalars, first_rank, core_at, shard, count, deps):
    width, rows = left.shape
    slots = (scalars.shape[0] - first_rank) // 2
    at = lambda k: (lambda i, s: (s[first_rank + k * slots + i], 0))
    two = lambda lanes: [pl.BlockSpec((shard, lanes), at(k)) for k in range(2)]
    ins, specs = [left, left, *rights], two(rows) + [whole(r.shape) for r in rights]
    if extra is not None:
        ins += [extra[0], extra[0], extra[1]]
        specs += two(rows) + [whole(extra[1].shape)]
    ins += [column, column]
    specs += two(LANES)
    out = sds((slots, count, shard, 2 * LANES), bf)
    out_spec = pl.BlockSpec((1, count, shard, 2 * LANES), lambda i, s: (i, 0, 0, 0))
    return call(
        functools.partial(weight_grads_kernel, (len(rights), extra is not None, core_at, count)),
        name,
        (slots,),
        ins,
        specs,
        [out, out],
        [out_spec, out_spec],
        [],
        4 * rows * width * count * LANES,
        scalars,
        deps,
    )


def spread_kernel(sizes, sc, mine, theirs, *outs):
    block = 0
    for out, size in zip(outs, sizes):
        for b in range(max(1, size // (2 * LANES))):
            total = mine[0, block + b].astype(f32) + theirs[0, block + b].astype(f32)
            lanes = min(2 * LANES, out.shape[1])
            out[:, b * lanes : (b + 1) * lanes] = total[:, :lanes]
        block += max(1, size // (2 * LANES))


def spread(mine, theirs, sizes, core):
    shard = mine.shape[2]
    outs = [sds((shard, size), f32) for size in sizes]
    ins = [mine, theirs]
    kernel = functools.partial(spread_kernel, sizes)
    return call(kernel, "spread", (1,), ins, [whole(a.shape) for a in ins], outs, [whole(o.shape) for o in outs], [], 0, core)


def unproject_kernel(sc, tok, cosine, sine, *refs):
    *ins, w_own, low_out, part_out, gain_out, w, sem = refs
    parts = len(ins) // 3
    dqs, sums, mores = ins[:parts], ins[parts : 2 * parts], ins[2 * parts :]
    step = pl.program_id(0)

    @pl.when(step == 0)
    def _():
        pltpu.make_async_copy(w_own, w, sem).start()
        pltpu.make_async_copy(w_own, w, sem).wait()
        gain_out[...] = jnp.zeros_like(gain_out)

    shared = jnp.where(step < pl.num_programs(0) // 2, 1.0, 0.0).astype(f32)
    at = 0
    for is_key in (True, False):
        for own, more in zip(sums, mores):
            kvs = own.shape[0] // 2
            for kv in range(0, kvs, 2):
                heads = [kv + k + (0 if is_key else kvs) for k in range(2)]
                other = [jnp.where(step == 0, more[h, :, :HEAD_DIM], more[h, :, HEAD_DIM:]) for h in heads]
                pair = jnp.concatenate([own[h] + o * shared for h, o in zip(heads, other)], axis=1)
                if is_key:
                    pair = rope(pair, cosine[...], -sine[...])
                low_out[:, at : at + LANES] = pair.astype(bf)
                at += LANES
    low = jnp.concatenate([d[...] for d in dqs] + [low_out[...]], axis=1)
    part = mm_nt(low, lanes_of(w, 0, w.shape[0]))
    part_out[...] = part
    x = tok[...].astype(f32)
    scale = lax.rsqrt(jnp.mean(x * x, axis=-1, keepdims=True) + norm_eps)
    gain_out[...] += jnp.sum(part * x * scale, axis=0, keepdims=True)


def unproject(tokens, cosine, sine, dqs, sums, mores, w_own, core, deps, block=256):
    rows, width = tokens.shape
    cols = sum(s.shape[0] for s in sums) * HEAD_DIM
    own = lambda a: pl.BlockSpec((a.shape[0], block, HEAD_DIM), lambda i, s: (0, i, 0))
    return call(
        unproject_kernel,
        "unproject",
        (rows // block,),
        [tokens, cosine, sine, *dqs, *sums, *mores, w_own],
        [rows_of(block, width), rows_of(block, LANES), rows_of(block, LANES)]
        + [rows_of(block, d.shape[1]) for d in dqs]
        + [own(a) for a in sums]
        + [whole(a.shape) for a in mores]
        + [any_space()],
        [sds((rows, cols), bf), sds((rows, width), f32), sds((1, width), f32)],
        [rows_of(block, cols), rows_of(block, width), whole((1, width))],
        [pltpu.VMEM(w_own.shape, bf), pltpu.SemaphoreType.DMA],
        2 * rows * width * w_own.shape[0] * LANES,
        core,
        deps,
    )


def finish_kernel(sc, tok, part, extra, rg, *refs):
    *fars, w_mine, w_theirs, out, w, sem = refs

    @pl.when(pl.program_id(0) == 0)
    def _():
        load_halves(sc, w_mine, w_theirs, 0, w, sem)
        pltpu.make_async_copy(w, w, sem).wait()

    far = jnp.concatenate([f[...] for f in fars], axis=1)
    grad = part[...] + mm_nt(far, lanes_of(w, 0, w.shape[0]))
    passed, _ = norm_back(tok[...].astype(f32), extra[0:1, :].astype(f32), grad)
    out[...] = rg[...] + passed


def finish(tokens, part, extra, rg, fars, w_mine, w_theirs, core, deps, block=256):
    rows, width = tokens.shape
    wide = rows_of(block, width)
    return call(
        finish_kernel,
        "finish",
        (rows // block,),
        [tokens, part, extra, rg, *fars, w_mine, w_theirs],
        [wide, wide, whole(extra.shape), wide, *[rows_of(block, f.shape[1]) for f in fars], any_space(), any_space()],
        [sds((rows, width), f32)],
        [wide],
        [pltpu.VMEM((2 * w_mine.shape[0], width, LANES), bf), pltpu.SemaphoreType.DMA],
        2 * rows * width * 2 * w_mine.shape[0] * LANES,
        core,
        deps,
    )[0]


def body(
    tokens,
    routes,
    cotangent,
    norm_one,
    w_query,
    key_weight,
    value_weight,
    w_output,
    norm_two,
    w_router,
    w_gate,
    w_up,
    w_down,
):
    window.turn()
    window.turn()
    count = lax.axis_size("dp")
    core = lax.axis_index("ctx")
    place = ring_place(lax.axis_index("dp"), count)
    rows, width = tokens.shape[2:]
    prompt = PROMPT_TOKENS // lax.axis_size("ctx")
    heads = w_query.shape[1] // HEAD_DIM
    kvs = key_weight.shape[1] // HEAD_DIM
    shard, hidden = w_gate.shape[1:]
    core_only = jnp.stack([core, core]).astype(jnp.int32)
    ranks = gather_sources(place, core, count)
    slots = scatter_sources(place, core, count)
    first_rank, core_at = len(ranks) + 1, len(ranks)

    def scalars(*more):
        return jnp.stack([*ranks, core, *slots, *more]).astype(jnp.int32)

    plain = scalars()
    tok = tokens.reshape(rows, width)
    cot = cotangent.reshape(rows, width)
    ids = routes.reshape(rows, TOPK)

    packed = pack(w_query, key_weight, value_weight, w_output, w_router, norm_one, norm_two, core_only)
    firsts = Gather(packed, core, count, 0).finish()

    sizes = [4, 4, 4, 4]
    starts = [sum(sizes[:k]) for k in range(len(sizes))]
    chunks = []

    owns = [jnp.stack([w[at : at + size] for w in (w_gate, w_up, w_down)], axis=0) for at, size in zip(starts, sizes)]

    def open_chunk(*held):
        chunks.append(Gather(after(owns[len(chunks)], *held), core, count, 3))

    offsets = jnp.arange(rows, dtype=jnp.int32)
    positions = jnp.where(offsets < prompt, core * prompt + offsets, PROMPT_TOKENS + offsets - prompt)
    half_dim = HEAD_DIM // 2
    inverse = rope_base ** (-2.0 * jnp.arange(half_dim).astype(f32) / HEAD_DIM)
    angles = positions.astype(f32)[:, None] * inverse
    cosine = jnp.tile(jnp.cos(angles), (1, LANES // half_dim))
    sine = jnp.sin(angles)
    sine = jnp.tile(jnp.concatenate([-sine, sine], axis=1), (1, LANES // HEAD_DIM))
    cott = cot.T

    open_chunk(firsts.mine[-1])
    c0 = chunks[0]
    window.turn()
    window.turn()
    c0.step()
    w_first, w_out, w_out_half, extra, q, kv, kv_prompt, n1t = project(
        tok, cosine, sine, plain, firsts.bufs, heads, kvs, prompt, [cott, *owns, *window.turn()]
    )
    other = swap(kv_prompt, "ctx")
    out_far_mine = swap(after(w_out_half, kv_prompt), "tp")
    c0.step(kv_prompt)
    mixed_b, lse_b = attend(q, kv, other, core_only, 1, window.turn())
    far_b = swap(mixed_b, "tp")
    c0.step(lse_b)
    open_chunk(lse_b)
    c1 = chunks[1]
    c1.step()
    out_far_theirs = swap(after(out_far_mine, lse_b), "ctx")
    mixed_a, lse_a = attend(q, kv, other, core_only, 0, window.turn())
    far_a = swap(mixed_a, "tp")
    c0.step(lse_a)
    c1.step(lse_a)
    mixed, lse = (mixed_a, mixed_b), (lse_a, lse_b)
    first_part = w_first.shape[0] // 2
    res, n2, n2t, wt = settle(
        tok, ids, mixed, (far_a, far_b), extra, w_out, out_far_mine, out_far_theirs, core_only, window.turn()
    )
    first_far_mine = swap(take(after(w_first, wt), core * first_part, first_part), "tp")

    scatters = [Scatter(core, count, plain, core_at) for _ in range(2)]
    total_pairs = EXPERTS // 2
    state = dict(sums=None, pick=None)

    def work(pair):
        at = 2 * pair
        k = max(k for k in range(len(starts)) if starts[k] <= at)
        sc = scalars(jnp.int32(at), jnp.int32(at + 1))
        carried = None if state["sums"] is None else (*state["sums"], state["pick"])
        made = experts(n2, n2t, cot, cott, wt, sc, chunks[k].bufs, at - starts[k], carried, pair == total_pairs - 1, window.turn())
        state["sums"], state["pick"] = made[:2], made[4]
        state["last"] = made[-1]
        return made[2], made[3], made[4]

    s0, s1 = scatters
    c0.share(wt)
    c1.step(wt)
    open_chunk(wt)
    c2 = chunks[2]
    c2.step()
    keep, send, token = work(0)

    s0.add(keep, send)
    c1.step(token)
    c2.step(token)
    keep, send, token = work(1)

    s0.add(keep, send)
    c1.share(token)
    c2.step(token)
    open_chunk(token)
    c3 = chunks[3]
    c3.step()
    first_far_theirs = swap(after(first_far_mine, token), "ctx")
    keep, send, token = work(2)

    s0.add(keep, send)
    c2.step(token)
    c3.step(token)
    keep, send, token = work(3)

    s0.add(keep, send)
    c2.share(token)
    c3.step(token)
    s0.step([token])
    keep, send, token = work(4)

    s1.add(keep, send)
    c3.step(token)
    s0.step([token])
    keep, send, token = work(5)

    s1.add(keep, send)
    c3.share(token)
    s0.step([token])
    keep, send, token = work(6)

    s1.add(keep, send)
    s0.step([token])
    keep, send, token = work(7)
    moe_low, back_low = state["sums"]
    pick_t = state["last"]

    back_far = swap(back_low, "tp")
    got = s1.add(keep, send)
    pick_far = swap(after(pick_t, got), "tp")
    a = s1.step([token])
    s0_mine, s0_theirs = s0.finish([a])
    s1.step([s0_mine])
    emitted = emit((s0_mine, s0_theirs), 0, EXPERTS, None, core_only, [s0_mine])
    rg, low_t, dout, ll, gain_two = unsettle(
        (back_low, back_far), (pick_t, pick_far), wt, res, cot, extra, w_out, core_only, [emitted[0], *window.turn()]
    )
    moe_far = swap(after(moe_low, ll), "tp")

    lane = jnp.arange(LANES)
    column = lambda gain, at: jnp.where(lane == at, gain[0][:, None], 0.0)
    parts = 2
    s1.step([ll])
    window.now = [x for x in window.now if x is not moe_far]
    dq_a, dkv_a, dother_a = attend_back(q, kv, other, dout, mixed, lse, cosine, sine, core_only, 0, parts, window.turn())
    more_a = swap(dother_a, "ctx")
    s1.step([dother_a])
    out_keep, out_send = weight_grads(
        "output_grads", low_t, list(mixed), (n2t, ll), column(gain_two, 1), plain, first_rank, core_at, shard, heads // 4 + 1, [dother_a]
    )
    second = Scatter(core, count, plain, core_at)
    second.add(out_keep, out_send)
    dq_b, dkv_b, dother_b = attend_back(q, kv, other, dout, mixed, lse, cosine, sine, core_only, 1, parts, window.turn())
    more_b = swap(dother_b, "ctx")
    far_qa = swap(after(dq_a, moe_far, dother_b), "tp")
    second.step([dother_b])
    s1_mine, s1_theirs = s1.finish([dother_b])
    dqs, dkvs, mores = [dq_a, dq_b], [dkv_a, dkv_b], [more_a, more_b]
    low_kv, part, gain_one = unproject(tok, cosine, sine, dqs, dkvs, mores, w_first, core_only, [moe_far, *window.turn()])
    far_qb = swap(after(dq_b, gain_one), "tp")
    far_qs = [far_qa, far_qb]
    second.step([gain_one])
    first_keep, first_send = weight_grads(
        "project_grads", n1t, [*dqs, low_kv], None, column(gain_one, 0), plain, first_rank, core_at, shard, w_first.shape[0] // 2 + 1, window.turn()
    )
    first = Scatter(core, count, plain, core_at)
    far_kv = swap(after(low_kv, first_keep), "tp")
    first.add(first_keep, first_send)
    a = first.step()
    second.step([first_keep])
    grad_gate, grad_up, grad_down = emit((s1_mine, s1_theirs), EXPERTS // 2, EXPERTS, emitted, core_only, [first_keep, *window.turn()])
    first.step([grad_gate])
    second.step([grad_gate])
    result = (res + (moe_low.astype(f32) + after(moe_far, grad_gate).astype(f32))).astype(bf).reshape(tokens.shape)
    token_grad = finish(
        tok, part, extra, rg, [*far_qs, far_kv], first_far_mine, first_far_theirs, core_only, [grad_gate]
    ).reshape(tokens.shape)
    a = first.step()
    second_mine, second_theirs = second.finish()
    first.step()
    grad_output, extra_two = spread(second_mine, second_theirs, (heads * HEAD_DIM, LANES), core_only)
    kv_width = kvs * HEAD_DIM
    grad_query, grad_key, grad_value, extra_one = spread(*first.finish(), (heads * HEAD_DIM, kv_width, kv_width, LANES), core_only)
    gain_part = extra_one[:, 0]
    grad_norm_one = gain_part + swap(gain_part, "tp")
    grad_norm_two = extra_two[:, 1]
    grad_router = extra_two[:, ROUTER_LANE : ROUTER_LANE + EXPERTS]
    return (
        result,
        token_grad,
        grad_norm_one,
        grad_query,
        grad_key,
        grad_value,
        grad_output,
        grad_norm_two,
        grad_router,
        grad_gate,
        grad_up,
        grad_down,
    )


def solution(mesh):
    slab = P("dp", "ctx", None, None)
    split, rows_only, expert = P("dp", "tp"), P("dp"), P(None, "dp", "tp")
    return jax.shard_map(
        body,
        mesh=mesh,
        in_specs=(slab, slab, slab, rows_only, split, split, split, split, rows_only, P("dp", None), expert, expert, expert),
        out_specs=(slab, slab, rows_only, split, split, split, split, rows_only, P("dp", None), expert, expert, expert),
        check_vma=False,
    )
```

```python
import functools

import jax
import jax.numpy as jnp
from jax import lax
from jax.experimental import pallas as pl
from jax.experimental.pallas import tpu as pltpu
from jax.sharding import PartitionSpec as P

HEAD_DIM = 64
EXPERTS = 16
TOPK = 8
PROMPT_TOKENS = 1024
LANES = 128
ROUTER_LANE = 16

norm_eps = 1e-06
rope_base = 10000.0
masked_score = -1e30
bf = jnp.bfloat16
f32 = jnp.float32
contract_cols = (((1,), (1,)), ((), ()))
COSTS = dict(experts_all=24, experts_front_end=18, experts_rest_end=13, experts_front=18, experts_rest=13, attend=19, project=18, settle=16, unsettle=17, attend_back=25)
COSTS.update(early_grads=12, key_value_grads=7, late_grads=10, finish=18, emit=5, hop_sum=5, combine=5)
vmem_bytes = 63 * 1024 * 1024


def mm(a, b):
    return jnp.dot(a, b, preferred_element_type=f32)


def mm_nt(a, b):
    return lax.dot_general(a, b, contract_cols, preferred_element_type=f32)


def whole(shape):
    return pl.BlockSpec(shape, lambda *_: (0,) * len(shape), pipeline_mode=pl.Buffered(1))


def rows_of(block, width):
    return pl.BlockSpec((block, width), lambda i, *_: (i, 0))


def any_space():
    return pl.BlockSpec(memory_space=pltpu.HBM)


def call(kernel, name, grid, ins, in_specs, outs, out_specs, scratch, flops, scalars, deps=(), limit=vmem_bytes, aliases=None):
    moved = sum(a.size * a.dtype.itemsize for a in (*ins, *outs))
    return pl.pallas_call(
        lambda sc, *refs: kernel(sc, *refs[len(deps) :]),
        out_shape=tuple(outs),
        grid_spec=pltpu.PrefetchScalarGridSpec(
            num_scalar_prefetch=1,
            grid=grid,
            in_specs=[pl.BlockSpec(memory_space=pltpu.HBM) for _ in deps] + list(in_specs),
            out_specs=tuple(out_specs),
            scratch_shapes=scratch,
        ),
        compiler_params=pltpu.CompilerParams(vmem_limit_bytes=limit),
        cost_estimate=pl.CostEstimate(flops=COSTS.get(name, 3) * 1_153_000_000, bytes_accessed=1, transcendentals=0),
        name=name,
        input_output_aliases=aliases or {},
    )(scalars, *deps, *ins)


def after(values, *deps):
    return lax.optimization_barrier((values, *deps))[0]


def sds(shape, dtype):
    return jax.ShapeDtypeStruct(tuple(shape), dtype)


def ring_rank(place, count):
    place = lax.rem(place + 2 * count, count)
    return jnp.where(place < count // 2, 2 * place, 2 * count - 1 - 2 * place)


def ring_place(rank, count):
    return jnp.where(rank % 2 == 0, rank // 2, (2 * count - 1 - rank) // 2)


def ring_hop(values, count):
    order = list(range(0, count, 2)) + list(range(count - 1, 0, -2))
    pairs = []
    for k in range(count):
        here, there = order[k], order[(k + 1) % count]
        pairs += [(2 * here, 2 * there), (2 * there + 1, 2 * here + 1)]
    return sent(lax.ppermute(values, ("dp", "ctx"), pairs))


def swap(values, axis):
    swapped = lax.ppermute(values, axis, [(0, 1), (1, 0)])
    return sent(swapped) if axis == "ctx" or not window.gated else swapped


class Window:
    def __init__(self):
        self.now, self.before, self.soon = [], [], []
        self.gated = False

    def turn(self):
        due, self.before, self.now, self.soon = self.before + self.soon, self.now, [], []
        return due

    def step(self):
        due, self.before, self.now, self.soon = self.soon, self.before + self.now, [], []
        return due

    def gate(self, token, *more):
        token = after(token, *self.before, *more)
        self.before = []
        return token


window = Window()


def sent(values):
    window.now.append(values)
    return values


def take(values, start, size, axis=0):
    return lax.dynamic_slice_in_dim(values, start, size, axis)


def place_half(values, core, axis):
    zeros = jnp.zeros_like(values)
    return jnp.where(core == 0, jnp.concatenate([values, zeros], axis), jnp.concatenate([zeros, values], axis))


PLANNED = 4


class Gather:
    def __init__(self, own, core, count, axis):
        self.own, self.core, self.count, self.axis = own, core, count, axis
        self.mine, self.mate, self.hops = [], [], 0

    def share(self, *held):
        if len(self.mate) < len(self.mine):
            self.mate.append(swap(after(self.mine[-1], *held), "ctx"))

    def step(self, *held):
        for _ in range(1 if self.hops else self.count // 2 - PLANNED + 1):
            got = self.hop(*held)
        return got

    def hop(self, *held):
        self.share(*held)
        self.hops += 1
        last = after(self.mine[-1] if self.mine else self.own, *held)
        if self.hops == self.count // 2:
            size = last.shape[self.axis] // 2
            last = take(last, self.core * size, size, self.axis)
        self.mine.append(ring_hop(last, self.count))
        return self.mine[-1]

    def finish(self):
        while self.hops < self.count // 2:
            self.step()
        self.share()
        return self

    @property
    def bufs(self):
        return [self.own, *self.mine, *self.mate]


def gather_sources(place, core, count):
    sign = 1 - 2 * core
    away = list(range(1, count // 2 + 1))
    return [ring_rank(place, count)] + [ring_rank(place - sign * a, count) for a in away] + [ring_rank(place + sign * a, count) for a in away]


def scatter_sources(place, core, count):
    sign = 1 - 2 * core
    away = list(range(1, count // 2))
    keep = [ring_rank(place + sign * a, count) for a in away] + [ring_rank(place + count // 2, count)]
    send = [ring_rank(place - sign * a, count) for a in away] + [ring_rank(place, count)]
    return keep + send


class Scatter:
    def __init__(self, core, count, scalars, core_at):
        self.core, self.count, self.scalars, self.core_at = core, count, scalars, core_at
        self.keeps, self.gots, self.hops, self.got = [], [], 0, None

    def add(self, keep, send, *held):
        self.keeps.append(keep)
        self.gots.append(swap(after(send, *held), "ctx"))
        return self.gots[-1]

    def step(self, deps=()):
        for _ in range(1 if self.hops else self.count // 2 - PLANNED + 1):
            got = self.hop(deps)
        return got

    def hop(self, deps):
        self.hops += 1
        stage = {1: None, 2: "second"}.get(self.hops, "middle")
        slot = self.count // 2 - self.hops if self.hops > 1 else self.count // 2 - 1
        value = hop_sum(self.keeps, self.gots, self.got, slot, stage, self.scalars, self.core_at, deps)
        self.value = value
        window.soon.append(value)
        self.got = ring_hop(value, self.count)
        return self.got

    def finish(self, deps=()):
        while self.hops < self.count // 2:
            self.step()
        mine = hop_sum(self.keeps, self.gots, self.got, self.count // 2 - 1, "end", self.scalars, self.core_at, deps)
        return mine, swap(mine, "ctx")


def load_shards(sc, bufs, dst, shard, sem):
    total = len(bufs)
    hops = total // 2
    half = dst.shape[0] // 2
    for k, buf in enumerate(bufs):
        rows = pl.ds(pl.multiple_of(sc[k] * shard, shard), shard)
        if k in (hops, 2 * hops):
            side = sc[total] if k == hops else 1 - sc[total]
            target = dst.at[pl.ds(side * half, half), rows, :]
        else:
            target = dst.at[:, rows, :]
        pltpu.make_async_copy(buf, target, sem).start()


def lanes_of(ref, first, count):
    return jnp.concatenate([ref[first + b] for b in range(count)], axis=1)


def rope(x, cosine, sine):
    lane = lax.broadcasted_iota(jnp.int32, x.shape, x.ndim - 1)
    ahead = pltpu.roll(x, x.shape[-1] - HEAD_DIM // 2, x.ndim - 1)
    behind = pltpu.roll(x, HEAD_DIM // 2, x.ndim - 1)
    return x * cosine + jnp.where(lax.rem(lane, HEAD_DIM) < HEAD_DIM // 2, ahead, behind) * sine


def lane_column(row, shape, lane_at):
    lane = lax.broadcasted_iota(jnp.int32, shape, 1)
    return jnp.where(lane == lane_at, jnp.broadcast_to(row, (shape[1], shape[0])).T, 0.0)


def pack_kernel(sc, query, key, value, output, router, gain_one, gain_two, out):
    at = 0
    for ref in (query, key, value):
        for b in range(ref.shape[1] // LANES):
            out[at] = ref[:, b * LANES : (b + 1) * LANES]
            at += 1
    shape = out.shape[1:]
    extra = lane_column(gain_one[...].astype(f32), shape, 0) + lane_column(gain_two[...].astype(f32), shape, 1)
    out[at] = extra.astype(bf)
    out[at, :, ROUTER_LANE : ROUTER_LANE + EXPERTS] = router[...]
    for b in range(output.shape[1] // LANES):
        out[at + 1 + b] = output[:, b * LANES : (b + 1) * LANES]
    for b in range(at + 1 + output.shape[1] // LANES, out.shape[0]):
        out[b] = jnp.zeros(shape, bf)


def pack(query, key, value, output, router, gain_one, gain_two, core):
    shard = query.shape[0]
    ins = [query, key, value, output, router, gain_one.reshape(1, shard), gain_two.reshape(1, shard)]
    blocks = (query.shape[1] + key.shape[1] + value.shape[1] + output.shape[1]) // LANES + 1
    blocks += blocks % 2
    out = sds((blocks, shard, LANES), bf)
    return call(pack_kernel, "pack", (1,), ins, [whole(a.shape) for a in ins], [out], [whole(out.shape)], [], 0, core)[0]


def qkv_kernel(shard, kinds, sc, tok, cosine, sine, *refs):
    heads, kvs, total = kinds
    bufs, (w_first, w_out, w_half, extra_out, q_out, kv_out, packed_out, nt_out, w, et, sem, out_sem) = refs[:total], refs[total:]
    step = pl.program_id(0)
    count, half = w_first.shape[0], w_half.shape[0]
    copies = [
        (w.at[pl.ds(0, count)], w_first),
        (w.at[pl.ds(count, 2 * half)], w_out),
        (w.at[pl.ds(count + sc[total] * half, half)], w_half),
    ]

    @pl.when(step == 0)
    def _():
        load_shards(sc, bufs, w, shard, sem)
        pltpu.make_async_copy(w, w, sem).wait()
        for k, (src, dst) in enumerate(copies):
            pltpu.make_async_copy(src, dst, out_sem.at[k]).start()
        et[...] = w[count - 1].T

    extra_out[...] = et[...]
    x = tok[...].astype(f32)
    scale = lax.rsqrt(jnp.mean(x * x, axis=-1, keepdims=True) + norm_eps)
    normed = (x * scale * et[0:1, :].astype(f32)).astype(bf)
    nt_out[...] = normed.T
    cs, sn = cosine[...], sine[...]
    for pair in range((heads + 2 * kvs) // 4):
        made = mm(normed, lanes_of(w, 2 * pair, 2))
        for side in range(2):
            first = 4 * pair + 2 * side
            part = made[:, side * LANES : (side + 1) * LANES]
            if first < heads + kvs:
                part = rope(part, cs, sn)
            out, at = kv_out, first - heads
            if first < heads:
                part, out, at = part * (1.0 / HEAD_DIM), q_out, first
            low = part.astype(bf)
            for k in range(2):
                one = low[:, k * HEAD_DIM : (k + 1) * HEAD_DIM]
                out[at + k] = one
                if first >= heads:
                    for quarter in range(2):

                        @pl.when(step == quarter)
                        def _():
                            packed_out[at + k, :, quarter * HEAD_DIM : (quarter + 1) * HEAD_DIM] = one

    @pl.when(step == pl.num_programs(0) - 1)
    def _():
        for k, (src, dst) in enumerate(copies):
            pltpu.make_async_copy(src, dst, out_sem.at[k]).wait()


def project(tokens, cosine, sine, scalars, bufs, heads, kvs, prompt, deps, block=256):
    rows, width = tokens.shape
    blocks, shard = bufs[0].shape[:2]
    count = (heads + 2 * kvs) // 2 + 1
    head_spec = lambda n: pl.BlockSpec((n, block, HEAD_DIM), lambda i, s: (0, i, 0))
    outs = [
        sds((count, width, LANES), bf),
        sds((heads // 2, width, LANES), bf),
        sds((heads // 4, width, LANES), bf),
        sds((LANES, width), bf),
        sds((heads, rows, HEAD_DIM), bf),
        sds((2 * kvs, rows, HEAD_DIM), bf),
        sds((2 * kvs, prompt // 2, LANES), bf),
        sds((width, rows), bf),
    ]
    return call(
        functools.partial(qkv_kernel, shard, (heads, kvs, len(bufs))),
        "project",
        (rows // block,),
        [tokens, cosine, sine, *bufs],
        [rows_of(block, width), rows_of(block, LANES), rows_of(block, LANES)] + [any_space()] * len(bufs),
        outs,
        [
            any_space(),
            any_space(),
            any_space(),
            whole((LANES, width)),
            head_spec(heads),
            head_spec(2 * kvs),
            whole((2 * kvs, prompt // 2, LANES)),
            pl.BlockSpec((width, block), lambda i, s: (0, i)),
        ],
        [
            pltpu.VMEM((blocks, width, LANES), bf),
            pltpu.VMEM((LANES, width), bf),
            pltpu.SemaphoreType.DMA,
            pltpu.SemaphoreType.DMA((3,)),
        ],
        2 * rows * width * count * LANES,
        scalars,
        deps,
    )


def causal(scores):
    key = lax.broadcasted_iota(jnp.int32, scores.shape, 0)
    query = lax.broadcasted_iota(jnp.int32, scores.shape, 1)
    return jnp.where(key <= query, scores, masked_score)


def block_scores(query, keys, other_keys, at, block, prompt, bias):
    parts = []
    if at:
        parts.append(mm_nt(keys[0:at], query))
    parts.append(causal(mm_nt(keys[at : at + block], query)))
    other = mm_nt(other_keys, query)
    if at < prompt:
        other = other + bias
    parts.append(other)
    return parts


def unpack(ref):
    return jnp.concatenate([ref[0, :, :HEAD_DIM], ref[0, :, HEAD_DIM:]], axis=0)


def attend_kernel(cfg, sc, q, k0, k1, o0, o1, v0, v1, w0, w1, mixed, lse):
    starts, block, prompt = cfg
    bias = jnp.where(sc[0] == 0, masked_score, 0.0).astype(f32)
    for side, (keys, other, values, other_values) in enumerate(((k0, o0, v0, w0), (k1, o1, v1, w1))):
        values_t = values[0].T
        other_t = unpack(other_values).T
        other_keys = unpack(other)
        for a, at in enumerate(starts):
            rows = slice(a * block, a * block + block)
            scores = block_scores(q[side, rows, :], keys[0], other_keys, at, block, prompt, bias)
            peak = functools.reduce(jnp.maximum, [jnp.max(s, axis=0, keepdims=True) for s in scores])
            raw = [jnp.exp(s - peak) for s in scores]
            total = sum(jnp.sum(r, axis=0, keepdims=True) for r in raw)
            low = [r.astype(bf) for r in raw]
            out = mm(other_t, low[-1]) + mm(values_t[:, at : at + block], low[-2])
            if at:
                out = out + mm(values_t[:, 0:at], low[0])
            out = out * (1.0 / total)
            mixed[rows, side * HEAD_DIM : side * HEAD_DIM + HEAD_DIM] = out.T.astype(bf)
            lse[0, side : side + 1, rows] = peak + jnp.log(total)


def kv_specs(kvs, rows, prompt, rep, first_pair):
    index = lambda side, base: (lambda p, s: (base + (2 * (p + first_pair) + side) // rep, 0, 0))
    specs = []
    for base in (0, kvs):
        specs += [pl.BlockSpec((1, rows, HEAD_DIM), index(side, base)) for side in range(2)]
        specs += [pl.BlockSpec((1, prompt // 2, LANES), index(side, base)) for side in range(2)]
    return specs


def attend(q, kv, other, core, part, deps, block=256):
    heads, rows, _ = q.shape
    kvs, prompt = other.shape[0] // 2, 2 * other.shape[1]
    count = prompt if part == 0 else rows - prompt
    first = 0 if part == 0 else prompt
    starts = tuple(range(first, first + count, block))
    return call(
        functools.partial(attend_kernel, (starts, block, prompt)),
        "attend",
        (heads // 2,),
        [q, kv, kv, other, other, kv, kv, other, other],
        [pl.BlockSpec((2, count, HEAD_DIM), lambda p, s: (p, part, 0)), *kv_specs(kvs, rows, prompt, heads // kvs, 0)],
        [sds((count, heads * HEAD_DIM), bf), sds((heads // 2, 2, count), f32)],
        [
            pl.BlockSpec((count, LANES), lambda p, s: (0, p)),
            pl.BlockSpec((1, 2, count), lambda p, s: (p, 0, 0)),
        ],
        [],
        16 * heads * count * 1024 * HEAD_DIM,
        core,
        deps,
    )


def attend_back_kernel(cfg, sc, q, k0, k1, o0, o1, v0, v1, w0, w1, dout, mixed_a, mixed_b, lse_a, lse_b, cosine, sine, dq, dkv, dother_out, dother):
    rows_total, block, prompt, rep = cfg
    pair = pl.program_id(0)
    bias = jnp.where(sc[0] == 0, masked_score, 0.0).astype(f32)
    kvs = dkv.shape[0] // 2

    @pl.when(pair == 0)
    def _():
        dkv[...] = jnp.zeros_like(dkv)
        dother[...] = jnp.zeros_like(dother)

    heads = ((k0, unpack(o0), v0, unpack(w0)), (k1, unpack(o1), v1, unpack(w1)))
    keys_t = [(keys[0].T, other.T) for keys, other, _, _ in heads]
    for at in range(0, rows_total, block):
        rows = slice(at, at + block)
        mixed, lse, local = (mixed_a, lse_a, at) if at < prompt else (mixed_b, lse_b, at - prompt)
        inner = slice(local, local + block)
        dot = (dout[rows, :].astype(f32) * mixed[inner, :].astype(f32)).T
        grads = []
        for side, (keys, other, values, other_values) in enumerate(heads):
            head = (2 * pair + side) // rep
            query = q[side, rows, :]
            grad = dout[rows, side * HEAD_DIM : side * HEAD_DIM + HEAD_DIM]
            weighted = jnp.sum(dot[side * HEAD_DIM : side * HEAD_DIM + HEAD_DIM], axis=0, keepdims=True)
            norm = lse[0, side : side + 1, inner]
            scores = block_scores(query, keys[0], other, at, block, prompt, bias)
            spans = ([(False, 0, at)] if at else []) + [(False, at, block), (True, 0, prompt)]
            back = None
            for score, (is_other, first, size) in zip(scores, spans):
                probs = jnp.exp(score - norm)
                value = other_values if is_other else values[0, first : first + size]
                score_low = (probs * (mm_nt(value, grad) - weighted)).astype(bf)
                sums = dother if is_other else dkv
                span = pl.ds(first, size)
                sums[kvs + head, span, :] += mm(probs.astype(bf), grad)
                sums[head, span, :] += mm(score_low, query)
                key_t = keys_t[side][1] if is_other else keys_t[side][0][:, first : first + size]
                term = mm(key_t, score_low)
                back = term if back is None else back + term
            grads.append(back)
        both = jnp.concatenate(grads, axis=0).T * (1.0 / HEAD_DIM)
        dq[rows, :] = rope(both, cosine[rows, :], -sine[rows, :]).astype(bf)

    @pl.when(pair == pl.num_programs(0) - 1)
    def _():
        for h in range(dother.shape[0]):
            for quarter in range(2):
                part = dother[h, quarter * (prompt // 2) : (quarter + 1) * (prompt // 2), :]
                dother_out[h, :, quarter * HEAD_DIM : (quarter + 1) * HEAD_DIM] = part


def attend_back(q, kv, other, dout, mixed, lse, cosine, sine, core, part, parts, deps, block=256):
    heads, rows, _ = q.shape
    kvs, prompt = other.shape[0] // 2, 2 * other.shape[1]
    pairs = heads // 2 // parts
    first = part * pairs
    mine = 2 * kvs // parts
    pair = pl.BlockSpec((rows, LANES), lambda p, s: (0, p + first))
    mixed_spec = lambda a: pl.BlockSpec((a.shape[0], LANES), lambda p, s: (0, p + first))
    lse_spec = lambda a: pl.BlockSpec((1, 2, a.shape[2]), lambda p, s: (p + first, 0, 0))
    return call(
        functools.partial(attend_back_kernel, (rows, block, prompt, heads // kvs)),
        "attend_back",
        (pairs,),
        [q, kv, kv, other, other, kv, kv, other, other, dout, *mixed, *lse, cosine, sine],
        [
            pl.BlockSpec((2, rows, HEAD_DIM), lambda p, s: (p + first, 0, 0)),
            *kv_specs(kvs, rows, prompt, heads // kvs, first),
            pair,
            *[mixed_spec(a) for a in mixed],
            *[lse_spec(a) for a in lse],
            whole(cosine.shape),
            whole(sine.shape),
        ],
        [
            sds((rows, pairs * LANES), bf),
            sds((mine, rows, HEAD_DIM), f32),
            sds((mine, prompt // 2, LANES), f32),
        ],
        [
            pl.BlockSpec((rows, LANES), lambda p, s: (0, p)),
            whole((mine, rows, HEAD_DIM)),
            whole((mine, prompt // 2, LANES)),
        ],
        [pltpu.VMEM((mine, prompt, HEAD_DIM), f32)],
        40 * heads // parts * rows * 1024 * HEAD_DIM,
        core,
        deps,
    )


def load_halves(sc, mine, theirs, first_block, w, sem):
    half = mine.shape[0]
    pltpu.make_async_copy(mine, w.at[pl.ds(first_block + sc[0] * half, half)], sem).start()
    pltpu.make_async_copy(theirs, w.at[pl.ds(first_block + (1 - sc[0]) * half, half)], sem).start()


def settle_kernel(sc, tok, ids, own_a, own_b, far_a, far_b, extra, w_own, w_mine, w_theirs, res_out, n_out, nt_out, wt_out, w, sem):
    step = pl.program_id(0)
    blocks = w_own.shape[0]

    @pl.when(step == 0)
    def _():
        pltpu.make_async_copy(w_own, w.at[pl.ds(0, blocks)], sem).start()
        load_halves(sc, w_mine, w_theirs, blocks, w, sem)
        pltpu.make_async_copy(w, w, sem).wait()

    early = step < pl.num_programs(0) // 2
    own = jnp.where(early, own_a[...], own_b[...])
    far = jnp.where(early, far_a[...], far_b[...])
    branch = mm_nt(own, lanes_of(w, 0, blocks)) + mm_nt(far, lanes_of(w, blocks, blocks))
    residual = tok[...].astype(f32) + branch
    res_out[...] = residual
    scale = lax.rsqrt(jnp.mean(residual * residual, axis=-1, keepdims=True) + norm_eps)
    normed = (residual * scale * extra[1:2, :].astype(f32)).astype(bf)
    n_out[...] = normed
    nt_out[...] = normed.T
    logits = mm_nt(normed, extra[...])
    lane = lax.broadcasted_iota(jnp.int32, logits.shape, 1)
    routed = lane < 0
    for k in range(TOPK):
        routed = jnp.logical_or(routed, lane == ids[:, k : k + 1] + ROUTER_LANE)
    logits = jnp.where(routed, logits, masked_score)
    raw = jnp.where(routed, jnp.exp(logits - jnp.max(logits, axis=-1, keepdims=True)), 0.0)
    wt_out[...] = raw / jnp.sum(raw, axis=-1, keepdims=True)


def settle(tokens, ids, own, far, extra, w_own, w_mine, w_theirs, core, deps, block=256):
    rows, width = tokens.shape
    halves = rows // block // 2
    cols = own[0].shape[1]
    low = pl.BlockSpec((block, cols), lambda i, s: (jnp.minimum(i, halves - 1), 0))
    high = pl.BlockSpec((block, cols), lambda i, s: (jnp.maximum(i - halves, 0), 0))
    return call(
        settle_kernel,
        "settle",
        (rows // block,),
        [tokens, ids, *own, *far, extra, w_own, w_mine, w_theirs],
        [rows_of(block, width), rows_of(block, TOPK), low, high, low, high, whole(extra.shape)] + [any_space()] * 3,
        [sds((rows, width), f32), sds((rows, width), bf), sds((width, rows), bf)] + [sds((rows, LANES), f32)],
        [rows_of(block, width), rows_of(block, width), pl.BlockSpec((width, block), lambda i, s: (0, i))]
        + [rows_of(block, LANES)],
        [pltpu.VMEM((2 * w_own.shape[0], width, LANES), bf), pltpu.SemaphoreType.DMA],
        4 * rows * width * cols,
        core,
        deps,
    )


def mix_halves(core, kept, sent):
    first = jnp.concatenate([kept[0], sent[0]], axis=-1)
    second = jnp.concatenate([kept[1], sent[1]], axis=-1)
    return jnp.where(core == 0, first, second), jnp.where(core == 0, second, first)


PARTS = ((3, 1), (2, 2))


def fetch_weights(sc, bufs, w, kinds, local, shard, hidden, sem):
    hops = len(bufs) // 2
    core = sc[len(bufs)]
    for side in range(2):
        for k, buf in enumerate(bufs):
            rows = pl.ds(pl.multiple_of(sc[k] * shard, shard), shard)
            lanes = pl.ds(side * hidden, hidden)
            if k in (hops, 2 * hops):
                at = core if k == hops else 1 - core
                lanes = pl.ds(pl.multiple_of(side * hidden + at * (hidden // 2), LANES), hidden // 2)
            pltpu.make_async_copy(buf.at[kinds, local + side], w.at[kinds, rows, lanes], sem).start()


def activate(ids, hidden, rows, x, grad_rows, w, wt, pick_in, pick, scaled, acts):
    lane = lax.broadcasted_iota(jnp.int32, (x.shape[0], LANES), 1)
    gate = mm(x, w[0])
    up = mm(x, w[1])
    grad = mm(grad_rows, w[2])
    table = wt[rows, :]
    sig = 1.0 / (1.0 + jnp.exp(-gate))
    silu = gate * sig
    act = silu * up
    dots = act * grad
    picked = jnp.zeros(table.shape, f32) if pick_in is None else pick_in[rows, :]
    for side, expert in enumerate(ids):
        cols = slice(side * hidden, side * hidden + hidden)
        weight = jnp.sum(jnp.where(lane == expert, table, 0.0), axis=1, keepdims=True)
        picked = picked + jnp.where(lane == expert, jnp.sum(dots[:, cols], axis=1, keepdims=True), 0.0)
        scaled[rows, cols] = (act[:, cols] * weight).astype(bf)
        g = grad[:, cols] * weight
        s = sig[:, cols]
        acts[rows, cols] = (g * up[:, cols] * s * (1.0 + gate[:, cols] * (1.0 - s))).astype(bf)
        acts[rows, slice((2 + side) * hidden, (3 + side) * hidden)] = (g * silu[:, cols]).astype(bf)
    pick[rows, :] = picked
    return picked


def pair_grads(sc, total, shard, hidden, xt, ct, scaled, acts, keep_s, send_s, keep, send, g_sem):
    core, ranks, slots = sc[total], total + 1, total // 2
    for slot in range(slots):
        at = [pl.ds(pl.multiple_of(sc[ranks + slots * k + slot] * shard, shard), shard) for k in range(2)]
        left = lambda ref: jnp.concatenate([ref[at[0], :], ref[at[1], :]], axis=0)
        gate_up = mm(left(xt), acts[...]).astype(bf)
        down = mm(left(ct), scaled[...]).astype(bf)
        kinds = (gate_up[:, : 2 * hidden], gate_up[:, 2 * hidden :], down)
        for kind, made in enumerate(kinds):
            for side in range(2):
                part = made[:, side * hidden : side * hidden + hidden]
                kept, sent_part = part[:shard], part[shard:]
                if slot == slots - 1:
                    cut = lambda a: (a[:, : hidden // 2], a[:, hidden // 2 :])
                    kept, sent_part = mix_halves(core, cut(kept), cut(sent_part))
                keep_s[slot, side * 3 + kind] = kept
                send_s[slot, side * 3 + kind] = sent_part
        pltpu.make_async_copy(keep_s.at[slot], keep.at[slot], g_sem.at[0]).start()
        pltpu.make_async_copy(send_s.at[slot], send.at[slot], g_sem.at[1]).start()


def experts_kernel(cfg, sc, *refs):
    shard, hidden, local, first, mode, total = cfg
    block = 256
    it = iter(refs)
    front, rest, ends = mode.startswith("front"), mode.startswith("rest"), mode.endswith("_end")
    n2, cot, wt = (None, None, None) if rest else (next(it), next(it), next(it))
    n2t, cott = (None, None) if front else (next(it), next(it))
    bufs = [next(it) for _ in range(total)]
    moe_in = None if first or front else next(it)
    back_in, pick_in = (None, None) if first or rest else (next(it), next(it))
    scaled_in, acts_in = (next(it), next(it)) if rest else (None, None)
    take_out = lambda: tuple(next(it) for _ in range(len(PARTS[front]) if ends else 1))
    moe_out = None if front else take_out()
    back_out = None if rest else take_out()
    keep, send = (None, None) if front else (next(it), next(it))
    pick = None if rest else next(it)
    scaled_out, acts_out = (next(it), next(it)) if front else (None, None)
    pick_t = next(it) if front and ends else None
    w, scaled, acts, w_sem, in_sem, out_sem = (next(it) for _ in range(6))
    moe = None if front else next(it)
    back = None if rest else next(it)
    xs, cs, x_sem, c_sem = (None,) * 4 if rest else (next(it) for _ in range(4))
    xt, ct, keep_s, send_s, t_sem, g_sem = (None,) * 6 if front else (next(it) for _ in range(6))
    low = next(it) if ends else None
    rows_total = scaled.shape[0]
    spans = [pl.ds(at, block) for at in range(0, rows_total, block)]
    ids = [sc[total + 1 + 2 * (total // 2) + side] + ROUTER_LANE for side in range(2)]

    def load_rows(i):
        pltpu.make_async_copy(n2.at[spans[i]], xs.at[spans[i]], x_sem.at[i]).start()
        pltpu.make_async_copy(cot.at[spans[i]], cs.at[spans[i]], c_sem.at[i]).start()

    def load_wide():
        for k, (src, dst) in enumerate(((moe_in, moe), (back_in, back))):
            if src is not None:
                pltpu.make_async_copy(src, dst, in_sem.at[k]).start()
        if not front:
            pltpu.make_async_copy(n2t, xt, t_sem.at[0]).start()
            pltpu.make_async_copy(cott, ct, t_sem.at[1]).start()

    kinds = pl.ds(2, 1) if rest else pl.ds(0, 3)
    fetch_weights(sc, bufs, w, kinds, local, shard, hidden, w_sem)
    if rest:
        pltpu.make_async_copy(scaled_in, scaled, out_sem.at[2]).start()
        load_wide()
        pltpu.make_async_copy(acts_in, acts, out_sem.at[3]).start()
        pltpu.make_async_copy(w.at[kinds], w.at[kinds], w_sem).wait()
        pltpu.make_async_copy(scaled_in, scaled, out_sem.at[2]).wait()
    else:
        for i in range(len(spans)):
            load_rows(i)
        pltpu.make_async_copy(w.at[kinds], w.at[kinds], w_sem).wait()
        for i, rows in enumerate(spans):
            pltpu.make_async_copy(n2.at[rows], xs.at[rows], x_sem.at[i]).wait()
            pltpu.make_async_copy(cot.at[rows], cs.at[rows], c_sem.at[i]).wait()
            if i == 1:
                load_wide()
            picked = activate(ids, hidden, rows, xs[rows, :], cs[rows, :], w, wt, pick_in, pick, scaled, acts)
            if pick_t is not None:
                pick_t[:, rows] = picked.T[ROUTER_LANE : ROUTER_LANE + EXPERTS]

    for k, (src, dst) in enumerate(((moe_in, moe), (back_in, back))):
        if src is not None:
            pltpu.make_async_copy(src, dst, in_sem.at[k]).wait()
    outs = []
    if not front:
        outs.append((moe, moe_out, 0, lambda rows: mm_nt(scaled[rows, :], w[2])))
    if not rest:
        two = lambda rows: mm_nt(acts[rows, 0 : 2 * hidden], w[0]) + mm_nt(acts[rows, 2 * hidden :], w[1])
        outs.append((back, back_out, 1, two))
    for i, rows in enumerate(spans):
        for acc, halves, k, make in outs:
            made = make(rows) + acc[rows, :]
            scr = acc if low is None else low
            scr[rows, :] = made.astype(scr.dtype)
            part, at = 0, i
            while len(halves) > 1 and at >= PARTS[front][part]:
                part, at = part + 1, at - PARTS[front][part]
            to = halves[part].at[pl.ds(at * block, block)]
            pltpu.make_async_copy(scr.at[rows], to, out_sem.at[k]).start()
    if front:
        pltpu.make_async_copy(scaled, scaled_out, out_sem.at[2]).start()
        pltpu.make_async_copy(acts, acts_out, out_sem.at[3]).start()
    else:
        pltpu.make_async_copy(n2t, xt, t_sem.at[0]).wait()
        pltpu.make_async_copy(cott, ct, t_sem.at[1]).wait()
        if rest:
            pltpu.make_async_copy(acts_in, acts, out_sem.at[3]).wait()
        pair_grads(sc, total, shard, hidden, xt, ct, scaled, acts, keep_s, send_s, keep, send, g_sem)
    for acc, _, k, _ in outs:
        scr = acc if low is None else low
        pltpu.make_async_copy(scr, scr, out_sem.at[k]).wait()
    if front:
        pltpu.make_async_copy(scaled, scaled_out, out_sem.at[2]).wait()
        pltpu.make_async_copy(acts, acts_out, out_sem.at[3]).wait()
    else:
        pltpu.make_async_copy(keep_s, keep, g_sem.at[0]).wait()
        pltpu.make_async_copy(send_s, send, g_sem.at[1]).wait()


def experts(mode, dense, turned, wt, scalars, bufs, local, moe_in, back_in, pick_in, made, deps):
    width, rows = turned[0].shape
    shard, hidden = bufs[0].shape[2:]
    slots = len(bufs) // 2
    front, rest, ends = mode.startswith("front"), mode.startswith("rest"), mode.endswith("_end")
    first = False
    hbm, table = any_space(), whole((rows, LANES))
    ins, specs, outs, out_specs = [], [], [], []

    def put(arrays, spec):
        ins.extend(arrays)
        specs.extend([spec] * len(arrays))

    def give(shape, kind, spec=None):
        outs.append(sds(shape, kind))
        out_specs.append(spec or any_space())

    if not rest:
        put(dense, hbm)
        put([wt], table)
    if not front:
        put(turned, hbm)
    put(bufs, hbm)
    if not first and not front:
        put([moe_in], hbm)
    if not first and not rest:
        put([back_in], hbm)
        put([pick_in], table)
    if rest:
        put(made, hbm)
    pieces = [(256 * p, width) for p in PARTS[front]] if ends else [(rows, width)]
    for shape in pieces * (2 if mode == "all" else 1):
        give(shape, bf if ends else f32)
    if not front:
        give((slots, 6, shard, hidden), bf)
        give((slots, 6, shard, hidden), bf)
    if not rest:
        give((rows, LANES), f32, table)
    if front:
        give((rows, 2 * hidden), bf)
        give((rows, 4 * hidden), bf)
    if front and ends:
        give((EXPERTS, rows), f32, whole((EXPERTS, rows)))
    dma = pltpu.SemaphoreType.DMA
    scratch = [
        pltpu.VMEM((3, width, 2 * hidden), bf),
        pltpu.VMEM((rows, 2 * hidden), bf),
        pltpu.VMEM((rows, 4 * hidden), bf),
        dma,
        dma((2,)),
        dma((4,)),
    ]
    scratch += [pltpu.VMEM((rows, width), f32)] * (2 if mode == "all" else 1)
    if not rest:
        scratch += [pltpu.VMEM((rows, width), bf)] * 2 + [dma((rows // 256,))] * 2
    if not front:
        scratch += [pltpu.VMEM((width, rows), bf)] * 2 + [pltpu.VMEM((slots, 6, shard, hidden), bf)] * 2 + [dma((2,))] * 2
    if ends:
        scratch.append(pltpu.VMEM((rows, width), bf))
    return call(
        functools.partial(experts_kernel, (shard, hidden, local, first, mode, len(bufs))),
        "experts_" + mode,
        (1,),
        ins,
        specs,
        outs,
        out_specs,
        scratch,
        36 * rows * width * hidden,
        scalars,
        deps,
    )


def hop_kernel(cfg, sc, *refs):
    pairs, stage, core_at = cfg
    core = sc[core_at]
    it = iter(refs)
    keeps = [next(it) for _ in range(pairs)]
    gots = [next(it) for _ in range(pairs)]
    came = next(it) if stage else None
    out = next(it)
    for p in range(pairs):
        total = keeps[p][0].astype(f32) + gots[p][0].astype(f32)
        if stage == "end":
            total = place_half(total, core, 2) + came[p].astype(f32)
        elif stage == "second":
            total = total + place_half(came[p].astype(f32), core, 2)
        elif stage:
            total = total + came[p].astype(f32)
        out[p] = total.astype(bf)


def hop_sum(keeps, gots, came, slot, stage, scalars, core_at, deps=()):
    pairs = len(keeps)
    slots, mats, shard, hidden = keeps[0].shape
    lanes = hidden // 2 if stage in (None, "end") else hidden
    side = 1 if stage == "end" else 0
    per = mats // 2 if mats % 2 == 0 else mats
    piece = pl.BlockSpec((1, per, shard, lanes), lambda m, s: (slot, m, 0, side))
    wide = lambda a: pl.BlockSpec((pairs, per, shard, a.shape[3]), lambda m, s: (0, m, 0, 0))
    out = sds((pairs, mats, shard, hidden // 2 if stage is None else hidden), bf)
    ins = [*keeps, *gots] + ([] if came is None else [came])
    specs = [piece] * (2 * pairs) + ([] if came is None else [wide(came)])
    kernel = functools.partial(hop_kernel, (pairs, stage, core_at))
    return call(kernel, "hop_sum", (mats // per,), ins, specs, [out], [wide(out)], [], 0, scalars, deps)[0]


def emit_kernel(sc, mine, theirs, *refs):
    for m in range(6):
        refs[m % 3 - 3][m // 3] = mine[0, m].astype(f32) + theirs[0, m].astype(f32)


def emit(group, first, total, into, core, deps):
    pairs, mats, shard, hidden = group[0].shape
    ins = [*group, *(into or [])]
    spec = pl.BlockSpec((1, mats, shard, hidden), lambda i, s: (i, 0, 0, 0))
    out_spec = pl.BlockSpec((2, shard, hidden), lambda i, s: (i + first // 2, 0, 0))
    outs = [sds((total, shard, hidden), f32)] * 3
    aliases = {1 + len(deps) + 2 + k: k for k in range(3)} if into else {}
    specs = [spec, spec] + [any_space()] * (len(ins) - 2)
    return call(emit_kernel, "emit", (pairs,), ins, specs, outs, [out_spec] * 3, [], 0, core, deps, aliases=aliases)


def norm_back(values, gain, grad):
    scale = lax.rsqrt(jnp.mean(values * values, axis=-1, keepdims=True) + norm_eps)
    inner = jnp.mean(values * gain * grad, axis=-1, keepdims=True)
    passed = scale * gain * grad - values * (scale * scale * scale * inner)
    return passed, jnp.sum(grad * values * scale, axis=0, keepdims=True)


def pick_part(refs, parts):
    step = pl.program_id(0)
    value, at = refs[0][...], 0
    for ref, size in zip(refs, parts):
        value = jnp.where(step >= at, ref[...], value)
        at += size
    return value


def part_specs(block, parts):
    specs, first = [], 0
    for p in parts:
        per = p.shape[0] // block
        specs.append(pl.BlockSpec((block, p.shape[1]), lambda i, s, first=first, per=per: (jnp.clip(i - first, 0, per - 1), 0)))
        first += per
    return specs


def combine_kernel(sc, res, *refs):
    count = len(refs) // 2
    total = pick_part(refs[:count], PARTS[0]).astype(f32) + pick_part(refs[count : 2 * count], PARTS[0]).astype(f32)
    refs[-1][...] = (res[...] + total).astype(bf)


def combine(res, own, far, core, deps, block=256):
    rows, width = res.shape
    specs = [rows_of(block, width)] + part_specs(block, own) + part_specs(block, far)
    out = sds((rows, width), bf)
    return call(combine_kernel, "combine", (rows // block,), [res, *own, *far], specs, [out], [rows_of(block, width)], [], 0, core, deps)[0]


def unsettle_kernel(sc, *refs):
    count = len(PARTS[1])
    own, far, refs = refs[:count], refs[count : 2 * count], refs[2 * count :]
    unsettle_rows(own, far, *refs)


def unsettle_rows(own, far, pick_a, pick_b, wt, res, cot, extra, w_own, rg_out, low_t_out, dout_out, ll_out, gain_out, w, sem):
    step = pl.program_id(0)

    @pl.when(step == 0)
    def _():
        pltpu.make_async_copy(w_own, w, sem).start()
        pltpu.make_async_copy(w_own, w, sem).wait()
        gain_out[...] = jnp.zeros_like(gain_out)

    weights = wt[...]
    picked = pick_a[...] + pick_b[...]
    room = lambda n: jnp.zeros((n, picked.shape[1]), f32)
    picked = jnp.concatenate([room(ROUTER_LANE), picked, room(LANES - ROUTER_LANE - EXPERTS)], axis=0).T
    logit_low = (weights * (picked - jnp.sum(weights * picked, axis=-1, keepdims=True))).astype(bf)
    ll_out[...] = logit_low
    grad = pick_part(own, PARTS[1]).astype(f32) + pick_part(far, PARTS[1]).astype(f32) + mm(logit_low, extra[...])
    passed, gain = norm_back(res[...], extra[1:2, :].astype(f32), grad)
    gain_out[...] += gain
    total = cot[...].astype(f32) + passed
    rg_out[...] = total
    low = total.astype(bf)
    low_t_out[...] = low.T
    dout_out[...] = mm(low, lanes_of(w, 0, w.shape[0])).astype(bf)


def unsettle(back, far, picks, wt, res, cot, extra, w_own, core, deps, block=256):
    rows, width = res.shape
    cols = w_own.shape[0] * LANES
    wide, thin = rows_of(block, width), rows_of(block, LANES)
    across = pl.BlockSpec((EXPERTS, block), lambda i, s: (0, i))
    return call(
        unsettle_kernel,
        "unsettle",
        (rows // block,),
        [*back, *far, *picks, wt, res, cot, extra, w_own],
        [*part_specs(block, back), *part_specs(block, far), across, across, thin, wide, wide, whole(extra.shape), any_space()],
        [sds((rows, width), f32), sds((width, rows), bf), sds((rows, cols), bf), sds((rows, LANES), bf), sds((1, width), f32)],
        [wide, pl.BlockSpec((width, block), lambda i, s: (0, i)), rows_of(block, cols), thin, whole((1, width))],
        [pltpu.VMEM(w_own.shape, bf), pltpu.SemaphoreType.DMA],
        2 * rows * width * cols,
        core,
        deps,
    )


def scaled_sum(weights, grads, gain):
    return jnp.sum(weights.astype(f32) * grads, axis=1, keepdims=True) / gain.astype(f32)


def leave(parts, core, shard, keep, send):
    last = pl.program_id(0) == pl.num_programs(0) - 1
    cut = lambda a: (a[:, :LANES], a[:, LANES:])

    @pl.when(jnp.logical_not(last))
    def _():
        for b, part in enumerate(parts):
            keep[0, b] = part[:shard]
            send[0, b] = part[shard:]

    @pl.when(last)
    def _():
        for b, part in enumerate(parts):
            keep[0, b], send[0, b] = mix_halves(core, cut(part[:shard]), cut(part[shard:]))


def early_grads_kernel(core_at, sc, low_a, low_b, mixed_a, mixed_b, n2_a, n2_b, ll, col_a, col_b, n1_a, n1_b, dq, w_a, w_b, keep, send):
    prompt = mixed_a.shape[0]
    shard = low_a.shape[0]
    join = lambda a, b: jnp.concatenate([a[...], b[...]], axis=0)
    tall = join(low_a, low_b)
    made = mm(tall[:, 0:prompt], mixed_a[...]) + mm(tall[:, prompt:], mixed_b[...])
    query = mm(join(n1_a, n1_b), dq[...])
    blocks = dq.shape[1] // LANES
    weights = jnp.concatenate([lanes_of(ref, 0, blocks) for ref in (w_a, w_b)], axis=0)
    gains = jnp.concatenate([ref[ref.shape[0] - 1, :, 0:1] for ref in (w_a, w_b)], axis=0)
    first = scaled_sum(weights, query, gains)
    extra = mm(join(n2_a, n2_b), ll[...]) + join(col_a, col_b)
    lane = lax.broadcasted_iota(jnp.int32, extra.shape, 1)
    extra = jnp.where(lane == 0, first, extra)
    whole_row = jnp.concatenate([made, query, extra], axis=1).astype(bf)
    wide = 2 * LANES
    leave([whole_row[:, b * wide : (b + 1) * wide] for b in range(whole_row.shape[1] // wide)], sc[core_at], shard, keep, send)


def early_grads(low_t, mixed, n2t, ll, column, n1t, dq, w, scalars, first_rank, core_at, shard, deps):
    width, rows = low_t.shape
    slots = (scalars.shape[0] - first_rank) // 2
    cols = mixed[0].shape[1] + LANES + dq.shape[1]
    at = lambda k: (lambda i, s: (s[first_rank + k * slots + i], 0))
    w_at = lambda k: (lambda i, s: (0, s[first_rank + k * slots + i], 0))
    two = lambda lanes: [pl.BlockSpec((shard, lanes), at(k)) for k in range(2)]
    out = sds((slots, cols // (2 * LANES), shard, 2 * LANES), bf)
    out_spec = pl.BlockSpec((1, *out.shape[1:]), lambda i, s: (i, 0, 0, 0))
    return call(
        functools.partial(early_grads_kernel, core_at),
        "early_grads",
        (slots,),
        [low_t, low_t, *mixed, n2t, n2t, ll, column, column, n1t, n1t, dq, w, w],
        two(rows)
        + [whole(a.shape) for a in mixed]
        + two(rows)
        + [whole(ll.shape)]
        + two(LANES)
        + two(rows)
        + [whole(dq.shape)]
        + [pl.BlockSpec((w.shape[0], shard, LANES), w_at(k)) for k in range(2)],
        [out, out],
        [out_spec, out_spec],
        [],
        2 * rows * width * cols,
        scalars,
        deps,
    )


def late_grads_kernel(cfg, sc, left_a, left_b, dq, low_kv, w_a, w_b, keep, send):
    core_at, first_block, count = cfg
    core = sc[core_at]
    shard = left_a.shape[0]
    tall = jnp.concatenate([left_a[...], left_b[...]], axis=0)
    made = jnp.concatenate([mm(tall, dq[...]), mm(tall, low_kv[...])], axis=1)
    blocks = made.shape[1] // LANES
    weights = jnp.concatenate([lanes_of(ref, first_block, blocks) for ref in (w_a, w_b)], axis=0)
    gains = jnp.concatenate([ref[ref.shape[0] - 1, :, 0:1] for ref in (w_a, w_b)], axis=0)
    first = scaled_sum(weights, made, gains)
    lane = lax.broadcasted_iota(jnp.int32, (2 * shard, LANES), 1)
    made = jnp.concatenate([made, jnp.where(lane == 0, first, 0.0)], axis=1).astype(bf)
    wide = 2 * LANES
    leave([made[:, b * wide : (b + 1) * wide] for b in range(count)], core, shard, keep, send)


def late_grads(left, dq, low_kv, w, first_block, scalars, first_rank, core_at, shard, deps):
    width, rows = left.shape
    slots = (scalars.shape[0] - first_rank) // 2
    count = (dq.shape[1] + low_kv.shape[1] + LANES) // (2 * LANES)
    at = lambda k: (lambda i, s: (s[first_rank + k * slots + i], 0))
    w_at = lambda k: (lambda i, s: (0, s[first_rank + k * slots + i], 0))
    out = sds((slots, count, shard, 2 * LANES), bf)
    out_spec = pl.BlockSpec((1, count, shard, 2 * LANES), lambda i, s: (i, 0, 0, 0))
    return call(
        functools.partial(late_grads_kernel, (core_at, first_block, count)),
        "late_grads",
        (slots,),
        [left, left, dq, low_kv, w, w],
        [pl.BlockSpec((shard, rows), at(k)) for k in range(2)]
        + [whole(dq.shape), whole(low_kv.shape)]
        + [pl.BlockSpec((w.shape[0], shard, LANES), w_at(k)) for k in range(2)],
        [out, out],
        [out_spec, out_spec],
        [],
        4 * rows * width * count * LANES,
        scalars,
        deps,
    )


def spread_kernel(sc, early_a, early_b, late_a, late_b, output, query, key, value, extra):
    join = lambda a, b: jnp.concatenate([a[0, k].astype(f32) + b[0, k].astype(f32) for k in range(a.shape[1])], axis=1)
    early, late = join(early_a, early_b), join(late_a, late_b)
    cols = output.shape[1]
    output[...] = early[:, 0:cols]
    half = early.shape[1] - cols - LANES
    query[:, 0:half] = early[:, cols : cols + half]
    at = query.shape[1] - half
    query[:, half:] = late[:, 0:at]
    for out in (key, value):
        out[...] = late[:, at : at + out.shape[1]]
        at += out.shape[1]
    extra[...] = jnp.concatenate([early[:, cols + half :], late[:, at : at + LANES]], axis=1)


def spread(early, late, widths, core):
    shard = early[0].shape[2]
    outs = [sds((shard, size), f32) for size in (*widths, 2 * LANES)]
    ins = [*early, *late]
    return call(spread_kernel, "spread", (1,), ins, [whole(a.shape) for a in ins], outs, [whole(o.shape) for o in outs], [], 0, core)


def key_value_grads_kernel(sc, cosine, sine, *refs):
    *ins, out = refs
    parts = len(ins) // 2
    sums, mores = ins[:parts], ins[parts:]
    step = pl.program_id(0)
    shared = jnp.where(step < pl.num_programs(0) // 2, 1.0, 0.0).astype(f32)
    at = 0
    for is_key in (True, False):
        for own, more in zip(sums, mores):
            kvs = own.shape[0] // 2
            for kv in range(0, kvs, 2):
                heads = [kv + k + (0 if is_key else kvs) for k in range(2)]
                other = [jnp.where(step == 0, more[h, :, :HEAD_DIM], more[h, :, HEAD_DIM:]) for h in heads]
                pair = jnp.concatenate([own[h] + o * shared for h, o in zip(heads, other)], axis=1)
                if is_key:
                    pair = rope(pair, cosine[...], -sine[...])
                out[:, at : at + LANES] = pair.astype(bf)
                at += LANES


def key_value_grads(cosine, sine, sums, mores, core, deps, block=256):
    rows = cosine.shape[0]
    cols = sum(s.shape[0] for s in sums) * HEAD_DIM
    own = lambda a: pl.BlockSpec((a.shape[0], block, HEAD_DIM), lambda i, s: (0, i, 0))
    return call(
        key_value_grads_kernel,
        "key_value_grads",
        (rows // block,),
        [cosine, sine, *sums, *mores],
        [rows_of(block, LANES), rows_of(block, LANES)] + [own(a) for a in sums] + [whole(a.shape) for a in mores],
        [sds((rows, cols), bf)],
        [rows_of(block, cols)],
        [],
        0,
        core,
        deps,
    )[0]


def finish_kernel(sc, tok, extra, rg, *refs):
    *lows, w_own, mine_a, mine_b, theirs_a, theirs_b, out, w, sem = refs
    blocks = w.shape[0] // 2

    @pl.when(pl.program_id(0) == 0)
    def _():
        pltpu.make_async_copy(w_own.at[pl.ds(0, blocks)], w.at[pl.ds(0, blocks)], sem).start()
        for core, pieces in ((sc[0], (mine_a, mine_b)), (1 - sc[0], (theirs_a, theirs_b))):
            at = blocks + core * (blocks // 2)
            for piece in pieces:
                pltpu.make_async_copy(piece, w.at[pl.ds(at, piece.shape[0])], sem).start()
                at = at + piece.shape[0]
        pltpu.make_async_copy(w, w, sem).wait()

    low = jnp.concatenate([f[...] for f in lows], axis=1)
    grad = mm_nt(low, lanes_of(w, 0, 2 * blocks))
    passed, _ = norm_back(tok[...].astype(f32), extra[0:1, :].astype(f32), grad)
    out[...] = rg[...] + passed


def finish(tokens, extra, rg, lows, w_own, w_mine, w_theirs, core, deps, block=256):
    rows, width = tokens.shape
    wide = rows_of(block, width)
    blocks = 4 * sum(p.shape[0] for p in w_mine)
    return call(
        finish_kernel,
        "finish",
        (rows // block,),
        [tokens, extra, rg, *lows, w_own, *w_mine, *w_theirs],
        [wide, whole(extra.shape), wide, *[rows_of(block, f.shape[1]) for f in lows]] + [any_space()] * 5,
        [sds((rows, width), f32)],
        [wide],
        [pltpu.VMEM((blocks, width, LANES), bf), pltpu.SemaphoreType.DMA],
        2 * rows * width * blocks * LANES,
        core,
        deps,
    )[0]


def body(
    tokens,
    routes,
    cotangent,
    norm_one,
    w_query,
    key_weight,
    value_weight,
    w_output,
    norm_two,
    w_router,
    w_gate,
    w_up,
    w_down,
):
    window.turn()
    window.turn()
    window.gated = False
    count = lax.axis_size("dp")
    core = lax.axis_index("ctx")
    place = ring_place(lax.axis_index("dp"), count)
    rows, width = tokens.shape[2:]
    prompt = PROMPT_TOKENS // lax.axis_size("ctx")
    heads = w_query.shape[1] // HEAD_DIM
    kvs = key_weight.shape[1] // HEAD_DIM
    shard, hidden = w_gate.shape[1:]
    core_only = jnp.stack([core, core]).astype(jnp.int32)
    ranks = gather_sources(place, core, count)
    slots = scatter_sources(place, core, count)
    first_rank, core_at = len(ranks) + 1, len(ranks)

    def scalars(*more):
        return jnp.stack([*ranks, core, *slots, *more]).astype(jnp.int32)

    plain = scalars()
    tok = tokens.reshape(rows, width)
    cot = cotangent.reshape(rows, width)
    ids = routes.reshape(rows, TOPK)

    packed = pack(w_query, key_weight, value_weight, w_output, w_router, norm_one, norm_two, core_only)
    firsts = Gather(packed, core, count, 0)
    firsts.step()
    firsts.step()

    sizes = [4, 4, 4, 4]
    starts = [sum(sizes[:k]) for k in range(len(sizes))]
    chunks = []

    owns = [jnp.stack([w[at : at + size] for w in (w_gate, w_up, w_down)], axis=0) for at, size in zip(starts, sizes)]

    def open_chunk(*held):
        chunks.append(Gather(after(owns[len(chunks)], *held), core, count, 3))

    offsets = jnp.arange(rows, dtype=jnp.int32)
    positions = jnp.where(offsets < prompt, core * prompt + offsets, PROMPT_TOKENS + offsets - prompt)
    half_dim = HEAD_DIM // 2
    inverse = rope_base ** (-2.0 * jnp.arange(half_dim).astype(f32) / HEAD_DIM)
    angles = positions.astype(f32)[:, None] * inverse
    cosine = jnp.tile(jnp.cos(angles), (1, LANES // half_dim))
    sine = jnp.sin(angles)
    sine = jnp.tile(jnp.concatenate([-sine, sine], axis=1), (1, LANES // HEAD_DIM))
    cott = cot.T
    zero_wide, zero_table = jnp.zeros((rows, width), f32), jnp.zeros((rows, LANES), f32)

    firsts.mine[-1], cott, zero_wide, zero_table, cosine, sine, *owns = lax.optimization_barrier(
        (firsts.mine[-1], cott, zero_wide, zero_table, cosine, sine, *owns)
    )
    firsts.step()
    firsts.step()
    firsts.share()
    open_chunk(firsts.mine[-1])
    c0 = chunks[0]
    window.turn()
    window.turn()
    c0.step()
    w_first, w_out, w_out_half, extra, q, kv, kv_prompt, n1t = project(
        tok, cosine, sine, plain, firsts.bufs, heads, kvs, prompt, window.turn()
    )
    other = swap(kv_prompt, "ctx")
    out_far_mine = swap(after(w_out_half, kv_prompt), "tp")
    c0.step(kv_prompt)
    mixed_b, lse_b = attend(q, kv, other, core_only, 1, window.turn())
    far_b = swap(mixed_b, "tp")
    c0.step(lse_b)
    open_chunk(lse_b)
    c1 = chunks[1]
    c1.step()
    out_far_theirs = swap(after(out_far_mine, lse_b), "ctx")
    mixed_a, lse_a = attend(q, kv, other, core_only, 0, window.turn())
    far_a = swap(mixed_a, "tp")
    c0.step(lse_a)
    c1.step(lse_a)
    mixed, lse = (mixed_a, mixed_b), (lse_a, lse_b)
    res, n2, n2t, wt = settle(
        tok, ids, mixed, (far_a, far_b), extra, w_out, out_far_mine, out_far_theirs, core_only, [cott, zero_wide, *window.turn()]
    )
    scatters = [Scatter(core, count, plain, core_at) for _ in range(3)]
    state = dict(moe=zero_wide, back=zero_wide, pick=zero_table)

    def work(pair, mode="all", deps=None):
        at = 2 * pair
        k = max(k for k in range(len(starts)) if starts[k] <= at)
        sc = scalars(jnp.int32(at), jnp.int32(at + 1))
        bufs, local = chunks[k].bufs, at - starts[k]
        made = experts(
            mode, (n2, cot), (n2t, cott), wt, sc, bufs, local, state["moe"], state["back"], state["pick"], state.get("made"),
            window.turn() if deps is None else deps,
        )
        if mode == "all":
            state["moe"], state["back"], keep, send, state["pick"] = made
            return keep, send, state["pick"]
        if mode.startswith("front"):
            *back, state["pick"], scaled, acts = made[:-1] if mode.endswith("_end") else made
            state["back"] = back if mode.endswith("_end") else back[0]
            state["made"] = [scaled, acts]
            return made[-1]
        *moe, keep, send = made
        state["moe"] = moe if mode.endswith("_end") else moe[0]
        return keep, send, moe[0]

    s0, s1, s2 = scatters
    c0.share(wt)
    c1.step(wt)
    open_chunk(wt)
    c2 = chunks[2]
    c2.step()
    keep, send, token = work(0)

    s0.add(keep, send)
    c1.step(token)
    c2.step(token)
    first_part = w_first.shape[0] // 2
    split = (first_part + 1) // 2
    first_half = take(after(w_first, token), core * first_part, first_part)
    first_far_a = swap(first_half[:split], "tp")
    keep, send, token = work(1)

    s0.add(keep, send)
    c1.share(token)
    c2.step(token)
    open_chunk(token)
    c3 = chunks[3]
    c3.step()
    first_far_b = swap(after(first_half[split:], token), "tp")
    theirs_a = swap(after(first_far_a, token), "ctx")
    keep, send, token = work(2)

    s0.add(keep, send)
    c2.step(token)
    c3.step(token)
    keep, send, token = work(3)

    s1.add(keep, send)
    c2.share(token)
    c3.step(token)
    s0.step([token])
    theirs_b = swap(after(first_far_b, token), "ctx")
    keep, send, token = work(4)

    s1.add(keep, send)
    c3.step(token)
    s0.step([token])
    keep, send, token = work(5)

    s1.add(keep, send)
    c3.share(token)
    s0.step([token])
    token = work(6, "front")
    made_early = state["made"]

    window.gated = True
    token = window.gate(token)
    s0.step([token])
    pick_t = work(7, "front_end", window.step())
    made_late = state["made"]
    back = state["back"]

    back_far_a = swap(back[0], "tp")
    pick_far = swap(after(pick_t, back[0]), "tp")
    token = window.gate(pick_t)
    s1.step([token])
    s0_mine, s0_theirs = s0.finish([token])
    state["made"] = made_early
    keep_early, send_early, token = work(6, "rest", [s0_mine, *window.step()])
    token = window.gate(token, back_far_a, pick_far)
    back_far_b = swap(after(back[1], token), "tp")
    s2.add(keep_early, send_early, token)
    s1.step([token])
    emitted = emit((s0_mine, s0_theirs), 0, EXPERTS, None, core_only, [token])
    state["made"] = made_late
    keep, send, token = work(7, "rest_end", [emitted[0], *window.step()])
    moe = state["moe"]
    token = window.gate(token, back_far_b)
    s2.add(keep, send, token)
    s1.step([token])
    rg, low_t, dout, ll, gain_two = unsettle(
        back, (back_far_a, back_far_b), (pick_t, pick_far), wt, res, cot, extra, w_out, core_only, window.step()
    )
    token = window.gate(ll)
    moe_far_a = swap(after(moe[0], token), "tp")
    s1.step([token])
    s2.step([token])
    parts = 2
    dq_a, dkv_a, dother_a = attend_back(q, kv, other, dout, mixed, lse, cosine, sine, core_only, 0, parts, window.step())
    token = window.gate(dother_a)
    more_a = swap(after(dother_a, token), "ctx")
    s2.step([token])
    lane = jnp.arange(LANES)
    column = jnp.where(lane == 1, gain_two[0][:, None], 0.0)
    early_keep, early_send = early_grads(
        low_t, mixed, n2t, ll, column, n1t, dq_a, w_first, plain, first_rank, core_at, shard, [dother_a, *window.step()]
    )
    token = window.gate(early_keep, moe_far_a)
    far_qa = swap(after(dq_a, token), "tp")
    early = Scatter(core, count, plain, core_at)
    early.add(early_keep, early_send, token)
    s2.step([token])
    s1_mine, s1_theirs = s1.finish([token])
    dq_b, dkv_b, dother_b = attend_back(
        q, kv, other, dout, mixed, lse, cosine, sine, core_only, 1, parts, [s1_mine, *window.step()]
    )
    token = window.gate(dother_b, far_qa)
    more_b = swap(after(dother_b, token), "ctx")
    far_qb = swap(after(dq_b, token), "tp")
    early.step([token])
    low_kv = key_value_grads(cosine, sine, [dkv_a, dkv_b], [more_a, more_b], core_only, window.step())
    token = window.gate(low_kv)
    early.step([token])
    s2.step([token])
    half_blocks = heads // 4
    last_keep, last_send = late_grads(
        n1t, dq_b, low_kv, w_first, half_blocks, plain, first_rank, core_at, shard, window.step()
    )
    token = window.gate(last_keep, far_qb)
    far_kv = swap(after(low_kv, token), "tp")
    late = Scatter(core, count, plain, core_at)
    late.add(last_keep, last_send, token)
    early.step([token])
    emitted = emit((s1_mine, s1_theirs), EXPERTS * 3 // 8, EXPERTS, emitted, core_only, [token, early.value])
    late.step([emitted[0]])
    s2_mine, s2_theirs = s2.finish([late.value])
    early.step([s2_mine])
    late.step([s2_mine])
    moe_far_b = swap(after(moe[1], late.value), "tp")
    lows = [dq_a, dq_b, low_kv, far_qa, far_qb, far_kv]
    token_grad = finish(
        tok, extra, rg, lows, w_first, (first_far_a, first_far_b), (theirs_a, theirs_b), core_only, [late.value, early.value]
    ).reshape(tokens.shape)
    late.step([token_grad, moe_far_b])
    early_sums = early.finish([late.value])
    grad_gate, grad_up, grad_down = emit((s2_mine, s2_theirs), EXPERTS * 3 // 4, EXPERTS, emitted, core_only, [early_sums[0]])
    late.step([grad_gate])
    result = combine(res, moe, (moe_far_a, moe_far_b), core_only, [late.value]).reshape(tokens.shape)
    kv_width = kvs * HEAD_DIM
    widths = (w_output.shape[1], w_query.shape[1], kv_width, kv_width)
    grad_output, grad_query, grad_key, grad_value, extras = spread(early_sums, late.finish(), widths, core_only)
    grad_norm_two = extras[:, 1]
    grad_router = extras[:, ROUTER_LANE : ROUTER_LANE + EXPERTS]
    gain_part = extras[:, 0] + extras[:, LANES]
    grad_norm_one = gain_part + swap(gain_part, "tp")
    return (
        result,
        token_grad,
        grad_norm_one,
        grad_query,
        grad_key,
        grad_value,
        grad_output,
        grad_norm_two,
        grad_router,
        grad_gate,
        grad_up,
        grad_down,
    )


def solution(mesh):
    slab = P("dp", "ctx", None, None)
    split, rows_only, expert = P("dp", "tp"), P("dp"), P(None, "dp", "tp")
    return jax.shard_map(
        body,
        mesh=mesh,
        in_specs=(slab, slab, slab, rows_only, split, split, split, split, rows_only, P("dp", None), expert, expert, expert),
        out_specs=(slab, slab, rows_only, split, split, split, split, rows_only, P("dp", None), expert, expert, expert),
        check_vma=False,
    )
```

```python
import functools

import jax
import jax.numpy as jnp
from jax import lax
from jax.experimental import pallas as pl
from jax.experimental.pallas import tpu as pltpu
from jax.sharding import PartitionSpec as P

HEAD_DIM = 64
EXPERTS = 16
TOPK = 8
PROMPT_TOKENS = 1024
LANES = 128
ROUTER_LANE = 16

norm_eps = 1e-06
rope_base = 10000.0
masked_score = -1e30
bf = jnp.bfloat16
f32 = jnp.float32
contract_cols = (((1,), (1,)), ((), ()))
COSTS = dict(experts_all=24, experts_front_end=18, experts_rest_end=13, experts_front=18, experts_rest=13, attend=19, project=18, settle=16, unsettle=17, attend_back=25)
COSTS.update(early_grads=12, key_value_grads=7, late_grads=10, finish=18, emit=5, hop_sum=5, combine=5)
vmem_bytes = 63 * 1024 * 1024


def mm(a, b):
    return jnp.dot(a, b, preferred_element_type=f32)


def mm_nt(a, b):
    return lax.dot_general(a, b, contract_cols, preferred_element_type=f32)


def whole(shape):
    return pl.BlockSpec(shape, lambda *_: (0,) * len(shape), pipeline_mode=pl.Buffered(1))


def rows_of(block, width):
    return pl.BlockSpec((block, width), lambda i, *_: (i, 0))


def any_space():
    return pl.BlockSpec(memory_space=pltpu.HBM)


def call(kernel, name, grid, ins, in_specs, outs, out_specs, scratch, flops, scalars, deps=(), limit=vmem_bytes, aliases=None):
    moved = sum(a.size * a.dtype.itemsize for a in (*ins, *outs))
    return pl.pallas_call(
        lambda sc, *refs: kernel(sc, *refs[len(deps) :]),
        out_shape=tuple(outs),
        grid_spec=pltpu.PrefetchScalarGridSpec(
            num_scalar_prefetch=1,
            grid=grid,
            in_specs=[pl.BlockSpec(memory_space=pltpu.HBM) for _ in deps] + list(in_specs),
            out_specs=tuple(out_specs),
            scratch_shapes=scratch,
        ),
        compiler_params=pltpu.CompilerParams(vmem_limit_bytes=limit),
        cost_estimate=pl.CostEstimate(flops=COSTS.get(name, 3) * 1_153_000_000, bytes_accessed=1, transcendentals=0),
        name=name,
        input_output_aliases=aliases or {},
    )(scalars, *deps, *ins)


def after(values, *deps):
    return lax.optimization_barrier((values, *deps))[0]


def sds(shape, dtype):
    return jax.ShapeDtypeStruct(tuple(shape), dtype)


def ring_rank(place, count):
    place = lax.rem(place + 2 * count, count)
    return jnp.where(place < count // 2, 2 * place, 2 * count - 1 - 2 * place)


def ring_place(rank, count):
    return jnp.where(rank % 2 == 0, rank // 2, (2 * count - 1 - rank) // 2)


def ring_hop(values, count):
    order = list(range(0, count, 2)) + list(range(count - 1, 0, -2))
    pairs = []
    for k in range(count):
        here, there = order[k], order[(k + 1) % count]
        pairs += [(2 * here, 2 * there), (2 * there + 1, 2 * here + 1)]
    return sent(lax.ppermute(values, ("dp", "ctx"), pairs))


def swap(values, axis):
    swapped = lax.ppermute(values, axis, [(0, 1), (1, 0)])
    return sent(swapped) if axis == "ctx" or not window.gated else swapped


class Window:
    def __init__(self):
        self.now, self.before, self.soon = [], [], []
        self.gated = False

    def turn(self):
        due, self.before, self.now, self.soon = self.before + self.soon, self.now, [], []
        return due

    def step(self):
        due, self.before, self.now, self.soon = self.soon, self.before + self.now, [], []
        return due

    def gate(self, token, *more):
        token = after(token, *self.before, *more)
        self.before = []
        return token


window = Window()


def sent(values):
    window.now.append(values)
    return values


def take(values, start, size, axis=0):
    return lax.dynamic_slice_in_dim(values, start, size, axis)


def place_half(values, core, axis):
    zeros = jnp.zeros_like(values)
    return jnp.where(core == 0, jnp.concatenate([values, zeros], axis), jnp.concatenate([zeros, values], axis))


PLANNED = 4


class Gather:
    def __init__(self, own, core, count, axis):
        self.own, self.core, self.count, self.axis = own, core, count, axis
        self.mine, self.mate, self.hops = [], [], 0

    def share(self, *held):
        if len(self.mate) < len(self.mine):
            self.mate.append(swap(after(self.mine[-1], *held), "ctx"))

    def step(self, *held):
        for _ in range(1 if self.hops else self.count // 2 - PLANNED + 1):
            got = self.hop(*held)
        return got

    def hop(self, *held):
        self.share(*held)
        self.hops += 1
        last = after(self.mine[-1] if self.mine else self.own, *held)
        if self.hops == self.count // 2:
            size = last.shape[self.axis] // 2
            last = take(last, self.core * size, size, self.axis)
        self.mine.append(ring_hop(last, self.count))
        return self.mine[-1]

    def finish(self):
        while self.hops < self.count // 2:
            self.step()
        self.share()
        return self

    @property
    def bufs(self):
        return [self.own, *self.mine, *self.mate]


def gather_sources(place, core, count):
    sign = 1 - 2 * core
    away = list(range(1, count // 2 + 1))
    return [ring_rank(place, count)] + [ring_rank(place - sign * a, count) for a in away] + [ring_rank(place + sign * a, count) for a in away]


def scatter_sources(place, core, count):
    sign = 1 - 2 * core
    away = list(range(1, count // 2))
    keep = [ring_rank(place + sign * a, count) for a in away] + [ring_rank(place + count // 2, count)]
    send = [ring_rank(place - sign * a, count) for a in away] + [ring_rank(place, count)]
    return keep + send


class Scatter:
    def __init__(self, core, count, scalars, core_at):
        self.core, self.count, self.scalars, self.core_at = core, count, scalars, core_at
        self.keeps, self.gots, self.hops, self.got = [], [], 0, None

    def add(self, keep, send, *held):
        self.keeps.append(keep)
        self.gots.append(swap(after(send, *held), "ctx"))
        return self.gots[-1]

    def step(self, deps=()):
        for _ in range(1 if self.hops else self.count // 2 - PLANNED + 1):
            got = self.hop(deps)
        return got

    def hop(self, deps):
        self.hops += 1
        stage = {1: None, 2: "second"}.get(self.hops, "middle")
        slot = self.count // 2 - self.hops if self.hops > 1 else self.count // 2 - 1
        value = hop_sum(self.keeps, self.gots, self.got, slot, stage, self.scalars, self.core_at, deps)
        self.value = value
        window.soon.append(value)
        self.got = ring_hop(value, self.count)
        return self.got

    def finish(self, deps=()):
        while self.hops < self.count // 2:
            self.step()
        mine = hop_sum(self.keeps, self.gots, self.got, self.count // 2 - 1, "end", self.scalars, self.core_at, deps)
        return mine, swap(mine, "ctx")


def load_shards(sc, bufs, dst, shard, sem):
    total = len(bufs)
    hops = total // 2
    half = dst.shape[0] // 2
    for k, buf in enumerate(bufs):
        rows = pl.ds(pl.multiple_of(sc[k] * shard, shard), shard)
        if k in (hops, 2 * hops):
            side = sc[total] if k == hops else 1 - sc[total]
            target = dst.at[pl.ds(side * half, half), rows, :]
        else:
            target = dst.at[:, rows, :]
        pltpu.make_async_copy(buf, target, sem).start()


def lanes_of(ref, first, count):
    return jnp.concatenate([ref[first + b] for b in range(count)], axis=1)


def rope(x, cosine, sine):
    lane = lax.broadcasted_iota(jnp.int32, x.shape, x.ndim - 1)
    ahead = pltpu.roll(x, x.shape[-1] - HEAD_DIM // 2, x.ndim - 1)
    behind = pltpu.roll(x, HEAD_DIM // 2, x.ndim - 1)
    return x * cosine + jnp.where(lax.rem(lane, HEAD_DIM) < HEAD_DIM // 2, ahead, behind) * sine


def lane_column(row, shape, lane_at):
    lane = lax.broadcasted_iota(jnp.int32, shape, 1)
    return jnp.where(lane == lane_at, jnp.broadcast_to(row, (shape[1], shape[0])).T, 0.0)


def pack_kernel(sc, query, key, value, output, router, gain_one, gain_two, out):
    at = 0
    for ref in (query, key, value):
        for b in range(ref.shape[1] // LANES):
            out[at] = ref[:, b * LANES : (b + 1) * LANES]
            at += 1
    shape = out.shape[1:]
    extra = lane_column(gain_one[...].astype(f32), shape, 0) + lane_column(gain_two[...].astype(f32), shape, 1)
    out[at] = extra.astype(bf)
    out[at, :, ROUTER_LANE : ROUTER_LANE + EXPERTS] = router[...]
    for b in range(output.shape[1] // LANES):
        out[at + 1 + b] = output[:, b * LANES : (b + 1) * LANES]
    for b in range(at + 1 + output.shape[1] // LANES, out.shape[0]):
        out[b] = jnp.zeros(shape, bf)


def pack(query, key, value, output, router, gain_one, gain_two, core):
    shard = query.shape[0]
    ins = [query, key, value, output, router, gain_one.reshape(1, shard), gain_two.reshape(1, shard)]
    blocks = (query.shape[1] + key.shape[1] + value.shape[1] + output.shape[1]) // LANES + 1
    blocks += blocks % 2
    out = sds((blocks, shard, LANES), bf)
    return call(pack_kernel, "pack", (1,), ins, [whole(a.shape) for a in ins], [out], [whole(out.shape)], [], 0, core)[0]


def qkv_kernel(shard, kinds, sc, tok, cosine, sine, *refs):
    heads, kvs, total = kinds
    bufs, (w_first, w_out, w_half, extra_out, q_out, kv_out, packed_out, nt_out, w, et, sem, out_sem) = refs[:total], refs[total:]
    step = pl.program_id(0)
    count, half = w_first.shape[0], w_half.shape[0]
    copies = [
        (w.at[pl.ds(0, count)], w_first),
        (w.at[pl.ds(count, 2 * half)], w_out),
        (w.at[pl.ds(count + sc[total] * half, half)], w_half),
    ]

    @pl.when(step == 0)
    def _():
        load_shards(sc, bufs, w, shard, sem)
        pltpu.make_async_copy(w, w, sem).wait()
        for k, (src, dst) in enumerate(copies):
            pltpu.make_async_copy(src, dst, out_sem.at[k]).start()
        et[...] = w[count - 1].T

    extra_out[...] = et[...]
    x = tok[...].astype(f32)
    scale = lax.rsqrt(jnp.mean(x * x, axis=-1, keepdims=True) + norm_eps)
    normed = (x * scale * et[0:1, :].astype(f32)).astype(bf)
    nt_out[...] = normed.T
    cs, sn = cosine[...], sine[...]
    for pair in range((heads + 2 * kvs) // 4):
        made = mm(normed, lanes_of(w, 2 * pair, 2))
        for side in range(2):
            first = 4 * pair + 2 * side
            part = made[:, side * LANES : (side + 1) * LANES]
            if first < heads + kvs:
                part = rope(part, cs, sn)
            out, at = kv_out, first - heads
            if first < heads:
                part, out, at = part * (1.0 / HEAD_DIM), q_out, first
            low = part.astype(bf)
            for k in range(2):
                one = low[:, k * HEAD_DIM : (k + 1) * HEAD_DIM]
                out[at + k] = one
                if first >= heads:
                    for quarter in range(2):

                        @pl.when(step == quarter)
                        def _():
                            packed_out[at + k, :, quarter * HEAD_DIM : (quarter + 1) * HEAD_DIM] = one

    @pl.when(step == pl.num_programs(0) - 1)
    def _():
        for k, (src, dst) in enumerate(copies):
            pltpu.make_async_copy(src, dst, out_sem.at[k]).wait()


def project(tokens, cosine, sine, scalars, bufs, heads, kvs, prompt, deps, block=256):
    rows, width = tokens.shape
    blocks, shard = bufs[0].shape[:2]
    count = (heads + 2 * kvs) // 2 + 1
    head_spec = lambda n: pl.BlockSpec((n, block, HEAD_DIM), lambda i, s: (0, i, 0))
    outs = [
        sds((count, width, LANES), bf),
        sds((heads // 2, width, LANES), bf),
        sds((heads // 4, width, LANES), bf),
        sds((LANES, width), bf),
        sds((heads, rows, HEAD_DIM), bf),
        sds((2 * kvs, rows, HEAD_DIM), bf),
        sds((2 * kvs, prompt // 2, LANES), bf),
        sds((width, rows), bf),
    ]
    return call(
        functools.partial(qkv_kernel, shard, (heads, kvs, len(bufs))),
        "project",
        (rows // block,),
        [tokens, cosine, sine, *bufs],
        [rows_of(block, width), rows_of(block, LANES), rows_of(block, LANES)] + [any_space()] * len(bufs),
        outs,
        [
            any_space(),
            any_space(),
            any_space(),
            whole((LANES, width)),
            head_spec(heads),
            head_spec(2 * kvs),
            whole((2 * kvs, prompt // 2, LANES)),
            pl.BlockSpec((width, block), lambda i, s: (0, i)),
        ],
        [
            pltpu.VMEM((blocks, width, LANES), bf),
            pltpu.VMEM((LANES, width), bf),
            pltpu.SemaphoreType.DMA,
            pltpu.SemaphoreType.DMA((3,)),
        ],
        2 * rows * width * count * LANES,
        scalars,
        deps,
    )


def causal(scores):
    key = lax.broadcasted_iota(jnp.int32, scores.shape, 0)
    query = lax.broadcasted_iota(jnp.int32, scores.shape, 1)
    return jnp.where(key <= query, scores, masked_score)


def block_scores(query, keys, other_keys, at, block, prompt, bias):
    parts = []
    if at:
        parts.append(mm_nt(keys[0:at], query))
    parts.append(causal(mm_nt(keys[at : at + block], query)))
    other = mm_nt(other_keys, query)
    if at < prompt:
        other = other + bias
    parts.append(other)
    return parts


def unpack(ref):
    return jnp.concatenate([ref[0, :, :HEAD_DIM], ref[0, :, HEAD_DIM:]], axis=0)


def attend_kernel(cfg, sc, q, k0, k1, o0, o1, v0, v1, w0, w1, mixed, lse):
    starts, block, prompt = cfg
    bias = jnp.where(sc[0] == 0, masked_score, 0.0).astype(f32)
    for side, (keys, other, values, other_values) in enumerate(((k0, o0, v0, w0), (k1, o1, v1, w1))):
        values_t = values[0].T
        other_t = unpack(other_values).T
        other_keys = unpack(other)
        for a, at in enumerate(starts):
            rows = slice(a * block, a * block + block)
            scores = block_scores(q[side, rows, :], keys[0], other_keys, at, block, prompt, bias)
            peak = functools.reduce(jnp.maximum, [jnp.max(s, axis=0, keepdims=True) for s in scores])
            raw = [jnp.exp(s - peak) for s in scores]
            total = sum(jnp.sum(r, axis=0, keepdims=True) for r in raw)
            low = [r.astype(bf) for r in raw]
            out = mm(other_t, low[-1]) + mm(values_t[:, at : at + block], low[-2])
            if at:
                out = out + mm(values_t[:, 0:at], low[0])
            out = out * (1.0 / total)
            mixed[rows, side * HEAD_DIM : side * HEAD_DIM + HEAD_DIM] = out.T.astype(bf)
            lse[0, side : side + 1, rows] = peak + jnp.log(total)


def kv_specs(kvs, rows, prompt, rep, first_pair):
    index = lambda side, base: (lambda p, s: (base + (2 * (p + first_pair) + side) // rep, 0, 0))
    specs = []
    for base in (0, kvs):
        specs += [pl.BlockSpec((1, rows, HEAD_DIM), index(side, base)) for side in range(2)]
        specs += [pl.BlockSpec((1, prompt // 2, LANES), index(side, base)) for side in range(2)]
    return specs


def attend(q, kv, other, core, part, deps, block=256):
    heads, rows, _ = q.shape
    kvs, prompt = other.shape[0] // 2, 2 * other.shape[1]
    count = prompt if part == 0 else rows - prompt
    first = 0 if part == 0 else prompt
    starts = tuple(range(first, first + count, block))
    return call(
        functools.partial(attend_kernel, (starts, block, prompt)),
        "attend",
        (heads // 2,),
        [q, kv, kv, other, other, kv, kv, other, other],
        [pl.BlockSpec((2, count, HEAD_DIM), lambda p, s: (p, part, 0)), *kv_specs(kvs, rows, prompt, heads // kvs, 0)],
        [sds((count, heads * HEAD_DIM), bf), sds((heads // 2, 2, count), f32)],
        [
            pl.BlockSpec((count, LANES), lambda p, s: (0, p)),
            pl.BlockSpec((1, 2, count), lambda p, s: (p, 0, 0)),
        ],
        [],
        16 * heads * count * 1024 * HEAD_DIM,
        core,
        deps,
    )


def attend_back_kernel(cfg, sc, q, k0, k1, o0, o1, v0, v1, w0, w1, dout, mixed_a, mixed_b, lse_a, lse_b, cosine, sine, dq, dkv, dother_out, dother):
    rows_total, block, prompt, rep = cfg
    pair = pl.program_id(0)
    bias = jnp.where(sc[0] == 0, masked_score, 0.0).astype(f32)
    kvs = dkv.shape[0] // 2

    @pl.when(pair == 0)
    def _():
        dkv[...] = jnp.zeros_like(dkv)
        dother[...] = jnp.zeros_like(dother)

    heads = ((k0, unpack(o0), v0, unpack(w0)), (k1, unpack(o1), v1, unpack(w1)))
    keys_t = [(keys[0].T, other.T) for keys, other, _, _ in heads]
    for at in range(0, rows_total, block):
        rows = slice(at, at + block)
        mixed, lse, local = (mixed_a, lse_a, at) if at < prompt else (mixed_b, lse_b, at - prompt)
        inner = slice(local, local + block)
        dot = (dout[rows, :].astype(f32) * mixed[inner, :].astype(f32)).T
        grads = []
        for side, (keys, other, values, other_values) in enumerate(heads):
            head = (2 * pair + side) // rep
            query = q[side, rows, :]
            grad = dout[rows, side * HEAD_DIM : side * HEAD_DIM + HEAD_DIM]
            weighted = jnp.sum(dot[side * HEAD_DIM : side * HEAD_DIM + HEAD_DIM], axis=0, keepdims=True)
            norm = lse[0, side : side + 1, inner]
            scores = block_scores(query, keys[0], other, at, block, prompt, bias)
            spans = ([(False, 0, at)] if at else []) + [(False, at, block), (True, 0, prompt)]
            back = None
            for score, (is_other, first, size) in zip(scores, spans):
                probs = jnp.exp(score - norm)
                value = other_values if is_other else values[0, first : first + size]
                score_low = (probs * (mm_nt(value, grad) - weighted)).astype(bf)
                sums = dother if is_other else dkv
                span = pl.ds(first, size)
                sums[kvs + head, span, :] += mm(probs.astype(bf), grad)
                sums[head, span, :] += mm(score_low, query)
                key_t = keys_t[side][1] if is_other else keys_t[side][0][:, first : first + size]
                term = mm(key_t, score_low)
                back = term if back is None else back + term
            grads.append(back)
        both = jnp.concatenate(grads, axis=0).T * (1.0 / HEAD_DIM)
        dq[rows, :] = rope(both, cosine[rows, :], -sine[rows, :]).astype(bf)

    @pl.when(pair == pl.num_programs(0) - 1)
    def _():
        for h in range(dother.shape[0]):
            for quarter in range(2):
                part = dother[h, quarter * (prompt // 2) : (quarter + 1) * (prompt // 2), :]
                dother_out[h, :, quarter * HEAD_DIM : (quarter + 1) * HEAD_DIM] = part


def attend_back(q, kv, other, dout, mixed, lse, cosine, sine, core, part, parts, deps, block=256):
    heads, rows, _ = q.shape
    kvs, prompt = other.shape[0] // 2, 2 * other.shape[1]
    pairs = heads // 2 // parts
    first = part * pairs
    mine = 2 * kvs // parts
    pair = pl.BlockSpec((rows, LANES), lambda p, s: (0, p + first))
    mixed_spec = lambda a: pl.BlockSpec((a.shape[0], LANES), lambda p, s: (0, p + first))
    lse_spec = lambda a: pl.BlockSpec((1, 2, a.shape[2]), lambda p, s: (p + first, 0, 0))
    return call(
        functools.partial(attend_back_kernel, (rows, block, prompt, heads // kvs)),
        "attend_back",
        (pairs,),
        [q, kv, kv, other, other, kv, kv, other, other, dout, *mixed, *lse, cosine, sine],
        [
            pl.BlockSpec((2, rows, HEAD_DIM), lambda p, s: (p + first, 0, 0)),
            *kv_specs(kvs, rows, prompt, heads // kvs, first),
            pair,
            *[mixed_spec(a) for a in mixed],
            *[lse_spec(a) for a in lse],
            whole(cosine.shape),
            whole(sine.shape),
        ],
        [
            sds((rows, pairs * LANES), bf),
            sds((mine, rows, HEAD_DIM), f32),
            sds((mine, prompt // 2, LANES), f32),
        ],
        [
            pl.BlockSpec((rows, LANES), lambda p, s: (0, p)),
            whole((mine, rows, HEAD_DIM)),
            whole((mine, prompt // 2, LANES)),
        ],
        [pltpu.VMEM((mine, prompt, HEAD_DIM), f32)],
        40 * heads // parts * rows * 1024 * HEAD_DIM,
        core,
        deps,
    )


def load_halves(sc, mine, theirs, first_block, w, sem):
    half = mine.shape[0]
    pltpu.make_async_copy(mine, w.at[pl.ds(first_block + sc[0] * half, half)], sem).start()
    pltpu.make_async_copy(theirs, w.at[pl.ds(first_block + (1 - sc[0]) * half, half)], sem).start()


def settle_kernel(sc, tok, ids, own_a, own_b, far_a, far_b, extra, w_own, w_mine, w_theirs, res_out, n_out, nt_out, wt_out, w, sem):
    step = pl.program_id(0)
    blocks = w_own.shape[0]

    @pl.when(step == 0)
    def _():
        pltpu.make_async_copy(w_own, w.at[pl.ds(0, blocks)], sem).start()
        load_halves(sc, w_mine, w_theirs, blocks, w, sem)
        pltpu.make_async_copy(w, w, sem).wait()

    early = step < pl.num_programs(0) // 2
    own = jnp.where(early, own_a[...], own_b[...])
    far = jnp.where(early, far_a[...], far_b[...])
    branch = mm_nt(own, lanes_of(w, 0, blocks)) + mm_nt(far, lanes_of(w, blocks, blocks))
    residual = tok[...].astype(f32) + branch
    res_out[...] = residual
    scale = lax.rsqrt(jnp.mean(residual * residual, axis=-1, keepdims=True) + norm_eps)
    normed = (residual * scale * extra[1:2, :].astype(f32)).astype(bf)
    n_out[...] = normed
    nt_out[...] = normed.T
    logits = mm_nt(normed, extra[...])
    lane = lax.broadcasted_iota(jnp.int32, logits.shape, 1)
    routed = lane < 0
    for k in range(TOPK):
        routed = jnp.logical_or(routed, lane == ids[:, k : k + 1] + ROUTER_LANE)
    logits = jnp.where(routed, logits, masked_score)
    raw = jnp.where(routed, jnp.exp(logits - jnp.max(logits, axis=-1, keepdims=True)), 0.0)
    wt_out[...] = raw / jnp.sum(raw, axis=-1, keepdims=True)


def settle(tokens, ids, own, far, extra, w_own, w_mine, w_theirs, core, deps, block=256):
    rows, width = tokens.shape
    halves = rows // block // 2
    cols = own[0].shape[1]
    low = pl.BlockSpec((block, cols), lambda i, s: (jnp.minimum(i, halves - 1), 0))
    high = pl.BlockSpec((block, cols), lambda i, s: (jnp.maximum(i - halves, 0), 0))
    return call(
        settle_kernel,
        "settle",
        (rows // block,),
        [tokens, ids, *own, *far, extra, w_own, w_mine, w_theirs],
        [rows_of(block, width), rows_of(block, TOPK), low, high, low, high, whole(extra.shape)] + [any_space()] * 3,
        [sds((rows, width), f32), sds((rows, width), bf), sds((width, rows), bf)] + [sds((rows, LANES), f32)],
        [rows_of(block, width), rows_of(block, width), pl.BlockSpec((width, block), lambda i, s: (0, i))]
        + [rows_of(block, LANES)],
        [pltpu.VMEM((2 * w_own.shape[0], width, LANES), bf), pltpu.SemaphoreType.DMA],
        4 * rows * width * cols,
        core,
        deps,
    )


def mix_halves(core, kept, sent):
    first = jnp.concatenate([kept[0], sent[0]], axis=-1)
    second = jnp.concatenate([kept[1], sent[1]], axis=-1)
    return jnp.where(core == 0, first, second), jnp.where(core == 0, second, first)


PARTS = ((3, 1), (2, 2))


def fetch_weights(sc, bufs, w, kinds, local, shard, hidden, sem):
    hops = len(bufs) // 2
    core = sc[len(bufs)]
    for k, buf in enumerate(bufs):
        rows = pl.ds(pl.multiple_of(sc[k] * shard, shard), shard)
        target = w.at[kinds, :, rows, :]
        if k in (hops, 2 * hops):
            at = core if k == hops else 1 - core
            target = w.at[kinds, :, rows, pl.ds(pl.multiple_of(at * (hidden // 2), LANES), hidden // 2)]
        pltpu.make_async_copy(buf.at[kinds, pl.ds(local, 2)], target, sem).start()


def both(w, kind):
    return jnp.concatenate([w[kind, 0], w[kind, 1]], axis=1)


def activate(ids, hidden, rows, x, grad_rows, w, wt, pick_in, pick, scaled, acts):
    lane = lax.broadcasted_iota(jnp.int32, (x.shape[0], LANES), 1)
    gate = mm(x, both(w, 0))
    up = mm(x, both(w, 1))
    grad = mm(grad_rows, both(w, 2))
    table = wt[rows, :]
    sig = 1.0 / (1.0 + jnp.exp(-gate))
    silu = gate * sig
    act = silu * up
    dots = act * grad
    picked = jnp.zeros(table.shape, f32) if pick_in is None else pick_in[rows, :]
    for side, expert in enumerate(ids):
        cols = slice(side * hidden, side * hidden + hidden)
        weight = jnp.sum(jnp.where(lane == expert, table, 0.0), axis=1, keepdims=True)
        picked = picked + jnp.where(lane == expert, jnp.sum(dots[:, cols], axis=1, keepdims=True), 0.0)
        scaled[rows, cols] = (act[:, cols] * weight).astype(bf)
        g = grad[:, cols] * weight
        s = sig[:, cols]
        acts[rows, cols] = (g * up[:, cols] * s * (1.0 + gate[:, cols] * (1.0 - s))).astype(bf)
        acts[rows, slice((2 + side) * hidden, (3 + side) * hidden)] = (g * silu[:, cols]).astype(bf)
    pick[rows, :] = picked
    return picked


def pair_grads(sc, total, shard, hidden, xt, ct, scaled, acts, keep_s, send_s, keep, send, g_sem):
    core, ranks, slots = sc[total], total + 1, total // 2
    for slot in range(slots):
        at = [pl.ds(pl.multiple_of(sc[ranks + slots * k + slot] * shard, shard), shard) for k in range(2)]
        left = lambda ref: jnp.concatenate([ref[at[0], :], ref[at[1], :]], axis=0)
        gate_up = mm(left(xt), acts[...]).astype(bf)
        down = mm(left(ct), scaled[...]).astype(bf)
        kinds = (gate_up[:, : 2 * hidden], gate_up[:, 2 * hidden :], down)
        for kind, made in enumerate(kinds):
            for side in range(2):
                part = made[:, side * hidden : side * hidden + hidden]
                kept, sent_part = part[:shard], part[shard:]
                if slot == slots - 1:
                    cut = lambda a: (a[:, : hidden // 2], a[:, hidden // 2 :])
                    kept, sent_part = mix_halves(core, cut(kept), cut(sent_part))
                keep_s[slot, side * 3 + kind] = kept
                send_s[slot, side * 3 + kind] = sent_part
        pltpu.make_async_copy(keep_s.at[slot], keep.at[slot], g_sem.at[0]).start()
        pltpu.make_async_copy(send_s.at[slot], send.at[slot], g_sem.at[1]).start()


def experts_kernel(cfg, sc, *refs):
    shard, hidden, local, first, mode, total = cfg
    block = 256
    it = iter(refs)
    front, rest, ends = mode.startswith("front"), mode.startswith("rest"), mode.endswith("_end")
    n2, cot, wt = (None, None, None) if rest else (next(it), next(it), next(it))
    n2t, cott = (None, None) if front else (next(it), next(it))
    bufs = [next(it) for _ in range(total)]
    moe_in = None if first or front else next(it)
    back_in, pick_in = (None, None) if first or rest else (next(it), next(it))
    scaled_in, acts_in = (next(it), next(it)) if rest else (None, None)
    take_out = lambda: tuple(next(it) for _ in range(len(PARTS[front]) if ends else 1))
    moe_out = None if front else take_out()
    back_out = None if rest else take_out()
    keep, send = (None, None) if front else (next(it), next(it))
    pick = None if rest else next(it)
    scaled_out, acts_out = (next(it), next(it)) if front else (None, None)
    pick_t = next(it) if front and ends else None
    w, scaled, acts, w_sem, in_sem, out_sem = (next(it) for _ in range(6))
    moe = None if front else next(it)
    back = None if rest else next(it)
    xs, cs, x_sem, c_sem = (None,) * 4 if rest else (next(it) for _ in range(4))
    xt, ct, keep_s, send_s, t_sem, g_sem = (None,) * 6 if front else (next(it) for _ in range(6))
    low = next(it) if ends else None
    rows_total = scaled.shape[0]
    spans = [pl.ds(at, block) for at in range(0, rows_total, block)]
    ids = [sc[total + 1 + 2 * (total // 2) + side] + ROUTER_LANE for side in range(2)]

    loads = (pl.ds(0, block), pl.ds(block, rows_total - block))

    def row_copies(i):
        return [
            pltpu.make_async_copy(n2.at[loads[i]], xs.at[loads[i]], x_sem.at[i]),
            pltpu.make_async_copy(cot.at[loads[i]], cs.at[loads[i]], c_sem.at[i]),
        ]

    def load_wide():
        for k, (src, dst) in enumerate(((moe_in, moe), (back_in, back))):
            if src is not None:
                pltpu.make_async_copy(src, dst, in_sem.at[k]).start()
        if not front:
            pltpu.make_async_copy(n2t, xt, t_sem.at[0]).start()
            pltpu.make_async_copy(cott, ct, t_sem.at[1]).start()

    kinds = pl.ds(2, 1) if rest else pl.ds(0, 3)
    fetch_weights(sc, bufs, w, kinds, local, shard, hidden, w_sem)
    if rest:
        pltpu.make_async_copy(scaled_in, scaled, out_sem.at[2]).start()
        load_wide()
        pltpu.make_async_copy(acts_in, acts, out_sem.at[3]).start()
        pltpu.make_async_copy(w.at[kinds], w.at[kinds], w_sem).wait()
        pltpu.make_async_copy(scaled_in, scaled, out_sem.at[2]).wait()
    else:
        for copy in row_copies(0) + row_copies(1):
            copy.start()
        pltpu.make_async_copy(w.at[kinds], w.at[kinds], w_sem).wait()
        for i, rows in enumerate(spans):
            for copy in row_copies(i) if i < 2 else ():
                copy.wait()
            if i == 1:
                load_wide()
            picked = activate(ids, hidden, rows, xs[rows, :], cs[rows, :], w, wt, pick_in, pick, scaled, acts)
            if pick_t is not None:
                pick_t[:, rows] = picked.T[ROUTER_LANE : ROUTER_LANE + EXPERTS]

    for k, (src, dst) in enumerate(((moe_in, moe), (back_in, back))):
        if src is not None:
            pltpu.make_async_copy(src, dst, in_sem.at[k]).wait()
    outs = []
    if not front:
        outs.append((moe, moe_out, 0, lambda rows: mm_nt(scaled[rows, :], both(w, 2))))
    if not rest:
        two = lambda rows: mm_nt(acts[rows, 0 : 2 * hidden], both(w, 0)) + mm_nt(acts[rows, 2 * hidden :], both(w, 1))
        outs.append((back, back_out, 1, two))
    for i, rows in enumerate(spans):
        for acc, halves, k, make in outs:
            made = make(rows) + acc[rows, :]
            scr = acc if low is None else low
            scr[rows, :] = made.astype(scr.dtype)
            part, at = 0, i
            while len(halves) > 1 and at >= PARTS[front][part]:
                part, at = part + 1, at - PARTS[front][part]
            to = halves[part].at[pl.ds(at * block, block)]
            pltpu.make_async_copy(scr.at[rows], to, out_sem.at[k]).start()
    if front:
        pltpu.make_async_copy(scaled, scaled_out, out_sem.at[2]).start()
        pltpu.make_async_copy(acts, acts_out, out_sem.at[3]).start()
    else:
        pltpu.make_async_copy(n2t, xt, t_sem.at[0]).wait()
        pltpu.make_async_copy(cott, ct, t_sem.at[1]).wait()
        if rest:
            pltpu.make_async_copy(acts_in, acts, out_sem.at[3]).wait()
        pair_grads(sc, total, shard, hidden, xt, ct, scaled, acts, keep_s, send_s, keep, send, g_sem)
    for acc, _, k, _ in outs:
        scr = acc if low is None else low
        pltpu.make_async_copy(scr, scr, out_sem.at[k]).wait()
    if front:
        pltpu.make_async_copy(scaled, scaled_out, out_sem.at[2]).wait()
        pltpu.make_async_copy(acts, acts_out, out_sem.at[3]).wait()
    else:
        pltpu.make_async_copy(keep_s, keep, g_sem.at[0]).wait()
        pltpu.make_async_copy(send_s, send, g_sem.at[1]).wait()


def experts(mode, dense, turned, wt, scalars, bufs, local, moe_in, back_in, pick_in, made, deps):
    width, rows = turned[0].shape
    shard, hidden = bufs[0].shape[2:]
    slots = len(bufs) // 2
    front, rest, ends = mode.startswith("front"), mode.startswith("rest"), mode.endswith("_end")
    first = False
    hbm, table = any_space(), whole((rows, LANES))
    ins, specs, outs, out_specs = [], [], [], []

    def put(arrays, spec):
        ins.extend(arrays)
        specs.extend([spec] * len(arrays))

    def give(shape, kind, spec=None):
        outs.append(sds(shape, kind))
        out_specs.append(spec or any_space())

    if not rest:
        put(dense, hbm)
        put([wt], table)
    if not front:
        put(turned, hbm)
    put(bufs, hbm)
    if not first and not front:
        put([moe_in], hbm)
    if not first and not rest:
        put([back_in], hbm)
        put([pick_in], table)
    if rest:
        put(made, hbm)
    pieces = [(256 * p, width) for p in PARTS[front]] if ends else [(rows, width)]
    for shape in pieces * (2 if mode == "all" else 1):
        give(shape, bf if ends else f32)
    if not front:
        give((slots, 6, shard, hidden), bf)
        give((slots, 6, shard, hidden), bf)
    if not rest:
        give((rows, LANES), f32, table)
    if front:
        give((rows, 2 * hidden), bf)
        give((rows, 4 * hidden), bf)
    if front and ends:
        give((EXPERTS, rows), f32, whole((EXPERTS, rows)))
    dma = pltpu.SemaphoreType.DMA
    scratch = [
        pltpu.VMEM((3, 2, width, hidden), bf),
        pltpu.VMEM((rows, 2 * hidden), bf),
        pltpu.VMEM((rows, 4 * hidden), bf),
        dma,
        dma((2,)),
        dma((4,)),
    ]
    scratch += [pltpu.VMEM((rows, width), f32)] * (2 if mode == "all" else 1)
    if not rest:
        scratch += [pltpu.VMEM((rows, width), bf)] * 2 + [dma((2,))] * 2
    if not front:
        scratch += [pltpu.VMEM((width, rows), bf)] * 2 + [pltpu.VMEM((slots, 6, shard, hidden), bf)] * 2 + [dma((2,))] * 2
    if ends:
        scratch.append(pltpu.VMEM((rows, width), bf))
    return call(
        functools.partial(experts_kernel, (shard, hidden, local, first, mode, len(bufs))),
        "experts_" + mode,
        (1,),
        ins,
        specs,
        outs,
        out_specs,
        scratch,
        36 * rows * width * hidden,
        scalars,
        deps,
    )


def hop_kernel(cfg, sc, *refs):
    pairs, stage, core_at = cfg
    core = sc[core_at]
    it = iter(refs)
    keeps = [next(it) for _ in range(pairs)]
    gots = [next(it) for _ in range(pairs)]
    came = next(it) if stage else None
    out = next(it)
    for p in range(pairs):
        total = keeps[p][0].astype(f32) + gots[p][0].astype(f32)
        if stage == "end":
            total = place_half(total, core, 2) + came[p].astype(f32)
        elif stage == "second":
            total = total + place_half(came[p].astype(f32), core, 2)
        elif stage:
            total = total + came[p].astype(f32)
        out[p] = total.astype(bf)


def hop_sum(keeps, gots, came, slot, stage, scalars, core_at, deps=()):
    pairs = len(keeps)
    slots, mats, shard, hidden = keeps[0].shape
    lanes = hidden // 2 if stage in (None, "end") else hidden
    side = 1 if stage == "end" else 0
    per = mats // 2 if pairs > 1 else mats
    piece = pl.BlockSpec((1, per, shard, lanes), lambda m, s: (slot, m, 0, side))
    wide = lambda a: pl.BlockSpec((pairs, per, shard, a.shape[3]), lambda m, s: (0, m, 0, 0))
    out = sds((pairs, mats, shard, hidden // 2 if stage is None else hidden), bf)
    ins = [*keeps, *gots] + ([] if came is None else [came])
    specs = [piece] * (2 * pairs) + ([] if came is None else [wide(came)])
    kernel = functools.partial(hop_kernel, (pairs, stage, core_at))
    return call(kernel, "hop_sum", (mats // per,), ins, specs, [out], [wide(out)], [], 0, scalars, deps)[0]


def emit_kernel(sc, mine, theirs, *refs):
    for m in range(6):
        refs[m % 3 - 3][m // 3] = mine[0, m].astype(f32) + theirs[0, m].astype(f32)


def emit(group, first, total, into, core, deps):
    pairs, mats, shard, hidden = group[0].shape
    ins = [*group, *(into or [])]
    spec = pl.BlockSpec((1, mats, shard, hidden), lambda i, s: (i, 0, 0, 0))
    out_spec = pl.BlockSpec((2, shard, hidden), lambda i, s: (i + first // 2, 0, 0))
    outs = [sds((total, shard, hidden), f32)] * 3
    aliases = {1 + len(deps) + 2 + k: k for k in range(3)} if into else {}
    specs = [spec, spec] + [any_space()] * (len(ins) - 2)
    return call(emit_kernel, "emit", (pairs,), ins, specs, outs, [out_spec] * 3, [], 0, core, deps, aliases=aliases)


def norm_back(values, gain, grad):
    scale = lax.rsqrt(jnp.mean(values * values, axis=-1, keepdims=True) + norm_eps)
    inner = jnp.mean(values * gain * grad, axis=-1, keepdims=True)
    passed = scale * gain * grad - values * (scale * scale * scale * inner)
    return passed, jnp.sum(grad * values * scale, axis=0, keepdims=True)


def pick_part(refs, parts):
    step = pl.program_id(0)
    value, at = refs[0][...], 0
    for ref, size in zip(refs, parts):
        value = jnp.where(step >= at, ref[...], value)
        at += size
    return value


def part_specs(block, parts):
    specs, first = [], 0
    for p in parts:
        per = p.shape[0] // block
        specs.append(pl.BlockSpec((block, p.shape[1]), lambda i, s, first=first, per=per: (jnp.clip(i - first, 0, per - 1), 0)))
        first += per
    return specs


def combine_kernel(sc, res, *refs):
    count = len(refs) // 2
    total = pick_part(refs[:count], PARTS[0]).astype(f32) + pick_part(refs[count : 2 * count], PARTS[0]).astype(f32)
    refs[-1][...] = (res[...] + total).astype(bf)


def combine(res, own, far, core, deps, block=256):
    rows, width = res.shape
    specs = [rows_of(block, width)] + part_specs(block, own) + part_specs(block, far)
    out = sds((rows, width), bf)
    return call(combine_kernel, "combine", (rows // block,), [res, *own, *far], specs, [out], [rows_of(block, width)], [], 0, core, deps)[0]


def unsettle_kernel(sc, *refs):
    count = len(PARTS[1])
    own, far, refs = refs[:count], refs[count : 2 * count], refs[2 * count :]
    unsettle_rows(own, far, *refs)


def unsettle_rows(own, far, pick_a, pick_b, wt, res, cot, extra, w_own, rg_out, low_t_out, dout_out, ll_out, gain_out, w, sem):
    step = pl.program_id(0)

    @pl.when(step == 0)
    def _():
        pltpu.make_async_copy(w_own, w, sem).start()
        pltpu.make_async_copy(w_own, w, sem).wait()
        gain_out[...] = jnp.zeros_like(gain_out)

    weights = wt[...]
    picked = pick_a[...] + pick_b[...]
    room = lambda n: jnp.zeros((n, picked.shape[1]), f32)
    picked = jnp.concatenate([room(ROUTER_LANE), picked, room(LANES - ROUTER_LANE - EXPERTS)], axis=0).T
    logit_low = (weights * (picked - jnp.sum(weights * picked, axis=-1, keepdims=True))).astype(bf)
    ll_out[...] = logit_low
    grad = pick_part(own, PARTS[1]).astype(f32) + pick_part(far, PARTS[1]).astype(f32) + mm(logit_low, extra[...])
    passed, gain = norm_back(res[...], extra[1:2, :].astype(f32), grad)
    gain_out[...] += gain
    total = cot[...].astype(f32) + passed
    rg_out[...] = total
    low = total.astype(bf)
    low_t_out[...] = low.T
    dout_out[...] = mm(low, lanes_of(w, 0, w.shape[0])).astype(bf)


def unsettle(back, far, picks, wt, res, cot, extra, w_own, core, deps, block=256):
    rows, width = res.shape
    cols = w_own.shape[0] * LANES
    wide, thin = rows_of(block, width), rows_of(block, LANES)
    across = pl.BlockSpec((EXPERTS, block), lambda i, s: (0, i))
    return call(
        unsettle_kernel,
        "unsettle",
        (rows // block,),
        [*back, *far, *picks, wt, res, cot, extra, w_own],
        [*part_specs(block, back), *part_specs(block, far), across, across, thin, wide, wide, whole(extra.shape), any_space()],
        [sds((rows, width), f32), sds((width, rows), bf), sds((rows, cols), bf), sds((rows, LANES), bf), sds((1, width), f32)],
        [wide, pl.BlockSpec((width, block), lambda i, s: (0, i)), rows_of(block, cols), thin, whole((1, width))],
        [pltpu.VMEM(w_own.shape, bf), pltpu.SemaphoreType.DMA],
        2 * rows * width * cols,
        core,
        deps,
    )


def scaled_sum(weights, grads, gain):
    return jnp.sum(weights.astype(f32) * grads, axis=1, keepdims=True) / gain.astype(f32)


def leave(parts, core, shard, keep, send):
    last = pl.program_id(0) == pl.num_programs(0) - 1
    cut = lambda a: (a[:, :LANES], a[:, LANES:])

    @pl.when(jnp.logical_not(last))
    def _():
        for b, part in enumerate(parts):
            keep[0, b] = part[:shard]
            send[0, b] = part[shard:]

    @pl.when(last)
    def _():
        for b, part in enumerate(parts):
            keep[0, b], send[0, b] = mix_halves(core, cut(part[:shard]), cut(part[shard:]))


def early_grads_kernel(core_at, sc, low_a, low_b, mixed_a, mixed_b, n2_a, n2_b, ll, col_a, col_b, n1_a, n1_b, dq, w_a, w_b, keep, send):
    prompt = mixed_a.shape[0]
    shard = low_a.shape[0]
    join = lambda a, b: jnp.concatenate([a[...], b[...]], axis=0)
    tall = join(low_a, low_b)
    made = mm(tall[:, 0:prompt], mixed_a[...]) + mm(tall[:, prompt:], mixed_b[...])
    query = mm(join(n1_a, n1_b), dq[...])
    blocks = dq.shape[1] // LANES
    weights = jnp.concatenate([lanes_of(ref, 0, blocks) for ref in (w_a, w_b)], axis=0)
    gains = jnp.concatenate([ref[ref.shape[0] - 1, :, 0:1] for ref in (w_a, w_b)], axis=0)
    first = scaled_sum(weights, query, gains)
    extra = mm(join(n2_a, n2_b), ll[...]) + join(col_a, col_b)
    lane = lax.broadcasted_iota(jnp.int32, extra.shape, 1)
    extra = jnp.where(lane == 0, first, extra)
    whole_row = jnp.concatenate([made, query, extra], axis=1).astype(bf)
    wide = 2 * LANES
    leave([whole_row[:, b * wide : (b + 1) * wide] for b in range(whole_row.shape[1] // wide)], sc[core_at], shard, keep, send)


def early_grads(low_t, mixed, n2t, ll, column, n1t, dq, w, scalars, first_rank, core_at, shard, deps):
    width, rows = low_t.shape
    slots = (scalars.shape[0] - first_rank) // 2
    cols = mixed[0].shape[1] + LANES + dq.shape[1]
    at = lambda k: (lambda i, s: (s[first_rank + k * slots + i], 0))
    w_at = lambda k: (lambda i, s: (0, s[first_rank + k * slots + i], 0))
    two = lambda lanes: [pl.BlockSpec((shard, lanes), at(k)) for k in range(2)]
    out = sds((slots, cols // (2 * LANES), shard, 2 * LANES), bf)
    out_spec = pl.BlockSpec((1, *out.shape[1:]), lambda i, s: (i, 0, 0, 0))
    return call(
        functools.partial(early_grads_kernel, core_at),
        "early_grads",
        (slots,),
        [low_t, low_t, *mixed, n2t, n2t, ll, column, column, n1t, n1t, dq, w, w],
        two(rows)
        + [whole(a.shape) for a in mixed]
        + two(rows)
        + [whole(ll.shape)]
        + two(LANES)
        + two(rows)
        + [whole(dq.shape)]
        + [pl.BlockSpec((w.shape[0], shard, LANES), w_at(k)) for k in range(2)],
        [out, out],
        [out_spec, out_spec],
        [],
        2 * rows * width * cols,
        scalars,
        deps,
    )


def late_grads_kernel(cfg, sc, left_a, left_b, dq, low_kv, w_a, w_b, keep, send):
    core_at, first_block, count = cfg
    core = sc[core_at]
    shard = left_a.shape[0]
    tall = jnp.concatenate([left_a[...], left_b[...]], axis=0)
    made = jnp.concatenate([mm(tall, dq[...]), mm(tall, low_kv[...])], axis=1)
    blocks = made.shape[1] // LANES
    weights = jnp.concatenate([lanes_of(ref, first_block, blocks) for ref in (w_a, w_b)], axis=0)
    gains = jnp.concatenate([ref[ref.shape[0] - 1, :, 0:1] for ref in (w_a, w_b)], axis=0)
    first = scaled_sum(weights, made, gains)
    lane = lax.broadcasted_iota(jnp.int32, (2 * shard, LANES), 1)
    made = jnp.concatenate([made, jnp.where(lane == 0, first, 0.0)], axis=1).astype(bf)
    wide = 2 * LANES
    leave([made[:, b * wide : (b + 1) * wide] for b in range(count)], core, shard, keep, send)


def late_grads(left, dq, low_kv, w, first_block, scalars, first_rank, core_at, shard, deps):
    width, rows = left.shape
    slots = (scalars.shape[0] - first_rank) // 2
    count = (dq.shape[1] + low_kv.shape[1] + LANES) // (2 * LANES)
    at = lambda k: (lambda i, s: (s[first_rank + k * slots + i], 0))
    w_at = lambda k: (lambda i, s: (0, s[first_rank + k * slots + i], 0))
    out = sds((slots, count, shard, 2 * LANES), bf)
    out_spec = pl.BlockSpec((1, count, shard, 2 * LANES), lambda i, s: (i, 0, 0, 0))
    return call(
        functools.partial(late_grads_kernel, (core_at, first_block, count)),
        "late_grads",
        (slots,),
        [left, left, dq, low_kv, w, w],
        [pl.BlockSpec((shard, rows), at(k)) for k in range(2)]
        + [whole(dq.shape), whole(low_kv.shape)]
        + [pl.BlockSpec((w.shape[0], shard, LANES), w_at(k)) for k in range(2)],
        [out, out],
        [out_spec, out_spec],
        [],
        4 * rows * width * count * LANES,
        scalars,
        deps,
    )


def spread_kernel(sc, early_a, early_b, late_a, late_b, output, query, key, value, extra):
    join = lambda a, b: jnp.concatenate([a[0, k].astype(f32) + b[0, k].astype(f32) for k in range(a.shape[1])], axis=1)
    early, late = join(early_a, early_b), join(late_a, late_b)
    cols = output.shape[1]
    output[...] = early[:, 0:cols]
    half = early.shape[1] - cols - LANES
    query[:, 0:half] = early[:, cols : cols + half]
    at = query.shape[1] - half
    query[:, half:] = late[:, 0:at]
    for out in (key, value):
        out[...] = late[:, at : at + out.shape[1]]
        at += out.shape[1]
    extra[...] = jnp.concatenate([early[:, cols + half :], late[:, at : at + LANES]], axis=1)


def spread(early, late, widths, core):
    shard = early[0].shape[2]
    outs = [sds((shard, size), f32) for size in (*widths, 2 * LANES)]
    ins = [*early, *late]
    return call(spread_kernel, "spread", (1,), ins, [whole(a.shape) for a in ins], outs, [whole(o.shape) for o in outs], [], 0, core)


def key_value_grads_kernel(sc, cosine, sine, *refs):
    *ins, out = refs
    parts = len(ins) // 2
    sums, mores = ins[:parts], ins[parts:]
    step = pl.program_id(0)
    shared = jnp.where(step < pl.num_programs(0) // 2, 1.0, 0.0).astype(f32)
    at = 0
    for is_key in (True, False):
        for own, more in zip(sums, mores):
            kvs = own.shape[0] // 2
            for kv in range(0, kvs, 2):
                heads = [kv + k + (0 if is_key else kvs) for k in range(2)]
                other = [jnp.where(step == 0, more[h, :, :HEAD_DIM], more[h, :, HEAD_DIM:]) for h in heads]
                pair = jnp.concatenate([own[h] + o * shared for h, o in zip(heads, other)], axis=1)
                if is_key:
                    pair = rope(pair, cosine[...], -sine[...])
                out[:, at : at + LANES] = pair.astype(bf)
                at += LANES


def key_value_grads(cosine, sine, sums, mores, core, deps, block=256):
    rows = cosine.shape[0]
    cols = sum(s.shape[0] for s in sums) * HEAD_DIM
    own = lambda a: pl.BlockSpec((a.shape[0], block, HEAD_DIM), lambda i, s: (0, i, 0))
    return call(
        key_value_grads_kernel,
        "key_value_grads",
        (rows // block,),
        [cosine, sine, *sums, *mores],
        [rows_of(block, LANES), rows_of(block, LANES)] + [own(a) for a in sums] + [whole(a.shape) for a in mores],
        [sds((rows, cols), bf)],
        [rows_of(block, cols)],
        [],
        0,
        core,
        deps,
    )[0]


def finish_kernel(sc, tok, extra, rg, *refs):
    *lows, w_own, mine_a, mine_b, theirs_a, theirs_b, out, w, sem = refs
    blocks = w.shape[0] // 2

    @pl.when(pl.program_id(0) == 0)
    def _():
        pltpu.make_async_copy(w_own.at[pl.ds(0, blocks)], w.at[pl.ds(0, blocks)], sem).start()
        for core, pieces in ((sc[0], (mine_a, mine_b)), (1 - sc[0], (theirs_a, theirs_b))):
            at = blocks + core * (blocks // 2)
            for piece in pieces:
                pltpu.make_async_copy(piece, w.at[pl.ds(at, piece.shape[0])], sem).start()
                at = at + piece.shape[0]
        pltpu.make_async_copy(w, w, sem).wait()

    low = jnp.concatenate([f[...] for f in lows], axis=1)
    grad = mm_nt(low, lanes_of(w, 0, 2 * blocks))
    passed, _ = norm_back(tok[...].astype(f32), extra[0:1, :].astype(f32), grad)
    out[...] = rg[...] + passed


def finish(tokens, extra, rg, lows, w_own, w_mine, w_theirs, core, deps, block=256):
    rows, width = tokens.shape
    wide = rows_of(block, width)
    blocks = 4 * sum(p.shape[0] for p in w_mine)
    return call(
        finish_kernel,
        "finish",
        (rows // block,),
        [tokens, extra, rg, *lows, w_own, *w_mine, *w_theirs],
        [wide, whole(extra.shape), wide, *[rows_of(block, f.shape[1]) for f in lows]] + [any_space()] * 5,
        [sds((rows, width), f32)],
        [wide],
        [pltpu.VMEM((blocks, width, LANES), bf), pltpu.SemaphoreType.DMA],
        2 * rows * width * blocks * LANES,
        core,
        deps,
    )[0]


def body(
    tokens,
    routes,
    cotangent,
    norm_one,
    w_query,
    key_weight,
    value_weight,
    w_output,
    norm_two,
    w_router,
    w_gate,
    w_up,
    w_down,
):
    window.turn()
    window.turn()
    window.gated = False
    count = lax.axis_size("dp")
    core = lax.axis_index("ctx")
    place = ring_place(lax.axis_index("dp"), count)
    rows, width = tokens.shape[2:]
    prompt = PROMPT_TOKENS // lax.axis_size("ctx")
    heads = w_query.shape[1] // HEAD_DIM
    kvs = key_weight.shape[1] // HEAD_DIM
    shard, hidden = w_gate.shape[1:]
    core_only = jnp.stack([core, core]).astype(jnp.int32)
    ranks = gather_sources(place, core, count)
    slots = scatter_sources(place, core, count)
    first_rank, core_at = len(ranks) + 1, len(ranks)

    def scalars(*more):
        return jnp.stack([*ranks, core, *slots, *more]).astype(jnp.int32)

    plain = scalars()
    tok = tokens.reshape(rows, width)
    cot = cotangent.reshape(rows, width)
    ids = routes.reshape(rows, TOPK)

    packed = pack(w_query, key_weight, value_weight, w_output, w_router, norm_one, norm_two, core_only)
    firsts = Gather(packed, core, count, 0)
    firsts.step()
    firsts.step()

    sizes = [4, 4, 4, 4]
    starts = [sum(sizes[:k]) for k in range(len(sizes))]
    chunks = []

    owns = [jnp.stack([w[at : at + size] for w in (w_gate, w_up, w_down)], axis=0) for at, size in zip(starts, sizes)]

    def open_chunk(*held):
        chunks.append(Gather(after(owns[len(chunks)], *held), core, count, 3))

    offsets = jnp.arange(rows, dtype=jnp.int32)
    positions = jnp.where(offsets < prompt, core * prompt + offsets, PROMPT_TOKENS + offsets - prompt)
    half_dim = HEAD_DIM // 2
    inverse = rope_base ** (-2.0 * jnp.arange(half_dim).astype(f32) / HEAD_DIM)
    angles = positions.astype(f32)[:, None] * inverse
    cosine = jnp.tile(jnp.cos(angles), (1, LANES // half_dim))
    sine = jnp.sin(angles)
    sine = jnp.tile(jnp.concatenate([-sine, sine], axis=1), (1, LANES // HEAD_DIM))
    cott = cot.T
    zero_wide, zero_table = jnp.zeros((rows, width), f32), jnp.zeros((rows, LANES), f32)

    firsts.mine[-1], cott, zero_wide, zero_table, cosine, sine, *owns = lax.optimization_barrier(
        (firsts.mine[-1], cott, zero_wide, zero_table, cosine, sine, *owns)
    )
    firsts.step()
    firsts.step()
    firsts.share()
    open_chunk(firsts.mine[-1])
    c0 = chunks[0]
    window.turn()
    window.turn()
    c0.step()
    w_first, w_out, w_out_half, extra, q, kv, kv_prompt, n1t = project(
        tok, cosine, sine, plain, firsts.bufs, heads, kvs, prompt, window.turn()
    )
    other = swap(kv_prompt, "ctx")
    out_far_mine = swap(after(w_out_half, kv_prompt), "tp")
    c0.step(kv_prompt)
    mixed_b, lse_b = attend(q, kv, other, core_only, 1, window.turn())
    far_b = swap(mixed_b, "tp")
    c0.step(lse_b)
    open_chunk(lse_b)
    c1 = chunks[1]
    c1.step()
    out_far_theirs = swap(after(out_far_mine, lse_b), "ctx")
    mixed_a, lse_a = attend(q, kv, other, core_only, 0, window.turn())
    far_a = swap(mixed_a, "tp")
    c0.step(lse_a)
    c1.step(lse_a)
    mixed, lse = (mixed_a, mixed_b), (lse_a, lse_b)
    res, n2, n2t, wt = settle(
        tok, ids, mixed, (far_a, far_b), extra, w_out, out_far_mine, out_far_theirs, core_only, [cott, zero_wide, *window.turn()]
    )
    scatters = [Scatter(core, count, plain, core_at) for _ in range(3)]
    state = dict(moe=zero_wide, back=zero_wide, pick=zero_table)

    def work(pair, mode="all", deps=None):
        at = 2 * pair
        k = max(k for k in range(len(starts)) if starts[k] <= at)
        sc = scalars(jnp.int32(at), jnp.int32(at + 1))
        bufs, local = chunks[k].bufs, at - starts[k]
        made = experts(
            mode, (n2, cot), (n2t, cott), wt, sc, bufs, local, state["moe"], state["back"], state["pick"], state.get("made"),
            window.turn() if deps is None else deps,
        )
        if mode == "all":
            state["moe"], state["back"], keep, send, state["pick"] = made
            return keep, send, state["pick"]
        if mode.startswith("front"):
            *back, state["pick"], scaled, acts = made[:-1] if mode.endswith("_end") else made
            state["back"] = back if mode.endswith("_end") else back[0]
            state["made"] = [scaled, acts]
            return made[-1]
        *moe, keep, send = made
        state["moe"] = moe if mode.endswith("_end") else moe[0]
        return keep, send, moe[0]

    s0, s1, s2 = scatters
    c0.share(wt)
    c1.step(wt)
    open_chunk(wt)
    c2 = chunks[2]
    c2.step()
    keep, send, token = work(0)

    s0.add(keep, send)
    c1.step(token)
    c2.step(token)
    first_part = w_first.shape[0] // 2
    split = (first_part + 1) // 2
    first_half = take(after(w_first, token), core * first_part, first_part)
    first_far_a = swap(first_half[:split], "tp")
    keep, send, token = work(1)

    s0.add(keep, send)
    c1.share(token)
    c2.step(token)
    open_chunk(token)
    c3 = chunks[3]
    c3.step()
    keep, send, token = work(2)

    s0.add(keep, send)
    c2.step(token)
    c3.step(token)
    keep, send, token = work(3)

    s1.add(keep, send)
    c2.share(token)
    c3.step(token)
    s0.step([token])
    keep, send, token = work(4)

    s1.add(keep, send)
    c3.step(token)
    s0.step([token])
    first_far_b = swap(after(first_half[split:], token), "tp")
    keep, send, token = work(5)

    s1.add(keep, send)
    c3.share(token)
    s0.step([token])
    token = work(6, "front")
    made_early = state["made"]

    window.gated = True
    theirs_a = swap(after(first_far_a, token), "ctx")
    theirs_b = swap(after(first_far_b, token), "ctx")
    pick_t = work(7, "front_end", window.step())
    made_late = state["made"]
    back = state["back"]

    back_far_a = swap(back[0], "tp")
    pick_far = swap(after(pick_t, back[0]), "tp")
    token = window.gate(pick_t)
    s0.step([token])
    s1.step([token])
    state["made"] = made_early
    keep_early, send_early, token = work(6, "rest", window.step())
    token = window.gate(token, back_far_a, pick_far)
    back_far_b = swap(after(back[1], token), "tp")
    s2.add(keep_early, send_early, token)
    s0_mine, s0_theirs = s0.finish([token])
    s1.step([token])
    emitted = emit((s0_mine, s0_theirs), 0, EXPERTS, None, core_only, [token])
    state["made"] = made_late
    keep, send, token = work(7, "rest_end", [emitted[0], *window.step()])
    moe = state["moe"]
    token = window.gate(token, back_far_b)
    s2.add(keep, send, token)
    s1.step([token])
    rg, low_t, dout, ll, gain_two = unsettle(
        back, (back_far_a, back_far_b), (pick_t, pick_far), wt, res, cot, extra, w_out, core_only, window.step()
    )
    token = window.gate(ll)
    moe_far_a = swap(after(moe[0], token), "tp")
    s1.step([token])
    s2.step([token])
    parts = 2
    dq_a, dkv_a, dother_a = attend_back(q, kv, other, dout, mixed, lse, cosine, sine, core_only, 0, parts, window.step())
    token = window.gate(dother_a)
    more_a = swap(after(dother_a, token), "ctx")
    s2.step([token])
    lane = jnp.arange(LANES)
    column = jnp.where(lane == 1, gain_two[0][:, None], 0.0)
    early_keep, early_send = early_grads(
        low_t, mixed, n2t, ll, column, n1t, dq_a, w_first, plain, first_rank, core_at, shard, [dother_a, *window.step()]
    )
    token = window.gate(early_keep, moe_far_a)
    far_qa = swap(after(dq_a, token), "tp")
    early = Scatter(core, count, plain, core_at)
    early.add(early_keep, early_send, token)
    s2.step([token])
    s1_mine, s1_theirs = s1.finish([token])
    dq_b, dkv_b, dother_b = attend_back(
        q, kv, other, dout, mixed, lse, cosine, sine, core_only, 1, parts, [s1_mine, *window.step()]
    )
    token = window.gate(dother_b, far_qa)
    more_b = swap(after(dother_b, token), "ctx")
    far_qb = swap(after(dq_b, token), "tp")
    early.step([token])
    low_kv = key_value_grads(cosine, sine, [dkv_a, dkv_b], [more_a, more_b], core_only, window.step())
    token = window.gate(low_kv)
    early.step([token])
    s2.step([token])
    half_blocks = heads // 4
    last_keep, last_send = late_grads(
        n1t, dq_b, low_kv, w_first, half_blocks, plain, first_rank, core_at, shard, window.step()
    )
    token = window.gate(last_keep, far_qb)
    far_kv = swap(after(low_kv, token), "tp")
    late = Scatter(core, count, plain, core_at)
    late.add(last_keep, last_send, token)
    late.step([token])
    early.step([late.value])
    emitted = emit((s1_mine, s1_theirs), EXPERTS * 3 // 8, EXPERTS, emitted, core_only, [late.value])
    late.step([emitted[0], early.value])
    moe_far_b = swap(after(moe[1], late.value), "tp")
    lows = [dq_a, dq_b, low_kv, far_qa, far_qb, far_kv]
    token_grad = finish(
        tok, extra, rg, lows, w_first, (first_far_a, first_far_b), (theirs_a, theirs_b), core_only, [late.value]
    ).reshape(tokens.shape)
    late.step([token_grad, moe_far_b])
    s2_mine, s2_theirs = s2.finish([late.value])
    early.step([late.value])
    late.step([s2_mine, early.value])
    result = combine(res, moe, (moe_far_a, moe_far_b), core_only, [late.value])
    grad_gate, grad_up, grad_down = emit((s2_mine, s2_theirs), EXPERTS * 3 // 4, EXPERTS, emitted, core_only, [late.value])
    early_sums = early.finish([result])
    late_sums = late.finish([result, grad_gate])
    result = result.reshape(tokens.shape)
    kv_width = kvs * HEAD_DIM
    widths = (w_output.shape[1], w_query.shape[1], kv_width, kv_width)
    grad_output, grad_query, grad_key, grad_value, extras = spread(early_sums, late_sums, widths, core_only)
    grad_norm_two = extras[:, 1]
    grad_router = extras[:, ROUTER_LANE : ROUTER_LANE + EXPERTS]
    gain_part = extras[:, 0] + extras[:, LANES]
    grad_norm_one = gain_part + swap(gain_part, "tp")
    return (
        result,
        token_grad,
        grad_norm_one,
        grad_query,
        grad_key,
        grad_value,
        grad_output,
        grad_norm_two,
        grad_router,
        grad_gate,
        grad_up,
        grad_down,
    )


def solution(mesh):
    slab = P("dp", "ctx", None, None)
    split, rows_only, expert = P("dp", "tp"), P("dp"), P(None, "dp", "tp")
    return jax.shard_map(
        body,
        mesh=mesh,
        in_specs=(slab, slab, slab, rows_only, split, split, split, split, rows_only, P("dp", None), expert, expert, expert),
        out_specs=(slab, slab, rows_only, split, split, split, split, rows_only, P("dp", None), expert, expert, expert),
        check_vma=False,
    )
```

```python
import functools

import jax
import jax.numpy as jnp
from jax import lax
from jax.experimental import pallas as pl
from jax.experimental.pallas import tpu as pltpu
from jax.sharding import PartitionSpec as P

HEAD_DIM = 64
EXPERTS = 16
TOPK = 8
PROMPT_TOKENS = 1024
LANES = 128
ROUTER_LANE = 16

norm_eps = 1e-06
rope_base = 10000.0
masked_score = -1e30
bf = jnp.bfloat16
f32 = jnp.float32
contract_cols = (((1,), (1,)), ((), ()))
COSTS = dict(experts_all=24, experts_front_end=18, experts_rest_end=13, experts_front=18, experts_rest=13, attend=19, project=18, settle=16, unsettle=17, attend_back=25)
COSTS.update(early_grads=12, key_value_grads=7, late_grads=10, finish=18, emit=5, hop_sum=5, combine=5)
vmem_bytes = 63 * 1024 * 1024


def mm(a, b):
    return jnp.dot(a, b, preferred_element_type=f32)


def mm_nt(a, b):
    return lax.dot_general(a, b, contract_cols, preferred_element_type=f32)


def whole(shape):
    return pl.BlockSpec(shape, lambda *_: (0,) * len(shape), pipeline_mode=pl.Buffered(1))


def rows_of(block, width):
    return pl.BlockSpec((block, width), lambda i, *_: (i, 0))


def any_space():
    return pl.BlockSpec(memory_space=pltpu.HBM)


def call(kernel, name, grid, ins, in_specs, outs, out_specs, scratch, flops, scalars, deps=(), limit=vmem_bytes, aliases=None):
    moved = sum(a.size * a.dtype.itemsize for a in (*ins, *outs))
    return pl.pallas_call(
        lambda sc, *refs: kernel(sc, *refs[len(deps) :]),
        out_shape=tuple(outs),
        grid_spec=pltpu.PrefetchScalarGridSpec(
            num_scalar_prefetch=1,
            grid=grid,
            in_specs=[pl.BlockSpec(memory_space=pltpu.HBM) for _ in deps] + list(in_specs),
            out_specs=tuple(out_specs),
            scratch_shapes=scratch,
        ),
        compiler_params=pltpu.CompilerParams(vmem_limit_bytes=limit),
        cost_estimate=pl.CostEstimate(flops=COSTS.get(name, 3) * 1_153_000_000, bytes_accessed=1, transcendentals=0),
        name=name,
        input_output_aliases=aliases or {},
    )(scalars, *deps, *ins)


def after(values, *deps):
    return lax.optimization_barrier((values, *deps))[0]


def sds(shape, dtype):
    return jax.ShapeDtypeStruct(tuple(shape), dtype)


def ring_rank(place, count):
    place = lax.rem(place + 2 * count, count)
    return jnp.where(place < count // 2, 2 * place, 2 * count - 1 - 2 * place)


def ring_place(rank, count):
    return jnp.where(rank % 2 == 0, rank // 2, (2 * count - 1 - rank) // 2)


def ring_hop(values, count):
    order = list(range(0, count, 2)) + list(range(count - 1, 0, -2))
    pairs = []
    for k in range(count):
        here, there = order[k], order[(k + 1) % count]
        pairs += [(2 * here, 2 * there), (2 * there + 1, 2 * here + 1)]
    return sent(lax.ppermute(values, ("dp", "ctx"), pairs))


def swap(values, axis):
    swapped = lax.ppermute(values, axis, [(0, 1), (1, 0)])
    return sent(swapped) if axis == "ctx" or not window.gated else swapped


class Window:
    def __init__(self):
        self.now, self.before, self.soon = [], [], []
        self.gated = False

    def turn(self):
        due, self.before, self.now, self.soon = self.before + self.soon, self.now, [], []
        return due

    def step(self):
        due, self.before, self.now, self.soon = self.soon, self.before + self.now, [], []
        return due

    def gate(self, token, *more):
        token = after(token, *self.before, *more)
        self.before = []
        return token


window = Window()


def sent(values):
    window.now.append(values)
    return values


def take(values, start, size, axis=0):
    return lax.dynamic_slice_in_dim(values, start, size, axis)


def place_half(values, core, axis):
    zeros = jnp.zeros_like(values)
    return jnp.where(core == 0, jnp.concatenate([values, zeros], axis), jnp.concatenate([zeros, values], axis))


PLANNED = 4


class Gather:
    def __init__(self, own, core, count, axis):
        self.own, self.core, self.count, self.axis = own, core, count, axis
        self.mine, self.mate, self.hops = [], [], 0

    def share(self, *held):
        if len(self.mate) < len(self.mine):
            self.mate.append(swap(after(self.mine[-1], *held), "ctx"))

    def step(self, *held):
        for _ in range(1 if self.hops else self.count // 2 - PLANNED + 1):
            got = self.hop(*held)
        return got

    def hop(self, *held):
        self.share(*held)
        self.hops += 1
        last = after(self.mine[-1] if self.mine else self.own, *held)
        if self.hops == self.count // 2:
            size = last.shape[self.axis] // 2
            last = take(last, self.core * size, size, self.axis)
        self.mine.append(ring_hop(last, self.count))
        return self.mine[-1]

    def finish(self):
        while self.hops < self.count // 2:
            self.step()
        self.share()
        return self

    @property
    def bufs(self):
        return [self.own, *self.mine, *self.mate]


def gather_sources(place, core, count):
    sign = 1 - 2 * core
    away = list(range(1, count // 2 + 1))
    return [ring_rank(place, count)] + [ring_rank(place - sign * a, count) for a in away] + [ring_rank(place + sign * a, count) for a in away]


def scatter_sources(place, core, count):
    sign = 1 - 2 * core
    away = list(range(1, count // 2))
    keep = [ring_rank(place + sign * a, count) for a in away] + [ring_rank(place + count // 2, count)]
    send = [ring_rank(place - sign * a, count) for a in away] + [ring_rank(place, count)]
    return keep + send


class Scatter:
    def __init__(self, core, count, scalars, core_at):
        self.core, self.count, self.scalars, self.core_at = core, count, scalars, core_at
        self.keeps, self.gots, self.hops, self.got = [], [], 0, None

    def add(self, keep, send, *held):
        self.keeps.append(keep)
        self.gots.append(swap(after(send, *held), "ctx"))
        return self.gots[-1]

    def step(self, deps=()):
        for _ in range(1 if self.hops else self.count // 2 - PLANNED + 1):
            got = self.hop(deps)
        return got

    def hop(self, deps):
        self.hops += 1
        stage = {1: None, 2: "second"}.get(self.hops, "middle")
        slot = self.count // 2 - self.hops if self.hops > 1 else self.count // 2 - 1
        value = hop_sum(self.keeps, self.gots, self.got, slot, stage, self.scalars, self.core_at, deps)
        self.value = value
        window.soon.append(value)
        self.got = ring_hop(value, self.count)
        return self.got

    def finish(self, deps=()):
        while self.hops < self.count // 2:
            self.step()
        mine = hop_sum(self.keeps, self.gots, self.got, self.count // 2 - 1, "end", self.scalars, self.core_at, deps)
        return mine, swap(mine, "ctx")


def load_shards(sc, bufs, dst, shard, sem):
    total = len(bufs)
    hops = total // 2
    half = dst.shape[0] // 2
    for k, buf in enumerate(bufs):
        rows = pl.ds(pl.multiple_of(sc[k] * shard, shard), shard)
        if k in (hops, 2 * hops):
            side = sc[total] if k == hops else 1 - sc[total]
            target = dst.at[pl.ds(side * half, half), rows, :]
        else:
            target = dst.at[:, rows, :]
        pltpu.make_async_copy(buf, target, sem).start()


def lanes_of(ref, first, count):
    return jnp.concatenate([ref[first + b] for b in range(count)], axis=1)


def rope(x, cosine, sine):
    lane = lax.broadcasted_iota(jnp.int32, x.shape, x.ndim - 1)
    ahead = pltpu.roll(x, x.shape[-1] - HEAD_DIM // 2, x.ndim - 1)
    behind = pltpu.roll(x, HEAD_DIM // 2, x.ndim - 1)
    return x * cosine + jnp.where(lax.rem(lane, HEAD_DIM) < HEAD_DIM // 2, ahead, behind) * sine


def lane_column(row, shape, lane_at):
    lane = lax.broadcasted_iota(jnp.int32, shape, 1)
    return jnp.where(lane == lane_at, jnp.broadcast_to(row, (shape[1], shape[0])).T, 0.0)


def pack_kernel(sc, query, key, value, output, router, gain_one, gain_two, out):
    at = 0
    for ref in (query, key, value):
        for b in range(ref.shape[1] // LANES):
            out[at] = ref[:, b * LANES : (b + 1) * LANES]
            at += 1
    shape = out.shape[1:]
    extra = lane_column(gain_one[...].astype(f32), shape, 0) + lane_column(gain_two[...].astype(f32), shape, 1)
    out[at] = extra.astype(bf)
    out[at, :, ROUTER_LANE : ROUTER_LANE + EXPERTS] = router[...]
    for b in range(output.shape[1] // LANES):
        out[at + 1 + b] = output[:, b * LANES : (b + 1) * LANES]
    for b in range(at + 1 + output.shape[1] // LANES, out.shape[0]):
        out[b] = jnp.zeros(shape, bf)


def pack(query, key, value, output, router, gain_one, gain_two, core):
    shard = query.shape[0]
    ins = [query, key, value, output, router, gain_one.reshape(1, shard), gain_two.reshape(1, shard)]
    blocks = (query.shape[1] + key.shape[1] + value.shape[1] + output.shape[1]) // LANES + 1
    blocks += blocks % 2
    out = sds((blocks, shard, LANES), bf)
    return call(pack_kernel, "pack", (1,), ins, [whole(a.shape) for a in ins], [out], [whole(out.shape)], [], 0, core)[0]


def qkv_kernel(shard, kinds, sc, tok, cosine, sine, *refs):
    heads, kvs, total = kinds
    bufs, (w_first, w_out, w_half, extra_out, q_out, kv_out, packed_out, nt_out, w, et, sem, out_sem) = refs[:total], refs[total:]
    step = pl.program_id(0)
    count, half = w_first.shape[0], w_half.shape[0]
    copies = [
        (w.at[pl.ds(0, count)], w_first),
        (w.at[pl.ds(count, 2 * half)], w_out),
        (w.at[pl.ds(count + sc[total] * half, half)], w_half),
    ]

    @pl.when(step == 0)
    def _():
        load_shards(sc, bufs, w, shard, sem)
        pltpu.make_async_copy(w, w, sem).wait()
        for k, (src, dst) in enumerate(copies):
            pltpu.make_async_copy(src, dst, out_sem.at[k]).start()
        et[...] = w[count - 1].T

    extra_out[...] = et[...]
    x = tok[...].astype(f32)
    scale = lax.rsqrt(jnp.mean(x * x, axis=-1, keepdims=True) + norm_eps)
    normed = (x * scale * et[0:1, :].astype(f32)).astype(bf)
    nt_out[...] = normed.T
    cs, sn = cosine[...], sine[...]
    for pair in range((heads + 2 * kvs) // 4):
        made = mm(normed, lanes_of(w, 2 * pair, 2))
        for side in range(2):
            first = 4 * pair + 2 * side
            part = made[:, side * LANES : (side + 1) * LANES]
            if first < heads + kvs:
                part = rope(part, cs, sn)
            out, at = kv_out, first - heads
            if first < heads:
                part, out, at = part * (1.0 / HEAD_DIM), q_out, first
            low = part.astype(bf)
            for k in range(2):
                one = low[:, k * HEAD_DIM : (k + 1) * HEAD_DIM]
                out[at + k] = one
                if first >= heads:
                    for quarter in range(2):

                        @pl.when(step == quarter)
                        def _():
                            packed_out[at + k, :, quarter * HEAD_DIM : (quarter + 1) * HEAD_DIM] = one

    @pl.when(step == pl.num_programs(0) - 1)
    def _():
        for k, (src, dst) in enumerate(copies):
            pltpu.make_async_copy(src, dst, out_sem.at[k]).wait()


def project(tokens, cosine, sine, scalars, bufs, heads, kvs, prompt, deps, block=256):
    rows, width = tokens.shape
    blocks, shard = bufs[0].shape[:2]
    count = (heads + 2 * kvs) // 2 + 1
    head_spec = lambda n: pl.BlockSpec((n, block, HEAD_DIM), lambda i, s: (0, i, 0))
    outs = [
        sds((count, width, LANES), bf),
        sds((heads // 2, width, LANES), bf),
        sds((heads // 4, width, LANES), bf),
        sds((LANES, width), bf),
        sds((heads, rows, HEAD_DIM), bf),
        sds((2 * kvs, rows, HEAD_DIM), bf),
        sds((2 * kvs, prompt // 2, LANES), bf),
        sds((width, rows), bf),
    ]
    return call(
        functools.partial(qkv_kernel, shard, (heads, kvs, len(bufs))),
        "project",
        (rows // block,),
        [tokens, cosine, sine, *bufs],
        [rows_of(block, width), rows_of(block, LANES), rows_of(block, LANES)] + [any_space()] * len(bufs),
        outs,
        [
            any_space(),
            any_space(),
            any_space(),
            whole((LANES, width)),
            head_spec(heads),
            head_spec(2 * kvs),
            whole((2 * kvs, prompt // 2, LANES)),
            pl.BlockSpec((width, block), lambda i, s: (0, i)),
        ],
        [
            pltpu.VMEM((blocks, width, LANES), bf),
            pltpu.VMEM((LANES, width), bf),
            pltpu.SemaphoreType.DMA,
            pltpu.SemaphoreType.DMA((3,)),
        ],
        2 * rows * width * count * LANES,
        scalars,
        deps,
    )


def causal(scores):
    key = lax.broadcasted_iota(jnp.int32, scores.shape, 0)
    query = lax.broadcasted_iota(jnp.int32, scores.shape, 1)
    return jnp.where(key <= query, scores, masked_score)


def block_scores(query, keys, other_keys, at, block, prompt, bias):
    parts = []
    if at:
        parts.append(mm_nt(keys[0:at], query))
    parts.append(causal(mm_nt(keys[at : at + block], query)))
    other = mm_nt(other_keys, query)
    if at < prompt:
        other = other + bias
    parts.append(other)
    return parts


def unpack(ref):
    return jnp.concatenate([ref[0, :, :HEAD_DIM], ref[0, :, HEAD_DIM:]], axis=0)


def attend_kernel(cfg, sc, q, k0, k1, o0, o1, v0, v1, w0, w1, mixed, lse):
    starts, block, prompt = cfg
    bias = jnp.where(sc[0] == 0, masked_score, 0.0).astype(f32)
    for side, (keys, other, values, other_values) in enumerate(((k0, o0, v0, w0), (k1, o1, v1, w1))):
        values_t = values[0].T
        other_t = unpack(other_values).T
        other_keys = unpack(other)
        for a, at in enumerate(starts):
            rows = slice(a * block, a * block + block)
            scores = block_scores(q[side, rows, :], keys[0], other_keys, at, block, prompt, bias)
            peak = functools.reduce(jnp.maximum, [jnp.max(s, axis=0, keepdims=True) for s in scores])
            raw = [jnp.exp(s - peak) for s in scores]
            total = sum(jnp.sum(r, axis=0, keepdims=True) for r in raw)
            low = [r.astype(bf) for r in raw]
            out = mm(other_t, low[-1]) + mm(values_t[:, at : at + block], low[-2])
            if at:
                out = out + mm(values_t[:, 0:at], low[0])
            out = out * (1.0 / total)
            mixed[rows, side * HEAD_DIM : side * HEAD_DIM + HEAD_DIM] = out.T.astype(bf)
            lse[0, side : side + 1, rows] = peak + jnp.log(total)


def kv_specs(kvs, rows, prompt, rep, first_pair):
    index = lambda side, base: (lambda p, s: (base + (2 * (p + first_pair) + side) // rep, 0, 0))
    specs = []
    for base in (0, kvs):
        specs += [pl.BlockSpec((1, rows, HEAD_DIM), index(side, base)) for side in range(2)]
        specs += [pl.BlockSpec((1, prompt // 2, LANES), index(side, base)) for side in range(2)]
    return specs


def attend(q, kv, other, core, part, deps, block=256):
    heads, rows, _ = q.shape
    kvs, prompt = other.shape[0] // 2, 2 * other.shape[1]
    count = prompt if part == 0 else rows - prompt
    first = 0 if part == 0 else prompt
    starts = tuple(range(first, first + count, block))
    return call(
        functools.partial(attend_kernel, (starts, block, prompt)),
        "attend",
        (heads // 2,),
        [q, kv, kv, other, other, kv, kv, other, other],
        [pl.BlockSpec((2, count, HEAD_DIM), lambda p, s: (p, part, 0)), *kv_specs(kvs, rows, prompt, heads // kvs, 0)],
        [sds((count, heads * HEAD_DIM), bf), sds((heads // 2, 2, count), f32)],
        [
            pl.BlockSpec((count, LANES), lambda p, s: (0, p)),
            pl.BlockSpec((1, 2, count), lambda p, s: (p, 0, 0)),
        ],
        [],
        16 * heads * count * 1024 * HEAD_DIM,
        core,
        deps,
    )


def attend_back_kernel(cfg, sc, q, k0, k1, o0, o1, v0, v1, w0, w1, dout, mixed_a, mixed_b, lse_a, lse_b, cosine, sine, dq, dkv, dother_out, dother):
    rows_total, block, prompt, rep = cfg
    pair = pl.program_id(0)
    bias = jnp.where(sc[0] == 0, masked_score, 0.0).astype(f32)
    kvs = dkv.shape[0] // 2

    @pl.when(pair == 0)
    def _():
        dkv[...] = jnp.zeros_like(dkv)
        dother[...] = jnp.zeros_like(dother)

    heads = ((k0, unpack(o0), v0, unpack(w0)), (k1, unpack(o1), v1, unpack(w1)))
    keys_t = [(keys[0].T, other.T) for keys, other, _, _ in heads]
    for at in range(0, rows_total, block):
        rows = slice(at, at + block)
        mixed, lse, local = (mixed_a, lse_a, at) if at < prompt else (mixed_b, lse_b, at - prompt)
        inner = slice(local, local + block)
        dot = (dout[rows, :].astype(f32) * mixed[inner, :].astype(f32)).T
        grads = []
        for side, (keys, other, values, other_values) in enumerate(heads):
            head = (2 * pair + side) // rep
            query = q[side, rows, :]
            grad = dout[rows, side * HEAD_DIM : side * HEAD_DIM + HEAD_DIM]
            weighted = jnp.sum(dot[side * HEAD_DIM : side * HEAD_DIM + HEAD_DIM], axis=0, keepdims=True)
            norm = lse[0, side : side + 1, inner]
            scores = block_scores(query, keys[0], other, at, block, prompt, bias)
            spans = ([(False, 0, at)] if at else []) + [(False, at, block), (True, 0, prompt)]
            back = None
            for score, (is_other, first, size) in zip(scores, spans):
                probs = jnp.exp(score - norm)
                value = other_values if is_other else values[0, first : first + size]
                score_low = (probs * (mm_nt(value, grad) - weighted)).astype(bf)
                sums = dother if is_other else dkv
                span = pl.ds(first, size)
                sums[kvs + head, span, :] += mm(probs.astype(bf), grad)
                sums[head, span, :] += mm(score_low, query)
                key_t = keys_t[side][1] if is_other else keys_t[side][0][:, first : first + size]
                term = mm(key_t, score_low)
                back = term if back is None else back + term
            grads.append(back)
        both = jnp.concatenate(grads, axis=0).T * (1.0 / HEAD_DIM)
        dq[rows, :] = rope(both, cosine[rows, :], -sine[rows, :]).astype(bf)

    @pl.when(pair == pl.num_programs(0) - 1)
    def _():
        for h in range(dother.shape[0]):
            for quarter in range(2):
                part = dother[h, quarter * (prompt // 2) : (quarter + 1) * (prompt // 2), :]
                dother_out[h, :, quarter * HEAD_DIM : (quarter + 1) * HEAD_DIM] = part


def attend_back(q, kv, other, dout, mixed, lse, cosine, sine, core, part, parts, deps, block=256):
    heads, rows, _ = q.shape
    kvs, prompt = other.shape[0] // 2, 2 * other.shape[1]
    pairs = heads // 2 // parts
    first = part * pairs
    mine = 2 * kvs // parts
    pair = pl.BlockSpec((rows, LANES), lambda p, s: (0, p + first))
    mixed_spec = lambda a: pl.BlockSpec((a.shape[0], LANES), lambda p, s: (0, p + first))
    lse_spec = lambda a: pl.BlockSpec((1, 2, a.shape[2]), lambda p, s: (p + first, 0, 0))
    return call(
        functools.partial(attend_back_kernel, (rows, block, prompt, heads // kvs)),
        "attend_back",
        (pairs,),
        [q, kv, kv, other, other, kv, kv, other, other, dout, *mixed, *lse, cosine, sine],
        [
            pl.BlockSpec((2, rows, HEAD_DIM), lambda p, s: (p + first, 0, 0)),
            *kv_specs(kvs, rows, prompt, heads // kvs, first),
            pair,
            *[mixed_spec(a) for a in mixed],
            *[lse_spec(a) for a in lse],
            whole(cosine.shape),
            whole(sine.shape),
        ],
        [
            sds((rows, pairs * LANES), bf),
            sds((mine, rows, HEAD_DIM), f32),
            sds((mine, prompt // 2, LANES), f32),
        ],
        [
            pl.BlockSpec((rows, LANES), lambda p, s: (0, p)),
            whole((mine, rows, HEAD_DIM)),
            whole((mine, prompt // 2, LANES)),
        ],
        [pltpu.VMEM((mine, prompt, HEAD_DIM), f32)],
        40 * heads // parts * rows * 1024 * HEAD_DIM,
        core,
        deps,
    )


def load_halves(sc, mine, theirs, first_block, w, sem):
    half = mine.shape[0]
    pltpu.make_async_copy(mine, w.at[pl.ds(first_block + sc[0] * half, half)], sem).start()
    pltpu.make_async_copy(theirs, w.at[pl.ds(first_block + (1 - sc[0]) * half, half)], sem).start()


def settle_kernel(sc, tok, ids, own_a, own_b, far_a, far_b, extra, w_own, w_mine, w_theirs, res_out, n_out, nt_out, wt_out, w, sem):
    step = pl.program_id(0)
    blocks = w_own.shape[0]

    @pl.when(step == 0)
    def _():
        pltpu.make_async_copy(w_own, w.at[pl.ds(0, blocks)], sem).start()
        load_halves(sc, w_mine, w_theirs, blocks, w, sem)
        pltpu.make_async_copy(w, w, sem).wait()

    early = step < pl.num_programs(0) // 2
    own = jnp.where(early, own_a[...], own_b[...])
    far = jnp.where(early, far_a[...], far_b[...])
    branch = mm_nt(own, lanes_of(w, 0, blocks)) + mm_nt(far, lanes_of(w, blocks, blocks))
    residual = tok[...].astype(f32) + branch
    res_out[...] = residual
    scale = lax.rsqrt(jnp.mean(residual * residual, axis=-1, keepdims=True) + norm_eps)
    normed = (residual * scale * extra[1:2, :].astype(f32)).astype(bf)
    n_out[...] = normed
    nt_out[...] = normed.T
    logits = mm_nt(normed, extra[...])
    lane = lax.broadcasted_iota(jnp.int32, logits.shape, 1)
    routed = lane < 0
    for k in range(TOPK):
        routed = jnp.logical_or(routed, lane == ids[:, k : k + 1] + ROUTER_LANE)
    logits = jnp.where(routed, logits, masked_score)
    raw = jnp.where(routed, jnp.exp(logits - jnp.max(logits, axis=-1, keepdims=True)), 0.0)
    wt_out[...] = raw / jnp.sum(raw, axis=-1, keepdims=True)


def settle(tokens, ids, own, far, extra, w_own, w_mine, w_theirs, core, deps, block=256):
    rows, width = tokens.shape
    halves = rows // block // 2
    cols = own[0].shape[1]
    low = pl.BlockSpec((block, cols), lambda i, s: (jnp.minimum(i, halves - 1), 0))
    high = pl.BlockSpec((block, cols), lambda i, s: (jnp.maximum(i - halves, 0), 0))
    return call(
        settle_kernel,
        "settle",
        (rows // block,),
        [tokens, ids, *own, *far, extra, w_own, w_mine, w_theirs],
        [rows_of(block, width), rows_of(block, TOPK), low, high, low, high, whole(extra.shape)] + [any_space()] * 3,
        [sds((rows, width), f32), sds((rows, width), bf), sds((width, rows), bf)] + [sds((rows, LANES), f32)],
        [rows_of(block, width), rows_of(block, width), pl.BlockSpec((width, block), lambda i, s: (0, i))]
        + [rows_of(block, LANES)],
        [pltpu.VMEM((2 * w_own.shape[0], width, LANES), bf), pltpu.SemaphoreType.DMA],
        4 * rows * width * cols,
        core,
        deps,
    )


def mix_halves(core, kept, sent):
    first = jnp.concatenate([kept[0], sent[0]], axis=-1)
    second = jnp.concatenate([kept[1], sent[1]], axis=-1)
    return jnp.where(core == 0, first, second), jnp.where(core == 0, second, first)


PARTS = ((3, 1), (2, 2))


def fetch_weights(sc, bufs, w, kinds, local, shard, hidden, sem):
    hops = len(bufs) // 2
    core = sc[len(bufs)]
    for k, buf in enumerate(bufs):
        rows = pl.ds(pl.multiple_of(sc[k] * shard, shard), shard)
        target = w.at[kinds, :, rows, :]
        if k in (hops, 2 * hops):
            at = core if k == hops else 1 - core
            target = w.at[kinds, :, rows, pl.ds(pl.multiple_of(at * (hidden // 2), LANES), hidden // 2)]
        pltpu.make_async_copy(buf.at[kinds, pl.ds(local, 2)], target, sem).start()


def both(w, kind):
    return jnp.concatenate([w[kind, 0], w[kind, 1]], axis=1)


def activate(ids, hidden, rows, x, grad_rows, w, wt, pick_in, pick, scaled, acts):
    lane = lax.broadcasted_iota(jnp.int32, (x.shape[0], LANES), 1)
    gate = mm(x, both(w, 0))
    up = mm(x, both(w, 1))
    grad = mm(grad_rows, both(w, 2))
    table = wt[rows, :]
    sig = 1.0 / (1.0 + jnp.exp(-gate))
    silu = gate * sig
    act = silu * up
    dots = act * grad
    picked = jnp.zeros(table.shape, f32) if pick_in is None else pick_in[rows, :]
    for side, expert in enumerate(ids):
        cols = slice(side * hidden, side * hidden + hidden)
        weight = jnp.sum(jnp.where(lane == expert, table, 0.0), axis=1, keepdims=True)
        picked = picked + jnp.where(lane == expert, jnp.sum(dots[:, cols], axis=1, keepdims=True), 0.0)
        scaled[rows, cols] = (act[:, cols] * weight).astype(bf)
        g = grad[:, cols] * weight
        s = sig[:, cols]
        acts[rows, cols] = (g * up[:, cols] * s * (1.0 + gate[:, cols] * (1.0 - s))).astype(bf)
        acts[rows, slice((2 + side) * hidden, (3 + side) * hidden)] = (g * silu[:, cols]).astype(bf)
    pick[rows, :] = picked
    return picked


def pair_grads(sc, total, shard, hidden, xt, ct, scaled, acts, keep_s, send_s, keep, send, g_sem):
    core, ranks, slots = sc[total], total + 1, total // 2
    for slot in range(slots):
        at = [pl.ds(pl.multiple_of(sc[ranks + slots * k + slot] * shard, shard), shard) for k in range(2)]
        left = lambda ref: jnp.concatenate([ref[at[0], :], ref[at[1], :]], axis=0)
        gate_up = mm(left(xt), acts[...]).astype(bf)
        down = mm(left(ct), scaled[...]).astype(bf)
        kinds = (gate_up[:, : 2 * hidden], gate_up[:, 2 * hidden :], down)
        for kind, made in enumerate(kinds):
            for side in range(2):
                part = made[:, side * hidden : side * hidden + hidden]
                kept, sent_part = part[:shard], part[shard:]
                if slot == slots - 1:
                    cut = lambda a: (a[:, : hidden // 2], a[:, hidden // 2 :])
                    kept, sent_part = mix_halves(core, cut(kept), cut(sent_part))
                keep_s[slot, side * 3 + kind] = kept
                send_s[slot, side * 3 + kind] = sent_part
        pltpu.make_async_copy(keep_s.at[slot], keep.at[slot], g_sem.at[0]).start()
        pltpu.make_async_copy(send_s.at[slot], send.at[slot], g_sem.at[1]).start()


def experts_kernel(cfg, sc, *refs):
    shard, hidden, local, first, mode, total = cfg
    block = 256
    it = iter(refs)
    front, rest, ends = mode.startswith("front"), mode.startswith("rest"), mode.endswith("_end")
    n2, cot, wt = (None, None, None) if rest else (next(it), next(it), next(it))
    n2t, cott = (None, None) if front else (next(it), next(it))
    bufs = [next(it) for _ in range(total)]
    moe_in = None if first or front else next(it)
    back_in, pick_in = (None, None) if first or rest else (next(it), next(it))
    scaled_in, acts_in = (next(it), next(it)) if rest else (None, None)
    take_out = lambda: tuple(next(it) for _ in range(len(PARTS[front]) if ends else 1))
    moe_out = None if front else take_out()
    back_out = None if rest else take_out()
    keep, send = (None, None) if front else (next(it), next(it))
    pick = None if rest else next(it)
    scaled_out, acts_out = (next(it), next(it)) if front else (None, None)
    pick_t = next(it) if front and ends else None
    w, scaled, acts, w_sem, in_sem, out_sem = (next(it) for _ in range(6))
    moe = None if front else next(it)
    back = None if rest else next(it)
    xs, cs, x_sem, c_sem = (None,) * 4 if rest else (next(it) for _ in range(4))
    xt, ct, keep_s, send_s, t_sem, g_sem = (None,) * 6 if front else (next(it) for _ in range(6))
    low = next(it) if ends else None
    rows_total = scaled.shape[0]
    spans = [pl.ds(at, block) for at in range(0, rows_total, block)]
    ids = [sc[total + 1 + 2 * (total // 2) + side] + ROUTER_LANE for side in range(2)]

    loads = (pl.ds(0, block), pl.ds(block, rows_total - block))

    def row_copies(i):
        return [
            pltpu.make_async_copy(n2.at[loads[i]], xs.at[loads[i]], x_sem.at[i]),
            pltpu.make_async_copy(cot.at[loads[i]], cs.at[loads[i]], c_sem.at[i]),
        ]

    def load_wide():
        for k, (src, dst) in enumerate(((moe_in, moe), (back_in, back))):
            if src is not None:
                pltpu.make_async_copy(src, dst, in_sem.at[k]).start()
        if not front:
            pltpu.make_async_copy(n2t, xt, t_sem.at[0]).start()
            pltpu.make_async_copy(cott, ct, t_sem.at[1]).start()

    kinds = pl.ds(2, 1) if rest else pl.ds(0, 3)
    fetch_weights(sc, bufs, w, kinds, local, shard, hidden, w_sem)
    if rest:
        pltpu.make_async_copy(scaled_in, scaled, out_sem.at[2]).start()
        load_wide()
        pltpu.make_async_copy(acts_in, acts, out_sem.at[3]).start()
        pltpu.make_async_copy(w.at[kinds], w.at[kinds], w_sem).wait()
        pltpu.make_async_copy(scaled_in, scaled, out_sem.at[2]).wait()
    else:
        for copy in row_copies(0) + row_copies(1):
            copy.start()
        pltpu.make_async_copy(w.at[kinds], w.at[kinds], w_sem).wait()
        for i, rows in enumerate(spans):
            for copy in row_copies(i) if i < 2 else ():
                copy.wait()
            if i == 1:
                load_wide()
            picked = activate(ids, hidden, rows, xs[rows, :], cs[rows, :], w, wt, pick_in, pick, scaled, acts)
            if pick_t is not None:
                pick_t[:, rows] = picked.T[ROUTER_LANE : ROUTER_LANE + EXPERTS]

    for k, (src, dst) in enumerate(((moe_in, moe), (back_in, back))):
        if src is not None:
            pltpu.make_async_copy(src, dst, in_sem.at[k]).wait()
    outs = []
    if not front:
        outs.append((moe, moe_out, 0, lambda rows: mm_nt(scaled[rows, :], both(w, 2))))
    if not rest:
        two = lambda rows: mm_nt(acts[rows, 0 : 2 * hidden], both(w, 0)) + mm_nt(acts[rows, 2 * hidden :], both(w, 1))
        outs.append((back, back_out, 1, two))
    for i, rows in enumerate(spans):
        for acc, halves, k, make in outs:
            made = make(rows) + acc[rows, :]
            scr = acc if low is None else low
            scr[rows, :] = made.astype(scr.dtype)
            part, at = 0, i
            while len(halves) > 1 and at >= PARTS[front][part]:
                part, at = part + 1, at - PARTS[front][part]
            to = halves[part].at[pl.ds(at * block, block)]
            pltpu.make_async_copy(scr.at[rows], to, out_sem.at[k]).start()
    if front:
        pltpu.make_async_copy(scaled, scaled_out, out_sem.at[2]).start()
        pltpu.make_async_copy(acts, acts_out, out_sem.at[3]).start()
    else:
        pltpu.make_async_copy(n2t, xt, t_sem.at[0]).wait()
        pltpu.make_async_copy(cott, ct, t_sem.at[1]).wait()
        if rest:
            pltpu.make_async_copy(acts_in, acts, out_sem.at[3]).wait()
        pair_grads(sc, total, shard, hidden, xt, ct, scaled, acts, keep_s, send_s, keep, send, g_sem)
    for acc, _, k, _ in outs:
        scr = acc if low is None else low
        pltpu.make_async_copy(scr, scr, out_sem.at[k]).wait()
    if front:
        pltpu.make_async_copy(scaled, scaled_out, out_sem.at[2]).wait()
        pltpu.make_async_copy(acts, acts_out, out_sem.at[3]).wait()
    else:
        pltpu.make_async_copy(keep_s, keep, g_sem.at[0]).wait()
        pltpu.make_async_copy(send_s, send, g_sem.at[1]).wait()


def experts(mode, dense, turned, wt, scalars, bufs, local, moe_in, back_in, pick_in, made, deps):
    width, rows = turned[0].shape
    shard, hidden = bufs[0].shape[2:]
    slots = len(bufs) // 2
    front, rest, ends = mode.startswith("front"), mode.startswith("rest"), mode.endswith("_end")
    first = False
    hbm, table = any_space(), whole((rows, LANES))
    ins, specs, outs, out_specs = [], [], [], []

    def put(arrays, spec):
        ins.extend(arrays)
        specs.extend([spec] * len(arrays))

    def give(shape, kind, spec=None):
        outs.append(sds(shape, kind))
        out_specs.append(spec or any_space())

    if not rest:
        put(dense, hbm)
        put([wt], table)
    if not front:
        put(turned, hbm)
    put(bufs, hbm)
    if not first and not front:
        put([moe_in], hbm)
    if not first and not rest:
        put([back_in], hbm)
        put([pick_in], table)
    if rest:
        put(made, hbm)
    pieces = [(256 * p, width) for p in PARTS[front]] if ends else [(rows, width)]
    for shape in pieces * (2 if mode == "all" else 1):
        give(shape, bf if ends else f32)
    if not front:
        give((slots, 6, shard, hidden), bf)
        give((slots, 6, shard, hidden), bf)
    if not rest:
        give((rows, LANES), f32, table)
    if front:
        give((rows, 2 * hidden), bf)
        give((rows, 4 * hidden), bf)
    if front and ends:
        give((EXPERTS, rows), f32, whole((EXPERTS, rows)))
    dma = pltpu.SemaphoreType.DMA
    scratch = [
        pltpu.VMEM((3, 2, width, hidden), bf),
        pltpu.VMEM((rows, 2 * hidden), bf),
        pltpu.VMEM((rows, 4 * hidden), bf),
        dma,
        dma((2,)),
        dma((4,)),
    ]
    scratch += [pltpu.VMEM((rows, width), f32)] * (2 if mode == "all" else 1)
    if not rest:
        scratch += [pltpu.VMEM((rows, width), bf)] * 2 + [dma((2,))] * 2
    if not front:
        scratch += [pltpu.VMEM((width, rows), bf)] * 2 + [pltpu.VMEM((slots, 6, shard, hidden), bf)] * 2 + [dma((2,))] * 2
    if ends:
        scratch.append(pltpu.VMEM((rows, width), bf))
    return call(
        functools.partial(experts_kernel, (shard, hidden, local, first, mode, len(bufs))),
        "experts_" + mode,
        (1,),
        ins,
        specs,
        outs,
        out_specs,
        scratch,
        36 * rows * width * hidden,
        scalars,
        deps,
    )


def hop_kernel(cfg, sc, *refs):
    pairs, stage, core_at = cfg
    core = sc[core_at]
    it = iter(refs)
    keeps = [next(it) for _ in range(pairs)]
    gots = [next(it) for _ in range(pairs)]
    came = next(it) if stage else None
    out = next(it)
    for p in range(pairs):
        total = keeps[p][0].astype(f32) + gots[p][0].astype(f32)
        if stage == "end":
            total = place_half(total, core, 2) + came[p].astype(f32)
        elif stage == "second":
            total = total + place_half(came[p].astype(f32), core, 2)
        elif stage:
            total = total + came[p].astype(f32)
        out[p] = total.astype(bf)


def hop_sum(keeps, gots, came, slot, stage, scalars, core_at, deps=()):
    pairs = len(keeps)
    slots, mats, shard, hidden = keeps[0].shape
    lanes = hidden // 2 if stage in (None, "end") else hidden
    side = 1 if stage == "end" else 0
    per = mats
    piece = pl.BlockSpec((1, per, shard, lanes), lambda m, s: (slot, m, 0, side))
    wide = lambda a: pl.BlockSpec((pairs, per, shard, a.shape[3]), lambda m, s: (0, m, 0, 0))
    out = sds((pairs, mats, shard, hidden // 2 if stage is None else hidden), bf)
    ins = [*keeps, *gots] + ([] if came is None else [came])
    specs = [piece] * (2 * pairs) + ([] if came is None else [wide(came)])
    kernel = functools.partial(hop_kernel, (pairs, stage, core_at))
    return call(kernel, "hop_sum", (mats // per,), ins, specs, [out], [wide(out)], [], 0, scalars, deps)[0]


def emit_kernel(sc, mine, theirs, *refs):
    for m in range(6):
        refs[m % 3 - 3][m // 3] = mine[0, m].astype(f32) + theirs[0, m].astype(f32)


def emit(group, first, total, into, core, deps):
    pairs, mats, shard, hidden = group[0].shape
    ins = [*group, *(into or [])]
    spec = pl.BlockSpec((1, mats, shard, hidden), lambda i, s: (i, 0, 0, 0))
    out_spec = pl.BlockSpec((2, shard, hidden), lambda i, s: (i + first // 2, 0, 0))
    outs = [sds((total, shard, hidden), f32)] * 3
    aliases = {1 + len(deps) + 2 + k: k for k in range(3)} if into else {}
    specs = [spec, spec] + [any_space()] * (len(ins) - 2)
    return call(emit_kernel, "emit", (pairs,), ins, specs, outs, [out_spec] * 3, [], 0, core, deps, aliases=aliases)


def norm_back(values, gain, grad):
    scale = lax.rsqrt(jnp.mean(values * values, axis=-1, keepdims=True) + norm_eps)
    inner = jnp.mean(values * gain * grad, axis=-1, keepdims=True)
    passed = scale * gain * grad - values * (scale * scale * scale * inner)
    return passed, jnp.sum(grad * values * scale, axis=0, keepdims=True)


def pick_part(refs, parts):
    step = pl.program_id(0)
    value, at = refs[0][...], 0
    for ref, size in zip(refs, parts):
        value = jnp.where(step >= at, ref[...], value)
        at += size
    return value


def part_specs(block, parts):
    specs, first = [], 0
    for p in parts:
        per = p.shape[0] // block
        specs.append(pl.BlockSpec((block, p.shape[1]), lambda i, s, first=first, per=per: (jnp.clip(i - first, 0, per - 1), 0)))
        first += per
    return specs


def combine_kernel(sc, res, *refs):
    count = len(refs) // 2
    total = pick_part(refs[:count], PARTS[0]).astype(f32) + pick_part(refs[count : 2 * count], PARTS[0]).astype(f32)
    refs[-1][...] = (res[...] + total).astype(bf)


def combine(res, own, far, core, deps, block=256):
    rows, width = res.shape
    specs = [rows_of(block, width)] + part_specs(block, own) + part_specs(block, far)
    out = sds((rows, width), bf)
    return call(combine_kernel, "combine", (rows // block,), [res, *own, *far], specs, [out], [rows_of(block, width)], [], 0, core, deps)[0]


def unsettle_kernel(sc, *refs):
    count = len(PARTS[1])
    own, far, refs = refs[:count], refs[count : 2 * count], refs[2 * count :]
    unsettle_rows(own, far, *refs)


def unsettle_rows(own, far, pick_a, pick_b, wt, res, cot, extra, w_own, rg_out, low_t_out, dout_out, ll_out, gain_out, w, sem):
    step = pl.program_id(0)

    @pl.when(step == 0)
    def _():
        pltpu.make_async_copy(w_own, w, sem).start()
        pltpu.make_async_copy(w_own, w, sem).wait()
        gain_out[...] = jnp.zeros_like(gain_out)

    weights = wt[...]
    picked = pick_a[...] + pick_b[...]
    room = lambda n: jnp.zeros((n, picked.shape[1]), f32)
    picked = jnp.concatenate([room(ROUTER_LANE), picked, room(LANES - ROUTER_LANE - EXPERTS)], axis=0).T
    logit_low = (weights * (picked - jnp.sum(weights * picked, axis=-1, keepdims=True))).astype(bf)
    ll_out[...] = logit_low
    grad = pick_part(own, PARTS[1]).astype(f32) + pick_part(far, PARTS[1]).astype(f32) + mm(logit_low, extra[...])
    passed, gain = norm_back(res[...], extra[1:2, :].astype(f32), grad)
    gain_out[...] += gain
    total = cot[...].astype(f32) + passed
    rg_out[...] = total
    low = total.astype(bf)
    low_t_out[...] = low.T
    dout_out[...] = mm(low, lanes_of(w, 0, w.shape[0])).astype(bf)


def unsettle(back, far, picks, wt, res, cot, extra, w_own, core, deps, block=256):
    rows, width = res.shape
    cols = w_own.shape[0] * LANES
    wide, thin = rows_of(block, width), rows_of(block, LANES)
    across = pl.BlockSpec((EXPERTS, block), lambda i, s: (0, i))
    return call(
        unsettle_kernel,
        "unsettle",
        (rows // block,),
        [*back, *far, *picks, wt, res, cot, extra, w_own],
        [*part_specs(block, back), *part_specs(block, far), across, across, thin, wide, wide, whole(extra.shape), any_space()],
        [sds((rows, width), f32), sds((width, rows), bf), sds((rows, cols), bf), sds((rows, LANES), bf), sds((1, width), f32)],
        [wide, pl.BlockSpec((width, block), lambda i, s: (0, i)), rows_of(block, cols), thin, whole((1, width))],
        [pltpu.VMEM(w_own.shape, bf), pltpu.SemaphoreType.DMA],
        2 * rows * width * cols,
        core,
        deps,
    )


def scaled_sum(weights, grads, gain):
    return jnp.sum(weights.astype(f32) * grads, axis=1, keepdims=True) / gain.astype(f32)


def leave(parts, core, shard, keep, send):
    last = pl.program_id(0) == pl.num_programs(0) - 1
    cut = lambda a: (a[:, :LANES], a[:, LANES:])

    @pl.when(jnp.logical_not(last))
    def _():
        for b, part in enumerate(parts):
            keep[0, b] = part[:shard]
            send[0, b] = part[shard:]

    @pl.when(last)
    def _():
        for b, part in enumerate(parts):
            keep[0, b], send[0, b] = mix_halves(core, cut(part[:shard]), cut(part[shard:]))


def early_grads_kernel(core_at, sc, low_a, low_b, mixed_a, mixed_b, n2_a, n2_b, ll, col_a, col_b, n1_a, n1_b, dq, w_a, w_b, keep, send):
    prompt = mixed_a.shape[0]
    shard = low_a.shape[0]
    join = lambda a, b: jnp.concatenate([a[...], b[...]], axis=0)
    tall = join(low_a, low_b)
    made = mm(tall[:, 0:prompt], mixed_a[...]) + mm(tall[:, prompt:], mixed_b[...])
    query = mm(join(n1_a, n1_b), dq[...])
    blocks = dq.shape[1] // LANES
    weights = jnp.concatenate([lanes_of(ref, 0, blocks) for ref in (w_a, w_b)], axis=0)
    gains = jnp.concatenate([ref[ref.shape[0] - 1, :, 0:1] for ref in (w_a, w_b)], axis=0)
    first = scaled_sum(weights, query, gains)
    extra = mm(join(n2_a, n2_b), ll[...]) + join(col_a, col_b)
    lane = lax.broadcasted_iota(jnp.int32, extra.shape, 1)
    extra = jnp.where(lane == 0, first, extra)
    whole_row = jnp.concatenate([made, query, extra], axis=1).astype(bf)
    wide = 2 * LANES
    leave([whole_row[:, b * wide : (b + 1) * wide] for b in range(whole_row.shape[1] // wide)], sc[core_at], shard, keep, send)


def early_grads(low_t, mixed, n2t, ll, column, n1t, dq, w, scalars, first_rank, core_at, shard, deps):
    width, rows = low_t.shape
    slots = (scalars.shape[0] - first_rank) // 2
    cols = mixed[0].shape[1] + LANES + dq.shape[1]
    at = lambda k: (lambda i, s: (s[first_rank + k * slots + i], 0))
    w_at = lambda k: (lambda i, s: (0, s[first_rank + k * slots + i], 0))
    two = lambda lanes: [pl.BlockSpec((shard, lanes), at(k)) for k in range(2)]
    out = sds((slots, cols // (2 * LANES), shard, 2 * LANES), bf)
    out_spec = pl.BlockSpec((1, *out.shape[1:]), lambda i, s: (i, 0, 0, 0))
    return call(
        functools.partial(early_grads_kernel, core_at),
        "early_grads",
        (slots,),
        [low_t, low_t, *mixed, n2t, n2t, ll, column, column, n1t, n1t, dq, w, w],
        two(rows)
        + [whole(a.shape) for a in mixed]
        + two(rows)
        + [whole(ll.shape)]
        + two(LANES)
        + two(rows)
        + [whole(dq.shape)]
        + [pl.BlockSpec((w.shape[0], shard, LANES), w_at(k)) for k in range(2)],
        [out, out],
        [out_spec, out_spec],
        [],
        2 * rows * width * cols,
        scalars,
        deps,
    )


def late_grads_kernel(cfg, sc, left_a, left_b, dq, low_kv, w_a, w_b, keep, send):
    core_at, first_block, count = cfg
    core = sc[core_at]
    shard = left_a.shape[0]
    tall = jnp.concatenate([left_a[...], left_b[...]], axis=0)
    made = jnp.concatenate([mm(tall, dq[...]), mm(tall, low_kv[...])], axis=1)
    blocks = made.shape[1] // LANES
    weights = jnp.concatenate([lanes_of(ref, first_block, blocks) for ref in (w_a, w_b)], axis=0)
    gains = jnp.concatenate([ref[ref.shape[0] - 1, :, 0:1] for ref in (w_a, w_b)], axis=0)
    first = scaled_sum(weights, made, gains)
    lane = lax.broadcasted_iota(jnp.int32, (2 * shard, LANES), 1)
    made = jnp.concatenate([made, jnp.where(lane == 0, first, 0.0)], axis=1).astype(bf)
    wide = 2 * LANES
    leave([made[:, b * wide : (b + 1) * wide] for b in range(count)], core, shard, keep, send)


def late_grads(left, dq, low_kv, w, first_block, scalars, first_rank, core_at, shard, deps):
    width, rows = left.shape
    slots = (scalars.shape[0] - first_rank) // 2
    count = (dq.shape[1] + low_kv.shape[1] + LANES) // (2 * LANES)
    at = lambda k: (lambda i, s: (s[first_rank + k * slots + i], 0))
    w_at = lambda k: (lambda i, s: (0, s[first_rank + k * slots + i], 0))
    out = sds((slots, count, shard, 2 * LANES), bf)
    out_spec = pl.BlockSpec((1, count, shard, 2 * LANES), lambda i, s: (i, 0, 0, 0))
    return call(
        functools.partial(late_grads_kernel, (core_at, first_block, count)),
        "late_grads",
        (slots,),
        [left, left, dq, low_kv, w, w],
        [pl.BlockSpec((shard, rows), at(k)) for k in range(2)]
        + [whole(dq.shape), whole(low_kv.shape)]
        + [pl.BlockSpec((w.shape[0], shard, LANES), w_at(k)) for k in range(2)],
        [out, out],
        [out_spec, out_spec],
        [],
        4 * rows * width * count * LANES,
        scalars,
        deps,
    )


def spread_kernel(sc, early_a, early_b, late_a, late_b, output, query, key, value, extra):
    join = lambda a, b: jnp.concatenate([a[0, k].astype(f32) + b[0, k].astype(f32) for k in range(a.shape[1])], axis=1)
    early, late = join(early_a, early_b), join(late_a, late_b)
    cols = output.shape[1]
    output[...] = early[:, 0:cols]
    half = early.shape[1] - cols - LANES
    query[:, 0:half] = early[:, cols : cols + half]
    at = query.shape[1] - half
    query[:, half:] = late[:, 0:at]
    for out in (key, value):
        out[...] = late[:, at : at + out.shape[1]]
        at += out.shape[1]
    extra[...] = jnp.concatenate([early[:, cols + half :], late[:, at : at + LANES]], axis=1)


def spread(early, late, widths, core):
    shard = early[0].shape[2]
    outs = [sds((shard, size), f32) for size in (*widths, 2 * LANES)]
    ins = [*early, *late]
    return call(spread_kernel, "spread", (1,), ins, [whole(a.shape) for a in ins], outs, [whole(o.shape) for o in outs], [], 0, core)


def key_value_grads_kernel(sc, cosine, sine, *refs):
    *ins, out = refs
    parts = len(ins) // 2
    sums, mores = ins[:parts], ins[parts:]
    step = pl.program_id(0)
    shared = jnp.where(step < pl.num_programs(0) // 2, 1.0, 0.0).astype(f32)
    at = 0
    for is_key in (True, False):
        for own, more in zip(sums, mores):
            kvs = own.shape[0] // 2
            for kv in range(0, kvs, 2):
                heads = [kv + k + (0 if is_key else kvs) for k in range(2)]
                other = [jnp.where(step == 0, more[h, :, :HEAD_DIM], more[h, :, HEAD_DIM:]) for h in heads]
                pair = jnp.concatenate([own[h] + o * shared for h, o in zip(heads, other)], axis=1)
                if is_key:
                    pair = rope(pair, cosine[...], -sine[...])
                out[:, at : at + LANES] = pair.astype(bf)
                at += LANES


def key_value_grads(cosine, sine, sums, mores, core, deps, block=256):
    rows = cosine.shape[0]
    cols = sum(s.shape[0] for s in sums) * HEAD_DIM
    own = lambda a: pl.BlockSpec((a.shape[0], block, HEAD_DIM), lambda i, s: (0, i, 0))
    return call(
        key_value_grads_kernel,
        "key_value_grads",
        (rows // block,),
        [cosine, sine, *sums, *mores],
        [rows_of(block, LANES), rows_of(block, LANES)] + [own(a) for a in sums] + [whole(a.shape) for a in mores],
        [sds((rows, cols), bf)],
        [rows_of(block, cols)],
        [],
        0,
        core,
        deps,
    )[0]


def finish_kernel(sc, tok, extra, rg, *refs):
    *lows, w_own, mine_a, mine_b, theirs_a, theirs_b, out, w, sem = refs
    blocks = w.shape[0] // 2

    @pl.when(pl.program_id(0) == 0)
    def _():
        pltpu.make_async_copy(w_own.at[pl.ds(0, blocks)], w.at[pl.ds(0, blocks)], sem).start()
        for core, pieces in ((sc[0], (mine_a, mine_b)), (1 - sc[0], (theirs_a, theirs_b))):
            at = blocks + core * (blocks // 2)
            for piece in pieces:
                pltpu.make_async_copy(piece, w.at[pl.ds(at, piece.shape[0])], sem).start()
                at = at + piece.shape[0]
        pltpu.make_async_copy(w, w, sem).wait()

    low = jnp.concatenate([f[...] for f in lows], axis=1)
    grad = mm_nt(low, lanes_of(w, 0, 2 * blocks))
    passed, _ = norm_back(tok[...].astype(f32), extra[0:1, :].astype(f32), grad)
    out[...] = rg[...] + passed


def finish(tokens, extra, rg, lows, w_own, w_mine, w_theirs, core, deps, block=256):
    rows, width = tokens.shape
    wide = rows_of(block, width)
    blocks = 4 * sum(p.shape[0] for p in w_mine)
    return call(
        finish_kernel,
        "finish",
        (rows // block,),
        [tokens, extra, rg, *lows, w_own, *w_mine, *w_theirs],
        [wide, whole(extra.shape), wide, *[rows_of(block, f.shape[1]) for f in lows]] + [any_space()] * 5,
        [sds((rows, width), f32)],
        [wide],
        [pltpu.VMEM((blocks, width, LANES), bf), pltpu.SemaphoreType.DMA],
        2 * rows * width * blocks * LANES,
        core,
        deps,
    )[0]


def body(
    tokens,
    routes,
    cotangent,
    norm_one,
    w_query,
    key_weight,
    value_weight,
    w_output,
    norm_two,
    w_router,
    w_gate,
    w_up,
    w_down,
):
    window.turn()
    window.turn()
    window.gated = False
    count = lax.axis_size("dp")
    core = lax.axis_index("ctx")
    place = ring_place(lax.axis_index("dp"), count)
    rows, width = tokens.shape[2:]
    prompt = PROMPT_TOKENS // lax.axis_size("ctx")
    heads = w_query.shape[1] // HEAD_DIM
    kvs = key_weight.shape[1] // HEAD_DIM
    shard, hidden = w_gate.shape[1:]
    core_only = jnp.stack([core, core]).astype(jnp.int32)
    ranks = gather_sources(place, core, count)
    slots = scatter_sources(place, core, count)
    first_rank, core_at = len(ranks) + 1, len(ranks)

    def scalars(*more):
        return jnp.stack([*ranks, core, *slots, *more]).astype(jnp.int32)

    plain = scalars()
    tok = tokens.reshape(rows, width)
    cot = cotangent.reshape(rows, width)
    ids = routes.reshape(rows, TOPK)

    packed = pack(w_query, key_weight, value_weight, w_output, w_router, norm_one, norm_two, core_only)
    firsts = Gather(packed, core, count, 0)
    firsts.step()
    firsts.step()

    sizes = [4, 4, 4, 4]
    starts = [sum(sizes[:k]) for k in range(len(sizes))]
    chunks = []

    owns = [jnp.stack([w[at : at + size] for w in (w_gate, w_up, w_down)], axis=0) for at, size in zip(starts, sizes)]

    def open_chunk(*held):
        chunks.append(Gather(after(owns[len(chunks)], *held), core, count, 3))

    offsets = jnp.arange(rows, dtype=jnp.int32)
    positions = jnp.where(offsets < prompt, core * prompt + offsets, PROMPT_TOKENS + offsets - prompt)
    half_dim = HEAD_DIM // 2
    inverse = rope_base ** (-2.0 * jnp.arange(half_dim).astype(f32) / HEAD_DIM)
    angles = positions.astype(f32)[:, None] * inverse
    cosine = jnp.tile(jnp.cos(angles), (1, LANES // half_dim))
    sine = jnp.sin(angles)
    sine = jnp.tile(jnp.concatenate([-sine, sine], axis=1), (1, LANES // HEAD_DIM))
    cott = cot.T
    zero_wide, zero_table = jnp.zeros((rows, width), f32), jnp.zeros((rows, LANES), f32)

    firsts.mine[-1], cott, zero_wide, zero_table, cosine, sine, *owns = lax.optimization_barrier(
        (firsts.mine[-1], cott, zero_wide, zero_table, cosine, sine, *owns)
    )
    firsts.step()
    firsts.step()
    firsts.share()
    open_chunk(firsts.mine[-1])
    c0 = chunks[0]
    window.turn()
    window.turn()
    c0.step()
    w_first, w_out, w_out_half, extra, q, kv, kv_prompt, n1t = project(
        tok, cosine, sine, plain, firsts.bufs, heads, kvs, prompt, window.turn()
    )
    other = swap(kv_prompt, "ctx")
    out_far_mine = swap(after(w_out_half, kv_prompt), "tp")
    c0.step(kv_prompt)
    mixed_b, lse_b = attend(q, kv, other, core_only, 1, window.turn())
    far_b = swap(mixed_b, "tp")
    c0.step(lse_b)
    open_chunk(lse_b)
    c1 = chunks[1]
    c1.step()
    out_far_theirs = swap(after(out_far_mine, lse_b), "ctx")
    mixed_a, lse_a = attend(q, kv, other, core_only, 0, window.turn())
    far_a = swap(mixed_a, "tp")
    c0.step(lse_a)
    c1.step(lse_a)
    mixed, lse = (mixed_a, mixed_b), (lse_a, lse_b)
    res, n2, n2t, wt = settle(
        tok, ids, mixed, (far_a, far_b), extra, w_out, out_far_mine, out_far_theirs, core_only, [cott, zero_wide, *window.turn()]
    )
    scatters = [Scatter(core, count, plain, core_at) for _ in range(3)]
    state = dict(moe=zero_wide, back=zero_wide, pick=zero_table)

    def work(pair, mode="all", deps=None):
        at = 2 * pair
        k = max(k for k in range(len(starts)) if starts[k] <= at)
        sc = scalars(jnp.int32(at), jnp.int32(at + 1))
        bufs, local = chunks[k].bufs, at - starts[k]
        made = experts(
            mode, (n2, cot), (n2t, cott), wt, sc, bufs, local, state["moe"], state["back"], state["pick"], state.get("made"),
            window.turn() if deps is None else deps,
        )
        if mode == "all":
            state["moe"], state["back"], keep, send, state["pick"] = made
            return keep, send, state["pick"]
        if mode.startswith("front"):
            *back, state["pick"], scaled, acts = made[:-1] if mode.endswith("_end") else made
            state["back"] = back if mode.endswith("_end") else back[0]
            state["made"] = [scaled, acts]
            return made[-1]
        *moe, keep, send = made
        state["moe"] = moe if mode.endswith("_end") else moe[0]
        return keep, send, moe[0]

    s0, s1, s2 = scatters
    c0.share(wt)
    c1.step(wt)
    open_chunk(wt)
    c2 = chunks[2]
    c2.step()
    keep, send, token = work(0)

    s0.add(keep, send)
    c1.step(token)
    c2.step(token)
    first_part = w_first.shape[0] // 2
    split = (first_part + 1) // 2
    first_half = take(after(w_first, token), core * first_part, first_part)
    first_far_a = swap(first_half[:split], "tp")
    keep, send, token = work(1)

    s0.add(keep, send)
    c1.share(token)
    c2.step(token)
    open_chunk(token)
    c3 = chunks[3]
    c3.step()
    keep, send, token = work(2)

    s0.add(keep, send)
    c2.step(token)
    c3.step(token)
    keep, send, token = work(3)

    s1.add(keep, send)
    c2.share(token)
    c3.step(token)
    s0.step([token])
    keep, send, token = work(4)

    s1.add(keep, send)
    c3.step(token)
    s0.step([token])
    first_far_b = swap(after(first_half[split:], token), "tp")
    keep, send, token = work(5)

    s1.add(keep, send)
    c3.share(token)
    s0.step([token])
    token = work(6, "front")
    made_early = state["made"]

    window.gated = True
    theirs_a = swap(after(first_far_a, token), "ctx")
    theirs_b = swap(after(first_far_b, token), "ctx")
    pick_t = work(7, "front_end", window.step())
    made_late = state["made"]
    back = state["back"]

    back_far_a = swap(back[0], "tp")
    pick_far = swap(after(pick_t, back[0]), "tp")
    token = window.gate(pick_t)
    s0.step([token])
    s1.step([token])
    state["made"] = made_early
    keep_early, send_early, token = work(6, "rest", window.step())
    token = window.gate(token, back_far_a, pick_far)
    back_far_b = swap(after(back[1], token), "tp")
    s2.add(keep_early, send_early, token)
    s0_mine, s0_theirs = s0.finish([token])
    s1.step([token])
    emitted = emit((s0_mine, s0_theirs), 0, EXPERTS, None, core_only, [token])
    state["made"] = made_late
    keep, send, token = work(7, "rest_end", [emitted[0], *window.step()])
    moe = state["moe"]
    token = window.gate(token, back_far_b)
    s2.add(keep, send, token)
    s1.step([token])
    rg, low_t, dout, ll, gain_two = unsettle(
        back, (back_far_a, back_far_b), (pick_t, pick_far), wt, res, cot, extra, w_out, core_only, window.step()
    )
    token = window.gate(ll)
    moe_far_a = swap(after(moe[0], token), "tp")
    s1.step([token])
    s2.step([token])
    parts = 2
    dq_a, dkv_a, dother_a = attend_back(q, kv, other, dout, mixed, lse, cosine, sine, core_only, 0, parts, window.step())
    token = window.gate(dother_a)
    more_a = swap(after(dother_a, token), "ctx")
    s2.step([token])
    lane = jnp.arange(LANES)
    column = jnp.where(lane == 1, gain_two[0][:, None], 0.0)
    early_keep, early_send = early_grads(
        low_t, mixed, n2t, ll, column, n1t, dq_a, w_first, plain, first_rank, core_at, shard, [dother_a, *window.step()]
    )
    token = window.gate(early_keep, moe_far_a)
    far_qa = swap(after(dq_a, token), "tp")
    early = Scatter(core, count, plain, core_at)
    early.add(early_keep, early_send, token)
    s2.step([token])
    s1_mine, s1_theirs = s1.finish([token])
    dq_b, dkv_b, dother_b = attend_back(
        q, kv, other, dout, mixed, lse, cosine, sine, core_only, 1, parts, [s1_mine, *window.step()]
    )
    token = window.gate(dother_b, far_qa)
    more_b = swap(after(dother_b, token), "ctx")
    far_qb = swap(after(dq_b, token), "tp")
    early.step([token])
    low_kv = key_value_grads(cosine, sine, [dkv_a, dkv_b], [more_a, more_b], core_only, window.step())
    token = window.gate(low_kv)
    early.step([token])
    s2.step([token])
    half_blocks = heads // 4
    last_keep, last_send = late_grads(
        n1t, dq_b, low_kv, w_first, half_blocks, plain, first_rank, core_at, shard, window.step()
    )
    token = window.gate(last_keep, far_qb)
    far_kv = swap(after(low_kv, token), "tp")
    late = Scatter(core, count, plain, core_at)
    late.add(last_keep, last_send, token)
    late.step([token])
    early.step([late.value])
    emitted = emit((s1_mine, s1_theirs), EXPERTS * 3 // 8, EXPERTS, emitted, core_only, [late.value])
    late.step([emitted[0], early.value])
    moe_far_b = swap(after(moe[1], late.value), "tp")
    lows = [dq_a, dq_b, low_kv, far_qa, far_qb, far_kv]
    token_grad = finish(
        tok, extra, rg, lows, w_first, (first_far_a, first_far_b), (theirs_a, theirs_b), core_only, [late.value]
    ).reshape(tokens.shape)
    late.step([token_grad, moe_far_b])
    s2_mine, s2_theirs = s2.finish([late.value])
    early.step([late.value])
    late.step([s2_mine, early.value])
    result = combine(res, moe, (moe_far_a, moe_far_b), core_only, [late.value])
    grad_gate, grad_up, grad_down = emit((s2_mine, s2_theirs), EXPERTS * 3 // 4, EXPERTS, emitted, core_only, [late.value])
    early_sums = early.finish([result])
    late_sums = late.finish([result, grad_gate])
    result = result.reshape(tokens.shape)
    kv_width = kvs * HEAD_DIM
    widths = (w_output.shape[1], w_query.shape[1], kv_width, kv_width)
    grad_output, grad_query, grad_key, grad_value, extras = spread(early_sums, late_sums, widths, core_only)
    grad_norm_two = extras[:, 1]
    grad_router = extras[:, ROUTER_LANE : ROUTER_LANE + EXPERTS]
    gain_part = extras[:, 0] + extras[:, LANES]
    grad_norm_one = gain_part + swap(gain_part, "tp")
    return (
        result,
        token_grad,
        grad_norm_one,
        grad_query,
        grad_key,
        grad_value,
        grad_output,
        grad_norm_two,
        grad_router,
        grad_gate,
        grad_up,
        grad_down,
    )


def solution(mesh):
    slab = P("dp", "ctx", None, None)
    split, rows_only, expert = P("dp", "tp"), P("dp"), P(None, "dp", "tp")
    return jax.shard_map(
        body,
        mesh=mesh,
        in_specs=(slab, slab, slab, rows_only, split, split, split, split, rows_only, P("dp", None), expert, expert, expert),
        out_specs=(slab, slab, rows_only, split, split, split, split, rows_only, P("dp", None), expert, expert, expert),
        check_vma=False,
    )
```
